32 devices in a mesh: dp: 16 (over z, y, core), feat: 2 (over x).
Axes of the slice: x: 2, y: 2, z: 4, core: 2. Of those that a mesh axis runs over, the one named last changes fastest.
Arguments:
- table: bfloat16 [2048, 3584], P('dp', 'feat'), may hold values from -64 to 64
- text: bfloat16 [2048, 3584], P('dp', 'feat'), may hold values from -64 to 64
- table_proj: bfloat16 [3584, 4096], P(None, 'feat'), may hold values from -1 to 1
- text_proj: bfloat16 [3584, 4096], P(None, 'feat'), may hold values from -1 to 1
Outputs:
- grad_table: float32 [2048, 3584], P('dp', 'feat')
- grad_text: float32 [2048, 3584], P('dp', 'feat')
- loss_mean: float32 [1], replicated
The draws below stay inside these ranges and needn't reach their ends.
All inputs are finite; a program needn't handle non-finite values.
Results may differ from the reference program's by a relative error of at most 0.0044.
Values may be sent and summed in bfloat16 or wider, within the bound.
No kernel may reach another device: no remote copies, remote signals or barrier semaphores. Data moves between devices by JAX's collectives and lax.ppermute only.
A program may use at most 128 MiB of HBM per device.

```python
import jax
import jax.numpy as jnp
from jax import lax

E = 3584
F = 4096
PAIRS = 2048


def embed_shared(key):
    key_row, key_col, key_base = jax.random.split(jax.random.fold_in(key, 5), 3)
    position = jnp.arange(PAIRS).astype(jnp.float32)[:, None] / PAIRS
    rising = jnp.exp(jnp.log(3.0) * position)
    row_scale = 0.3 * rising * jnp.exp(jax.random.uniform(key_row, (PAIRS, 1), jnp.float32, -1.15, 1.15))
    col_scale = jnp.exp(jax.random.uniform(key_col, (1, E), jnp.float32, -0.7, 0.7))
    scale = row_scale * col_scale
    return (scale, key_base)


def embed_noise(key_base):
    return jnp.clip(jax.random.normal(key_base, (PAIRS, E), jnp.float32), -4.0, 4.0)


def embed_draw(key, own_const):
    scale, key_base = embed_shared(key)
    shared = embed_noise(key_base)
    own_key = jax.random.fold_in(key, own_const)
    own_base = jax.random.fold_in(own_key, 0)
    own = embed_noise(own_base)
    return (scale * (0.8 * shared + 0.6 * own)).astype(jnp.bfloat16)


def draw_table(key, part):
    return embed_draw(key, 11)


def draw_text(key, part):
    return embed_draw(key, 23)


def proj_shared(key):
    base = jnp.clip(jax.random.normal(jax.random.fold_in(key, 7), (E, F), jnp.float32), -4.0, 4.0)
    return base * (1.0 / jnp.sqrt(jnp.float32(E)))


def draw_table_proj(key, part):
    return proj_shared(key).astype(jnp.bfloat16)


def draw_text_proj(key, part):
    shared = proj_shared(key)
    key = jax.random.fold_in(key, 31)
    key_noise, key_angle = jax.random.split(key, 2)
    noise = jnp.clip(jax.random.normal(key_noise, (E, F), jnp.float32), -4.0, 4.0) * (1.0 / jnp.sqrt(jnp.float32(E)))
    place = (jnp.arange(F).astype(jnp.float32) + 0.5) / F
    angle = 1.45 * place + jax.random.uniform(key_angle, (F,), jnp.float32, -0.05, 0.05)
    angle = jnp.clip(angle, 0.0, 1.5)
    return (jnp.cos(angle)[None, :] * shared + jnp.sin(angle)[None, :] * noise).astype(jnp.bfloat16)


def setup_inputs(seed: int = 0) -> dict:
    arg_keys = jax.random.split(jax.random.key(seed), 5)
    table = draw_table(jax.random.fold_in(arg_keys[4], 71), 0)
    text = draw_text(jax.random.fold_in(arg_keys[4], 71), 0)
    table_proj = draw_table_proj(jax.random.fold_in(arg_keys[4], 71), 0)
    text_proj = draw_text_proj(jax.random.fold_in(arg_keys[4], 71), 0)
    return {"table": table, "text": text, "table_proj": table_proj, "text_proj": text_proj}


OFF_WEIGHT = 0.1
EPS = 1e-05

def normalize(proj):
    center = lax.optimization_barrier(jnp.mean(proj, axis=0))
    spread = lax.optimization_barrier(jnp.mean(proj * proj, axis=0)) - center * center
    inverse = lax.rsqrt(spread + EPS)
    return ((proj - center) * inverse, inverse)

def backward(grad, normed, inverse):
    shift = lax.optimization_barrier(jnp.mean(grad, axis=0))
    tilt = lax.optimization_barrier(jnp.mean(grad * normed, axis=0))
    return (inverse * (grad - shift - normed * tilt)).astype(jnp.bfloat16)

def reference(table, text, table_proj, text_proj):
    z_table = jnp.dot(table, table_proj, preferred_element_type=jnp.float32)
    z_text = jnp.dot(text, text_proj, preferred_element_type=jnp.float32)
    normed_table, inverse_table = normalize(z_table)
    normed_text, inverse_text = normalize(z_text)
    half_table = normed_table.astype(jnp.bfloat16)
    half_text = normed_text.astype(jnp.bfloat16)
    corr = lax.dot_general(half_table, half_text, (((0,), (0,)), ((), ())), preferred_element_type=jnp.float32) / PAIRS
    row_ids = lax.broadcasted_iota(jnp.int32, (F, F), 0)
    col_ids = lax.broadcasted_iota(jnp.int32, (F, F), 1)
    on_diag = row_ids == col_ids
    terms = jnp.where(on_diag, (1.0 - corr) * (1.0 - corr), OFF_WEIGHT * corr * corr)
    loss_mean = (jnp.sum(terms) / F).reshape(1)
    kernel = jnp.where(on_diag, corr - 1.0, OFF_WEIGHT * corr).astype(jnp.bfloat16)
    d_table = lax.dot_general(half_text, kernel, (((1,), (1,)), ((), ())), preferred_element_type=jnp.float32)
    d_text = jnp.dot(half_table, kernel, preferred_element_type=jnp.float32)
    back_table = backward(d_table, normed_table, inverse_table)
    back_text = backward(d_text, normed_text, inverse_text)
    grad_table = lax.dot_general(back_table, table_proj, (((1,), (1,)), ((), ())), preferred_element_type=jnp.float32)
    grad_text = lax.dot_general(back_text, text_proj, (((1,), (1,)), ((), ())), preferred_element_type=jnp.float32)
    return (grad_table, grad_text, loss_mean)
```

```python
import jax
import jax.numpy as jnp
from jax import lax
from jax.sharding import Mesh
from jax.sharding import PartitionSpec as P

OFF_WEIGHT = 0.1
EPS = 1e-05
STAT_ROWS = 8
F32 = jnp.float32
BF16 = jnp.bfloat16


def dot(a, b, dims):
    return lax.dot_general(a, b, (dims, ((), ())), preferred_element_type=F32)


def shift(x, axis, step):
    size = lax.axis_size(axis)
    return lax.ppermute(x, axis, [(i, (i + step) % size) for i in range(size)])


def flip(x, axis, bit):
    size = lax.axis_size(axis)
    return lax.ppermute(x, axis, [(i, i ^ bit) for i in range(size)])


def cube_sum(x, axis):
    bit = 1
    while bit < lax.axis_size(axis):
        x = x + flip(x, axis, bit)
        bit *= 2
    return x


def own_block(x, index, count, axis):
    size = x.shape[axis] // count
    return lax.dynamic_slice_in_dim(x, index * size, size, axis)


def split_two(x):
    high = x.astype(BF16)
    return high, (x - high.astype(F32)).astype(BF16)


def project(mine, proj):
    num_feat = lax.axis_size("feat")
    feat = lax.axis_index("feat")
    core = lax.axis_index("core")
    z = dot(mine, own_block(proj, feat, num_feat, 0), ((1,), (0,)))
    for step in range(1, num_feat):
        other = shift(mine, "feat", step)
        z = z + dot(other, own_block(proj, (feat - step) % num_feat, num_feat, 0), ((1,), (0,)))
    keep = own_block(z, core, 2, 1)
    got = flip(own_block(z, 1 - core, 2, 1), "core", 1)
    return jnp.where(core == 0, jnp.concatenate([keep, got], 0), jnp.concatenate([got, keep], 0))


def gather_rows(z):
    rows = z.shape[0]
    local_mean = jnp.mean(z, axis=0)
    centered = z - local_mean
    local_square = jnp.sum(centered * centered, axis=0)
    stats = jnp.stack([*split_two(local_mean), *split_two(local_square)])
    stats = jnp.pad(stats, ((0, STAT_ROWS - stats.shape[0]), (0, 0)))
    packed = jnp.concatenate([centered.astype(BF16), stats], 0)
    return lax.all_gather(packed, "chip", axis=0, tiled=False), rows


def normalize(gathered, rows, z):
    pairs = gathered.shape[0] * rows
    stats = gathered[:, rows:].astype(F32)
    means = stats[:, 0] + stats[:, 1]
    squares = stats[:, 2] + stats[:, 3]
    center = jnp.mean(means, axis=0)
    offset = means - center
    spread = jnp.sum(squares + rows * offset * offset, axis=0) / pairs
    inverse = lax.rsqrt(spread + EPS)
    normed_all = (gathered[:, :rows].astype(F32) + offset[:, None, :]) * inverse
    half_all = normed_all.astype(BF16).reshape(pairs, -1)
    normed = (z - center) * inverse
    return half_all, normed, inverse


def gram_rows(half, half_all):
    core = lax.axis_index("core")
    part = dot(half, half_all, ((1,), (1,)))
    mine = own_block(part, core, 2, 0) + flip(own_block(part, 1 - core, 2, 0), "core", 1)
    total = mine
    sent = mine.astype(BF16)
    for step in range(1, lax.axis_size("feat")):
        total = total + shift(sent, "feat", step).astype(F32)
    keep = total.astype(BF16)
    got = flip(keep, "core", 1)
    return jnp.where(core == 0, jnp.concatenate([keep, got], 0), jnp.concatenate([got, keep], 0))


def backward(d, normed, inverse, pairs):
    sums = jnp.stack([jnp.sum(d, axis=0), jnp.sum(d * normed, axis=0)])
    mean, tilt = cube_sum(sums, "chip") / pairs
    return (inverse * (d - mean - normed * tilt)).astype(BF16), tilt


def embed_grad(back, proj):
    num_feat = lax.axis_size("feat")
    feat = lax.axis_index("feat")
    core = lax.axis_index("core")
    keep = own_block(back, core, 2, 0)
    got = flip(own_block(back, 1 - core, 2, 0), "core", 1)
    back = jnp.where(core == 0, jnp.concatenate([keep, got], 1), jnp.concatenate([got, keep], 1))
    others = []
    for step in range(1, num_feat):
        part = dot(back, own_block(proj, (feat + step) % num_feat, num_feat, 0), ((1,), (1,)))
        others.append(shift(part.astype(BF16), "feat", step))
    grad = dot(back, own_block(proj, feat, num_feat, 0), ((1,), (1,)))
    for other in others:
        grad = grad + other.astype(F32)
    return grad


def body(table, text, table_proj, text_proj):
    z_table = project(table, table_proj)
    all_table, rows = gather_rows(z_table)
    z_text = project(text, text_proj)
    all_text, _ = gather_rows(z_text)
    pairs = rows * lax.axis_size("chip")
    features = z_table.shape[1] * 2 * lax.axis_size("feat")

    halves_table, normed_table, inverse_table = normalize(all_table, rows, z_table)
    half_table = normed_table.astype(BF16)
    gram_table = gram_rows(half_table, halves_table)

    halves_text, normed_text, inverse_text = normalize(all_text, rows, z_text)
    half_text = normed_text.astype(BF16)
    gram_text = gram_rows(half_text, halves_text)

    diag = jnp.sum(halves_table.astype(F32) * halves_text.astype(F32), axis=0) / pairs
    diag_weight = (diag - 1.0).astype(BF16).astype(F32) - OFF_WEIGHT * diag

    d_text = (OFF_WEIGHT / pairs) * dot(gram_table, halves_text, ((1,), (0,))) + half_table.astype(F32) * diag_weight
    back_text, _ = backward(d_text, normed_text, inverse_text, pairs)
    grad_text = embed_grad(back_text, text_proj)

    d_table = (OFF_WEIGHT / pairs) * dot(gram_text, halves_table, ((1,), (0,))) + half_text.astype(F32) * diag_weight
    back_table, tilt_table = backward(d_table, normed_table, inverse_table, pairs)
    grad_table = embed_grad(back_table, table_proj)

    off_table = tilt_table - diag_weight * diag
    terms = (1.0 - diag) * (1.0 - diag) - OFF_WEIGHT * diag * diag + off_table
    loss_total = cube_sum(cube_sum(jnp.sum(terms).reshape(1), "core"), "feat")
    return grad_table, grad_text, loss_total / features


def solution(mesh):
    devices = mesh.devices
    split = Mesh(
        devices.reshape(devices.shape[0] // 2, 2, devices.shape[1]),
        ("chip", "core", "feat"),
    )
    placed = (P(("chip", "core"), "feat"), P(("chip", "core"), "feat"), P(None, "feat"), P(None, "feat"))
    return jax.shard_map(
        body,
        mesh=split,
        in_specs=placed,
        out_specs=(P(("chip", "core"), "feat"), P(("chip", "core"), "feat"), P()),
        check_vma=False,
    )
```

```python
import jax
import jax.numpy as jnp
from jax import lax
from jax.sharding import Mesh
from jax.sharding import PartitionSpec as P

OFF_WEIGHT = 0.1
EPS = 1e-05
Z_CHIPS = 4
F32 = jnp.float32
BF16 = jnp.bfloat16


def dot(a, b, dims):
    return lax.dot_general(a, b, (dims, ((), ())), preferred_element_type=F32)


def shift(x, axis, step):
    size = lax.axis_size(axis)
    return lax.ppermute(x, axis, [(i, (i + step) % size) for i in range(size)])


def flip(x, axis, bit=1):
    size = lax.axis_size(axis)
    return lax.ppermute(x, axis, [(i, i ^ bit) for i in range(size)])


def cube_sum(x, *axes):
    for axis in axes:
        bit = 1
        while bit < lax.axis_size(axis):
            x = x + flip(x, axis, bit)
            bit *= 2
    return x


def own_block(x, index, count, axis):
    size = x.shape[axis] // count
    return lax.dynamic_slice_in_dim(x, index * size, size, axis)


def both_cores(x):
    got = flip(x, "core")
    first = lax.axis_index("core") == 0
    return jnp.where(first, jnp.concatenate([x, got], 0), jnp.concatenate([got, x], 0))


def add_cores(x):
    core = lax.axis_index("core")
    return own_block(x, core, 2, 0) + flip(own_block(x, 1 - core, 2, 0), "core")


def weight_blocks(proj):
    num_feat = lax.axis_size("feat")
    feat = lax.axis_index("feat")
    cols = own_block(proj, lax.axis_index("core"), 2, 1)
    return [own_block(cols, (feat - step) % num_feat, num_feat, 0) for step in range(num_feat)]


def swap_feat(x):
    return [shift(x, "feat", step) for step in range(1, lax.axis_size("feat"))]


def project(mine, others, weights):
    z = dot(both_cores(mine), weights[0], ((1,), (0,)))
    for other, weight in zip(others, weights[1:]):
        z = z + dot(both_cores(other), weight, ((1,), (0,)))
    return z


def normalize(z, pairs):
    sums = cube_sum(jnp.stack([jnp.sum(z, axis=0), jnp.sum(z * z, axis=0)]), "z", "y")
    center = sums[0] / pairs
    spread = sums[1] / pairs - center * center
    inverse = lax.rsqrt(spread + EPS)
    return (z - center) * inverse, inverse


def gather_rows(own):
    z = lax.axis_index("z")
    end = (z == 0) | (z == Z_CHIPS - 1)
    half = own.shape[0] // 2
    near = flip(own, "z")
    mid = lax.ppermute(own, "z", [(1, 2), (2, 1)])
    far_in = lax.ppermute(near, "z", [(1, 2), (2, 1)])
    far_end = lax.ppermute(mid, "z", [(1, 0), (2, 3)])
    far = jnp.where(end, far_end, far_in)
    last_end = lax.ppermute(far_in, "z", [(1, 0), (2, 3)])
    last = jnp.where(end, last_end, mid)
    early, late = [own, near, far], [last]
    for step in range(1, lax.axis_size("y")):
        y_own = shift(own, "y", step)
        y_near = [shift(near[:half], "y", step), flip(y_own[half:], "z")]
        early += [y_own, *y_near, shift(far, "y", step)]
        late += [shift(last, "y", step)]
    return jnp.concatenate(early, 0), jnp.concatenate(late, 0)


def gram_rows(half, rows):
    mine = add_cores(dot(half, rows, ((1,), (1,))))
    sent = mine.astype(BF16)
    for other in swap_feat(sent):
        mine = mine + other.astype(F32)
    return both_cores(mine.astype(BF16))


def backward(d, normed, inverse, pairs):
    sums = jnp.stack([jnp.sum(d, axis=0), jnp.sum(d * normed, axis=0)])
    mean, tilt = cube_sum(sums, "z", "y") / pairs
    return (inverse * (d - mean - normed * tilt)).astype(BF16), tilt


def embed_grad(back, weights):
    num_feat = lax.axis_size("feat")
    others = []
    for step in range(1, num_feat):
        part = add_cores(dot(back, weights[step], ((1,), (1,))))
        others.append(shift(part.astype(BF16), "feat", num_feat - step))
    grad = add_cores(dot(back, weights[0], ((1,), (1,))))
    for other in others:
        grad = grad + other.astype(F32)
    return grad


def body(table, text, table_proj, text_proj):
    pairs = table.shape[0] * 2 * lax.axis_size("z") * lax.axis_size("y")
    features = table_proj.shape[1] * lax.axis_size("feat")
    table_weights = weight_blocks(table_proj)
    text_weights = weight_blocks(text_proj)

    others_table = swap_feat(table)
    text, others_table = lax.optimization_barrier((text, others_table))
    others_text = swap_feat(text)

    normed_table, inverse_table = normalize(project(table, others_table, table_weights), pairs)
    half_table = normed_table.astype(BF16)
    all_table = gather_rows(half_table)
    normed_text, inverse_text = normalize(project(text, others_text, text_weights), pairs)
    half_text = normed_text.astype(BF16)
    all_text = gather_rows(half_text)

    gram_table = [gram_rows(half_table, rows) for rows in all_table]
    gram_text = [gram_rows(half_text, rows) for rows in all_text]

    diag = 0.0
    for rows_table, rows_text in zip(all_table, all_text):
        diag = diag + jnp.sum(rows_table.astype(F32) * rows_text.astype(F32), axis=0)
    diag = diag / pairs
    diag_weight = (diag - 1.0).astype(BF16).astype(F32) - OFF_WEIGHT * diag

    off_text = 0.0
    for gram, rows in zip(gram_table, all_text):
        off_text = off_text + dot(gram, rows, ((1,), (0,)))
    d_text = (OFF_WEIGHT / pairs) * off_text + half_table.astype(F32) * diag_weight
    back_text, _ = backward(d_text, normed_text, inverse_text, pairs)
    grad_text = embed_grad(back_text, text_weights)

    off_table = 0.0
    for gram, rows in zip(gram_text, all_table):
        off_table = off_table + dot(gram, rows, ((1,), (0,)))
    d_table = (OFF_WEIGHT / pairs) * off_table + half_text.astype(F32) * diag_weight
    back_table, tilt_table = backward(d_table, normed_table, inverse_table, pairs)
    grad_table = embed_grad(back_table, table_weights)

    squares = tilt_table - diag_weight * diag
    terms = (1.0 - diag) * (1.0 - diag) - OFF_WEIGHT * diag * diag + squares
    loss_total = cube_sum(jnp.sum(terms).reshape(1), "core", "feat")
    return grad_table, grad_text, loss_total / features


def solution(mesh):
    devices = mesh.devices
    split = Mesh(
        devices.reshape(Z_CHIPS, devices.shape[0] // (2 * Z_CHIPS), 2, devices.shape[1]),
        ("z", "y", "core", "feat"),
    )
    rows = ("z", "y", "core")
    placed = (P(rows, "feat"), P(rows, "feat"), P(None, "feat"), P(None, "feat"))
    return jax.shard_map(
        body,
        mesh=split,
        in_specs=placed,
        out_specs=(P(rows, "feat"), P(rows, "feat"), P()),
        check_vma=False,
    )
```

```python
import jax
import jax.numpy as jnp
from jax import lax
from jax.sharding import Mesh
from jax.sharding import PartitionSpec as P

OFF_WEIGHT = 0.1
EPS = 1e-05
Z_CHIPS = 4
F32 = jnp.float32
BF16 = jnp.bfloat16


def dot(a, b, dims):
    return lax.dot_general(a, b, (dims, ((), ())), preferred_element_type=F32)


def shift(x, axis, step):
    size = lax.axis_size(axis)
    return lax.ppermute(x, axis, [(i, (i + step) % size) for i in range(size)])


def flip(x, axis, bit=1):
    size = lax.axis_size(axis)
    return lax.ppermute(x, axis, [(i, i ^ bit) for i in range(size)])


def cube_sum(x, *axes):
    for axis in axes:
        bit = 1
        while bit < lax.axis_size(axis):
            x = x + flip(x, axis, bit)
            bit *= 2
    return x


def hold(x, *first):
    return lax.optimization_barrier((x, *first))[0]


def own_block(x, index, count, axis):
    size = x.shape[axis] // count
    return lax.dynamic_slice_in_dim(x, index * size, size, axis)


def both_cores(x):
    got = flip(x, "core")
    first = lax.axis_index("core") == 0
    return jnp.where(first, jnp.concatenate([x, got], 0), jnp.concatenate([got, x], 0))


def add_cores(x):
    core = lax.axis_index("core")
    return own_block(x, core, 2, 0) + flip(own_block(x, 1 - core, 2, 0), "core")


def weight_blocks(proj):
    num_feat = lax.axis_size("feat")
    feat = lax.axis_index("feat")
    cols = own_block(proj, lax.axis_index("core"), 2, 1)
    return [own_block(cols, (feat - step) % num_feat, num_feat, 0) for step in range(num_feat)]


def swap_feat(x):
    return [shift(x, "feat", step) for step in range(1, lax.axis_size("feat"))]


def project(z, others, weights):
    for other, weight in zip(others, weights[1:]):
        z = z + dot(both_cores(other), weight, ((1,), (0,)))
    return z


def normalize(z, pairs):
    sums = cube_sum(jnp.stack([jnp.sum(z, axis=0), jnp.sum(z * z, axis=0)]), "z", "y")
    center = sums[0] / pairs
    spread = sums[1] / pairs - center * center
    inverse = lax.rsqrt(spread + EPS)
    return (z - center) * inverse, inverse


def gather_rows(own):
    z = lax.axis_index("z")
    end = (z == 0) | (z == Z_CHIPS - 1)
    half = own.shape[0] // 2
    near = flip(own, "z")
    mid = lax.ppermute(own, "z", [(1, 2), (2, 1)])
    far_in = lax.ppermute(near, "z", [(1, 2), (2, 1)])
    far_end = lax.ppermute(mid, "z", [(1, 0), (2, 3)])
    far = jnp.where(end, far_end, far_in)
    last_end = lax.ppermute(far_in, "z", [(1, 0), (2, 3)])
    last = jnp.where(end, last_end, mid)
    first, second, third = [own, near], [far], [last]
    for step in range(1, lax.axis_size("y")):
        y_own = shift(own, "y", step)
        first += [y_own, shift(near[:half], "y", step), flip(y_own[half:], "z")]
        second += [shift(far, "y", step)]
        third += [shift(last, "y", step)]
    return [jnp.concatenate(blocks, 0) for blocks in (first, second, third)]


def gram_rows(half, rows):
    mine = add_cores(dot(half, rows, ((1,), (1,))))
    sent = mine.astype(BF16)
    for other in swap_feat(sent):
        mine = mine + other.astype(F32)
    return both_cores(mine.astype(BF16))


def backward(d, normed, inverse, pairs):
    sums = jnp.stack([jnp.sum(d, axis=0), jnp.sum(d * normed, axis=0)])
    mean, tilt = cube_sum(sums, "z", "y") / pairs
    return (inverse * (d - mean - normed * tilt)).astype(BF16), tilt


def embed_parts(back, weights):
    return [add_cores(dot(back, weight, ((1,), (1,)))).astype(BF16) for weight in weights[1:]]


def swap_parts(sent):
    num_feat = lax.axis_size("feat")
    return [
        [shift(piece, "feat", num_feat - step) for step, piece in enumerate(pieces, 1)]
        for pieces in zip(*[jnp.split(part, [part.shape[0] * 3 // 4]) for part in sent])
    ]


def embed_grad(own, got):
    pieces = jnp.split(own, [own.shape[0] * 3 // 4])
    return jnp.concatenate([piece + sum(part.astype(F32) for part in parts) for piece, parts in zip(pieces, got)], 0)


def body(table, text, table_proj, text_proj):
    pairs = table.shape[0] * 2 * lax.axis_size("z") * lax.axis_size("y")
    features = table_proj.shape[1] * lax.axis_size("feat")
    table_weights = weight_blocks(table_proj)
    text_weights = weight_blocks(text_proj)

    others_table = swap_feat(table)
    z_table = dot(both_cores(table), table_weights[0], ((1,), (0,)))
    z_text = dot(both_cores(text), text_weights[0], ((1,), (0,)))
    text, z_table, z_text, *others_table = lax.optimization_barrier((text, z_table, z_text, *others_table))
    others_text = swap_feat(text)

    normed_table, inverse_table = normalize(project(z_table, others_table, table_weights), pairs)
    half_table = normed_table.astype(BF16)
    all_table = gather_rows(half_table)
    normed_text, inverse_text = normalize(project(z_text, others_text, text_weights), pairs)
    half_text = normed_text.astype(BF16)
    all_text = gather_rows(half_text)

    gram_table = [gram_rows(half_table, rows) for rows in all_table]
    gram_text = [gram_rows(half_text, rows) for rows in all_text]

    diag = 0.0
    for rows_table, rows_text in zip(all_table, all_text):
        diag = diag + jnp.sum(rows_table.astype(F32) * rows_text.astype(F32), axis=0)
    diag = diag / pairs
    diag_weight = (diag - 1.0).astype(BF16).astype(F32) - OFF_WEIGHT * diag

    off_text = 0.0
    for gram, rows in zip(gram_table, all_text):
        off_text = off_text + dot(gram, rows, ((1,), (0,)))
    d_text = (OFF_WEIGHT / pairs) * off_text + half_table.astype(F32) * diag_weight
    back_text, _ = backward(d_text, normed_text, inverse_text, pairs)
    sent_text = embed_parts(back_text, text_weights)
    got_text = swap_parts(sent_text)

    off_table = 0.0
    for gram, rows in zip(gram_text, all_table):
        off_table = off_table + dot(gram, rows, ((1,), (0,)))
    d_table = (OFF_WEIGHT / pairs) * off_table + half_text.astype(F32) * diag_weight
    d_table = hold(d_table, *sent_text)
    back_table, tilt_table = backward(d_table, normed_table, inverse_table, pairs)
    own_text = add_cores(dot(hold(back_text, *sent_text), text_weights[0], ((1,), (1,))))
    back_table, *got_text[0] = lax.optimization_barrier((back_table, *got_text[0]))
    sent_table = embed_parts(back_table, table_weights)
    *sent_table, got_text[1] = lax.optimization_barrier((*sent_table, got_text[1]))
    got_table = swap_parts(sent_table)
    own_table = add_cores(dot(hold(back_table, *sent_table), table_weights[0], ((1,), (1,))))
    grad_text = embed_grad(own_text, got_text)
    grad_table = embed_grad(own_table, got_table)

    squares = tilt_table - diag_weight * diag
    terms = (1.0 - diag) * (1.0 - diag) - OFF_WEIGHT * diag * diag + squares
    loss_total = cube_sum(hold(jnp.sum(terms).reshape(1), *sent_table), "core", "feat")
    return grad_table, grad_text, loss_total / features


def solution(mesh):
    devices = mesh.devices
    split = Mesh(
        devices.reshape(Z_CHIPS, devices.shape[0] // (2 * Z_CHIPS), 2, devices.shape[1]),
        ("z", "y", "core", "feat"),
    )
    rows = ("z", "y", "core")
    placed = (P(rows, "feat"), P(rows, "feat"), P(None, "feat"), P(None, "feat"))
    return jax.shard_map(
        body,
        mesh=split,
        in_specs=placed,
        out_specs=(P(rows, "feat"), P(rows, "feat"), P()),
        check_vma=False,
    )
```

```python
import jax
import jax.numpy as jnp
from jax import lax
from jax.sharding import Mesh
from jax.sharding import PartitionSpec as P

OFF_WEIGHT = 0.1
EPS = 1e-05
Z_CHIPS = 4
F32 = jnp.float32
BF16 = jnp.bfloat16


def dot(a, b, dims):
    return lax.dot_general(a, b, (dims, ((), ())), preferred_element_type=F32)


def shift(x, axis, step):
    size = lax.axis_size(axis)
    return lax.ppermute(x, axis, [(i, (i + step) % size) for i in range(size)])


def flip(x, axis, bit=1):
    size = lax.axis_size(axis)
    return lax.ppermute(x, axis, [(i, i ^ bit) for i in range(size)])


def tree_sum(x, *axes):
    size = 1
    for axis in axes:
        size *= lax.axis_size(axis)
    terms = [x] + [lax.ppermute(x, axes, [(i, i ^ mask) for i in range(size)]) for mask in range(1, size)]
    while len(terms) > 1:
        terms = [a + b for a, b in zip(terms[::2], terms[1::2])]
    return terms[0]


def hold(x, *first):
    return lax.optimization_barrier((x, *first))[0]


def own_block(x, index, count, axis):
    size = x.shape[axis] // count
    return lax.dynamic_slice_in_dim(x, index * size, size, axis)


def both_cores(x):
    got = flip(x, "core")
    first = lax.axis_index("core") == 0
    return jnp.where(first, jnp.concatenate([x, got], 0), jnp.concatenate([got, x], 0))


def add_cores(x):
    core = lax.axis_index("core")
    return own_block(x, core, 2, 0) + flip(own_block(x, 1 - core, 2, 0), "core")


def weight_blocks(proj):
    num_feat = lax.axis_size("feat")
    feat = lax.axis_index("feat")
    cols = own_block(proj, lax.axis_index("core"), 2, 1)
    return [own_block(cols, (feat - step) % num_feat, num_feat, 0) for step in range(num_feat)]


def swap_feat(x):
    return [shift(x, "feat", step) for step in range(1, lax.axis_size("feat"))]


def project(z, others, weights):
    for other, weight in zip(others, weights[1:]):
        z = z + dot(both_cores(other), weight, ((1,), (0,)))
    return z


def normalize(z, pairs):
    sums = tree_sum(jnp.stack([jnp.sum(z, axis=0), jnp.sum(z * z, axis=0)]), "z", "y")
    center = sums[0] / pairs
    spread = sums[1] / pairs - center * center
    inverse = lax.rsqrt(spread + EPS)
    return (z - center) * inverse, inverse


def stage(*groups):
    return lax.optimization_barrier(groups)


def shifts(x, axis):
    return [shift(x, axis, step) for step in range(1, lax.axis_size(axis))]


def send_own(own):
    return flip(own, "z"), lax.ppermute(own, "z", [(1, 2), (2, 1)]), shifts(own, "y")


def send_near(near, mid):
    half = near.shape[0] // 2
    return (
        lax.ppermute(near, "z", [(1, 2), (2, 1)]),
        lax.ppermute(mid, "z", [(1, 0), (2, 3)]),
        shifts(near[:half], "y"),
    )


def send_far(far_in, far_end, y_own):
    z = lax.axis_index("z")
    far = jnp.where((z == 0) | (z == Z_CHIPS - 1), far_end, far_in)
    half = far.shape[0] // 2
    return (
        far,
        lax.ppermute(far_in, "z", [(1, 0), (2, 3)]),
        shifts(far, "y"),
        [flip(block[half:], "z") for block in y_own],
    )


def send_last(last_end, mid):
    z = lax.axis_index("z")
    last = jnp.where((z == 0) | (z == Z_CHIPS - 1), last_end, mid)
    return last, shifts(last, "y")


def near_group(own, near, y_own, y_near, y_rest):
    blocks = [own, near]
    for parts in zip(y_own, y_near, y_rest):
        blocks += parts
    return jnp.concatenate(blocks, 0)


def gram_feat(part):
    return shifts(part.astype(BF16), "feat")


def gram_total(part, others):
    for other in others:
        part = part + other.astype(F32)
    return both_cores(part.astype(BF16))


def backward(d, normed, inverse, pairs):
    sums = jnp.stack([jnp.sum(d, axis=0), jnp.sum(d * normed, axis=0)])
    mean, tilt = tree_sum(sums, "z", "y") / pairs
    return (inverse * (d - mean - normed * tilt)).astype(BF16), tilt


def embed_parts(back, weights):
    return [add_cores(dot(back, weight, ((1,), (1,)))).astype(BF16) for weight in weights[1:]]


def swap_parts(sent):
    num_feat = lax.axis_size("feat")
    return [
        [shift(piece, "feat", num_feat - step) for step, piece in enumerate(pieces, 1)]
        for pieces in zip(*[jnp.split(part, [part.shape[0] * 3 // 4]) for part in sent])
    ]


def embed_grad(own, got):
    pieces = jnp.split(own, [own.shape[0] * 3 // 4])
    return jnp.concatenate([piece + sum(part.astype(F32) for part in parts) for piece, parts in zip(pieces, got)], 0)


def body(table, text, table_proj, text_proj):
    pairs = table.shape[0] * 2 * lax.axis_size("z") * lax.axis_size("y")
    features = table_proj.shape[1] * lax.axis_size("feat")
    table_weights = weight_blocks(table_proj)
    text_weights = weight_blocks(text_proj)

    others_table = swap_feat(table)
    z_table = dot(both_cores(table), table_weights[0], ((1,), (0,)))
    z_text = dot(both_cores(text), text_weights[0], ((1,), (0,)))
    text, z_table, z_text, *others_table = lax.optimization_barrier((text, z_table, z_text, *others_table))
    others_text = swap_feat(text)

    normed_table, inverse_table = normalize(project(z_table, others_table, table_weights), pairs)
    half_table = normed_table.astype(BF16)
    t_near, t_mid, t_yown = stage(*send_own(half_table))
    t_far_in, t_far_end, t_ynear = send_near(t_near, t_mid)

    normed_text, inverse_text = normalize(project(z_text, others_text, text_weights), pairs)
    half_text = normed_text.astype(BF16)
    x_near, x_mid, x_yown = send_own(half_text)

    t_far_in, t_far_end, t_ynear = stage(t_far_in, t_far_end, t_ynear)
    t_far, t_last_end, t_yfar, t_yrest = send_far(t_far_in, t_far_end, t_yown)

    x_near, x_mid, x_yown, t_last_end = stage(x_near, x_mid, x_yown, t_last_end)
    x_far_in, x_far_end, x_ynear = send_near(x_near, x_mid)
    t_last, t_ylast = send_last(t_last_end, t_mid)

    x_far_in, x_far_end, x_ynear, t_yfar, t_yrest = stage(x_far_in, x_far_end, x_ynear, t_yfar, t_yrest)
    x_far, x_last_end, x_yfar, x_yrest = send_far(x_far_in, x_far_end, x_yown)
    t_first = near_group(half_table, t_near, t_yown, t_ynear, t_yrest)
    t_second = jnp.concatenate([t_far, *t_yfar], 0)
    gt_first, gt_second = (add_cores(dot(half_table, rows, ((1,), (1,)))) for rows in (t_first, t_second))

    x_last_end, t_ylast, gt_first, gt_second = stage(x_last_end, t_ylast, gt_first, gt_second)
    x_last, x_ylast = send_last(x_last_end, x_mid)
    gt_others = gram_feat(gt_first), gram_feat(gt_second)
    t_third = jnp.concatenate([t_last, *t_ylast], 0)
    gt_third = add_cores(dot(half_table, t_third, ((1,), (1,))))

    x_yfar, x_yrest, gt_others, gt_third = stage(x_yfar, x_yrest, gt_others, gt_third)
    x_first = near_group(half_text, x_near, x_yown, x_ynear, x_yrest)
    x_second = jnp.concatenate([x_far, *x_yfar], 0)
    gx_first, gx_second = (add_cores(dot(half_text, rows, ((1,), (1,)))) for rows in (x_first, x_second))
    gt_first, gt_second = gram_total(gt_first, gt_others[0]), gram_total(gt_second, gt_others[1])
    gt_other = gram_feat(gt_third)

    gx_first, gx_second, gt_first, gt_second, gt_other = stage(gx_first, gx_second, gt_first, gt_second, gt_other)
    gx_others = gram_feat(gx_first), gram_feat(gx_second)
    gt_third = gram_total(gt_third, gt_other)

    x_ylast, gt_third = stage(x_ylast, gt_third)
    x_third = jnp.concatenate([x_last, *x_ylast], 0)
    gx_third = add_cores(dot(half_text, x_third, ((1,), (1,))))
    gx_other = gram_feat(gx_third)
    gx_first, gx_second = gram_total(gx_first, gx_others[0]), gram_total(gx_second, gx_others[1])
    gx_third = gram_total(gx_third, gx_other)
    all_table, all_text = (t_first, t_second, t_third), (x_first, x_second, x_third)
    gram_table, gram_text = (gt_first, gt_second, gt_third), (gx_first, gx_second, gx_third)

    diag = 0.0
    for rows_table, rows_text in zip(all_table, all_text):
        diag = diag + jnp.sum(rows_table.astype(F32) * rows_text.astype(F32), axis=0)
    diag = diag / pairs
    diag_weight = (diag - 1.0).astype(BF16).astype(F32) - OFF_WEIGHT * diag

    off_text = 0.0
    for gram, rows in zip(gram_table, all_text):
        off_text = off_text + dot(gram, rows, ((1,), (0,)))
    d_text = (OFF_WEIGHT / pairs) * off_text + half_table.astype(F32) * diag_weight
    back_text, _ = backward(d_text, normed_text, inverse_text, pairs)
    sent_text = embed_parts(back_text, text_weights)
    got_text = swap_parts(sent_text)

    off_table = 0.0
    for gram, rows in zip(gram_text, all_table):
        off_table = off_table + dot(gram, rows, ((1,), (0,)))
    d_table = (OFF_WEIGHT / pairs) * off_table + half_text.astype(F32) * diag_weight
    d_table = hold(d_table, *sent_text)
    back_table, tilt_table = backward(d_table, normed_table, inverse_table, pairs)
    own_text = add_cores(dot(hold(back_text, *sent_text), text_weights[0], ((1,), (1,))))
    back_table, *got_text[0] = lax.optimization_barrier((back_table, *got_text[0]))
    sent_table = embed_parts(back_table, table_weights)
    *sent_table, got_text[1] = lax.optimization_barrier((*sent_table, got_text[1]))
    got_table = swap_parts(sent_table)
    own_table = add_cores(dot(hold(back_table, *sent_table), table_weights[0], ((1,), (1,))))
    grad_text = embed_grad(own_text, got_text)
    grad_table = embed_grad(own_table, got_table)

    squares = tilt_table - diag_weight * diag
    terms = (1.0 - diag) * (1.0 - diag) - OFF_WEIGHT * diag * diag + squares
    loss_total = tree_sum(hold(jnp.sum(terms).reshape(1), *sent_table), "core", "feat")
    return grad_table, grad_text, loss_total / features


def solution(mesh):
    devices = mesh.devices
    split = Mesh(
        devices.reshape(Z_CHIPS, devices.shape[0] // (2 * Z_CHIPS), 2, devices.shape[1]),
        ("z", "y", "core", "feat"),
    )
    rows = ("z", "y", "core")
    placed = (P(rows, "feat"), P(rows, "feat"), P(None, "feat"), P(None, "feat"))
    return jax.shard_map(
        body,
        mesh=split,
        in_specs=placed,
        out_specs=(P(rows, "feat"), P(rows, "feat"), P()),
        check_vma=False,
    )
```

```python
import jax
import jax.numpy as jnp
from jax import lax
from jax.sharding import Mesh
from jax.sharding import PartitionSpec as P

OFF_WEIGHT = 0.1
EPS = 1e-05
Z_CHIPS = 4
F32 = jnp.float32
BF16 = jnp.bfloat16


def dot(a, b, dims):
    return lax.dot_general(a, b, (dims, ((), ())), preferred_element_type=F32)


def shift(x, axis, step):
    size = lax.axis_size(axis)
    return lax.ppermute(x, axis, [(i, (i + step) % size) for i in range(size)])


def flip(x, axis, bit=1):
    size = lax.axis_size(axis)
    return lax.ppermute(x, axis, [(i, i ^ bit) for i in range(size)])


def cube_sum(x, *axes):
    for axis in axes:
        bit = 1
        while bit < lax.axis_size(axis):
            x = x + flip(x, axis, bit)
            bit *= 2
    return x


def cube_gather(x, *axes):
    x = x[None]
    for axis in axes:
        bit = 1
        while bit < lax.axis_size(axis):
            x = jnp.concatenate([x, flip(x, axis, bit)], 0)
            bit *= 2
    return x


def merge(x):
    while x.shape[0] > 1:
        x = x[: x.shape[0] // 2] + x[x.shape[0] // 2 :]
    return x[0]


def split_two(x):
    high = x.astype(BF16)
    return high, (x - high.astype(F32)).astype(BF16)


def hold(x, *first):
    return lax.optimization_barrier((x, *first))[0]


def own_block(x, index, count, axis):
    size = x.shape[axis] // count
    return lax.dynamic_slice_in_dim(x, index * size, size, axis)


def both_cores(x):
    got = flip(x, "core")
    first = lax.axis_index("core") == 0
    return jnp.where(first, jnp.concatenate([x, got], 0), jnp.concatenate([got, x], 0))


def add_cores(x):
    core = lax.axis_index("core")
    return own_block(x, core, 2, 0) + flip(own_block(x, 1 - core, 2, 0), "core")


def weight_blocks(proj):
    num_feat = lax.axis_size("feat")
    feat = lax.axis_index("feat")
    cols = own_block(proj, lax.axis_index("core"), 2, 1)
    return [own_block(cols, (feat - step) % num_feat, num_feat, 0) for step in range(num_feat)]


def swap_feat(x):
    return [shift(x, "feat", step) for step in range(1, lax.axis_size("feat"))]


def project(z, others, weights):
    for other, weight in zip(others, weights[1:]):
        z = z + dot(both_cores(other), weight, ((1,), (0,)))
    return z


def center_rows(z):
    mean = jnp.mean(z, axis=0)
    centered = z - mean
    return centered, mean, jnp.sum(centered * centered, axis=0)


def normalize(centered, means, squares, pairs):
    rows = centered.shape[0]
    center = merge(means) / means.shape[0]
    offsets = means - center
    spread = (merge(squares) + rows * merge(offsets * offsets)) / pairs
    inverse = lax.rsqrt(spread + EPS)
    return (centered + offsets[0]) * inverse, inverse, offsets


def gather_rows(own):
    z = lax.axis_index("z")
    y_size = lax.axis_size("y")
    end = (z == 0) | (z == Z_CHIPS - 1)
    half = own.shape[0] // 2
    near = flip(own, "z")
    mid = lax.ppermute(own, "z", [(1, 2), (2, 1)])
    far_in = lax.ppermute(near, "z", [(1, 2), (2, 1)])
    far_end = lax.ppermute(mid, "z", [(1, 0), (2, 3)])
    far = jnp.where(end, far_end, far_in)
    last_end = lax.ppermute(far_in, "z", [(1, 0), (2, 3)])
    last = jnp.where(end, last_end, mid)
    early, late = [own, near, far, last], []
    early_index, late_index = [0, y_size, 2 * y_size, 3 * y_size], []
    for step in range(1, y_size):
        y_own = flip(own, "y", step)
        early += [y_own, flip(near[:half], "y", step), flip(y_own[half:], "z")]
        early_index += [step, y_size + step]
        late += [flip(far, "y", step), flip(last, "y", step)]
        late_index += [2 * y_size + step, 3 * y_size + step]
    return (jnp.concatenate(early, 0), early_index), (jnp.concatenate(late, 0), late_index)


def members(index, count, width):
    chips = jnp.repeat(jnp.array(index, jnp.int32), width)
    return (jnp.arange(count, dtype=jnp.int32)[:, None] == chips[None, :]).astype(BF16)


def gram_part(scaled, offsets, rows, index):
    count = offsets.shape[0]
    shifts = dot(scaled, jnp.concatenate(split_two(offsets), 0), ((1,), (1,)))
    shifts = jnp.concatenate(split_two(shifts[:, :count] + shifts[:, count:]), 1)
    chips = members(index, count, scaled.shape[0])
    return dot(scaled, rows, ((1,), (1,))) + dot(shifts, jnp.concatenate([chips, chips], 0), ((1,), (0,)))


def add_feat(mine, others):
    for other in others:
        mine = mine + other.astype(F32)
    return mine.astype(BF16)


def gram_times(grams, groups, offsets):
    count = offsets.shape[0]
    total, sums = 0.0, 0.0
    for gram, (rows, index) in zip(grams, groups):
        total = total + dot(gram, rows, ((1,), (0,)))
        sums = sums + dot(gram, members(index, count, gram.shape[0]), ((1,), (1,)))
    return total + lax.dot_general(
        sums, offsets, (((1,), (0,)), ((), ())), precision=lax.Precision.HIGHEST, preferred_element_type=F32
    )


def column_sums(d, normed):
    return jnp.stack([jnp.sum(d, axis=0), jnp.sum(d * normed, axis=0)])


def backward(d, normed, inverse, means):
    mean, tilt = means
    return (inverse * (d - mean - normed * tilt)).astype(BF16)


def swap_parts(sent):
    num_feat = lax.axis_size("feat")
    return [
        [shift(piece, "feat", num_feat - step) for step, piece in enumerate(pieces, 1)]
        for pieces in zip(*[jnp.split(part, [part.shape[0] * 3 // 4]) for part in sent])
    ]


def embed_grad(own, got):
    pieces = jnp.split(own, [own.shape[0] * 3 // 4])
    return jnp.concatenate([piece + sum(part.astype(F32) for part in parts) for piece, parts in zip(pieces, got)], 0)


def body(table, text, table_proj, text_proj):
    pairs = table.shape[0] * 2 * lax.axis_size("z") * lax.axis_size("y")
    features = table_proj.shape[1] * lax.axis_size("feat")
    table_weights = weight_blocks(table_proj)
    text_weights = weight_blocks(text_proj)

    others_table = swap_feat(table)
    z_table = dot(both_cores(table), table_weights[0], ((1,), (0,)))
    z_text = dot(both_cores(text), text_weights[0], ((1,), (0,)))
    text, z_table, z_text, *others_table = lax.optimization_barrier((text, z_table, z_text, *others_table))
    others_text = swap_feat(text)

    centered_table, mean_table, square_table = center_rows(project(z_table, others_table, table_weights))
    all_table = gather_rows(centered_table.astype(BF16))
    centered_text, mean_text, square_text = center_rows(project(z_text, others_text, text_weights))
    all_text = gather_rows(centered_text.astype(BF16))
    cross = jnp.sum(centered_table * centered_text, axis=0)

    stats = cube_gather(jnp.stack([mean_table, square_table, mean_text, square_text, cross]), "y", "z")
    normed_table, inverse_table, offsets_table = normalize(centered_table, stats[:, 0], stats[:, 1], pairs)
    normed_text, inverse_text, offsets_text = normalize(centered_text, stats[:, 2], stats[:, 3], pairs)
    rows = centered_table.shape[0]
    diag = inverse_table * inverse_text * ((merge(stats[:, 4]) + rows * merge(offsets_table * offsets_text)) / pairs)
    diag_weight = (diag - 1.0).astype(BF16).astype(F32) - OFF_WEIGHT * diag
    half_table = normed_table.astype(BF16)
    half_text = normed_text.astype(BF16)

    scaled_table = (normed_table * inverse_table).astype(BF16)
    scaled_text = (normed_text * inverse_text).astype(BF16)
    early_table, late_table = all_table
    early_text, late_text = all_text

    gt_early = add_cores(gram_part(scaled_table, offsets_table, *early_table))
    gt_early_others = swap_feat(gt_early.astype(BF16))
    early_rows, gt_early_others = lax.optimization_barrier((early_text[0], gt_early_others))
    early_text = early_rows, early_text[1]
    gt_late = add_cores(gram_part(scaled_table, offsets_table, *late_table))
    gx_early = add_cores(gram_part(scaled_text, offsets_text, *early_text))
    gt_late_others = swap_feat(gt_late.astype(BF16))
    gx_early_others = swap_feat(gx_early.astype(BF16))
    late_rows, gt_late_others, gx_early_others = lax.optimization_barrier((late_text[0], gt_late_others, gx_early_others))
    late_text = late_rows, late_text[1]
    gram_table = both_cores(add_feat(gt_early, gt_early_others)), both_cores(add_feat(gt_late, gt_late_others))
    all_text = early_text, late_text
    gx_late = add_cores(gram_part(scaled_text, offsets_text, *late_text))

    d_text = (OFF_WEIGHT / pairs) * inverse_text * gram_times(gram_table, all_text, offsets_text)
    d_text = d_text + half_table.astype(F32) * diag_weight
    sums_text = column_sums(d_text, normed_text)
    gx_late, sums_text = lax.optimization_barrier((gx_late, sums_text))
    gx_late_others = swap_feat(gx_late.astype(BF16))
    gx_early = both_cores(add_feat(gx_early, gx_early_others))
    sums_text = sums_text + flip(sums_text, "z", 1)
    gx_early, sums_text, *gx_late_others = lax.optimization_barrier((gx_early, sums_text, *gx_late_others))
    gx_late = both_cores(add_feat(gx_late, gx_late_others))
    sums_text = sums_text + flip(sums_text, "z", 2)
    gx_late, sums_text = lax.optimization_barrier((gx_late, sums_text))
    sums_text = cube_sum(sums_text, "y")

    d_table = (OFF_WEIGHT / pairs) * inverse_table * gram_times((gx_early, gx_late), all_table, offsets_table)
    d_table = d_table + half_text.astype(F32) * diag_weight
    sums_table = column_sums(d_table, normed_table)
    sums_table, sums_text = lax.optimization_barrier((sums_table, sums_text))
    sums_table = sums_table + flip(sums_table, "z", 1)
    back_text = backward(d_text, normed_text, inverse_text, sums_text / pairs)
    parts_text = [dot(back_text, weight, ((1,), (1,))) for weight in text_weights[1:]]
    sums_table, *parts_text = lax.optimization_barrier((sums_table, *parts_text))
    sums_table = sums_table + flip(sums_table, "z", 2)
    sent_text = [add_cores(part).astype(BF16) for part in parts_text]
    sums_table, back_text, *sent_text = lax.optimization_barrier((sums_table, back_text, *sent_text))
    got_text = swap_parts(sent_text)
    sums_table = cube_sum(sums_table, "y")
    own_text = dot(back_text, text_weights[0], ((1,), (1,)))

    sums_table, own_text = lax.optimization_barrier((sums_table, own_text))
    means_table = sums_table / pairs
    back_table = backward(d_table, normed_table, inverse_table, means_table)
    back_table, *got_text[0] = lax.optimization_barrier((back_table, *got_text[0]))
    parts_table = [dot(back_table, weight, ((1,), (1,))) for weight in table_weights[1:]]
    own_text, *parts_table = lax.optimization_barrier((own_text, *parts_table))
    sent_table = [add_cores(part).astype(BF16) for part in parts_table]
    sent_table, got_text[1] = lax.optimization_barrier((sent_table, got_text[1]))
    got_table = swap_parts(sent_table)
    back_table = hold(back_table, *sent_table)
    grad_text = embed_grad(add_cores(own_text), got_text)
    grad_table = embed_grad(add_cores(dot(back_table, table_weights[0], ((1,), (1,)))), got_table)

    squares = means_table[1] - diag_weight * diag
    terms = (1.0 - diag) * (1.0 - diag) - OFF_WEIGHT * diag * diag + squares
    loss_total = cube_sum(hold(jnp.sum(terms).reshape(1), *sent_table), "core", "feat")
    return grad_table, grad_text, loss_total / features


def solution(mesh):
    devices = mesh.devices
    split = Mesh(
        devices.reshape(Z_CHIPS, devices.shape[0] // (2 * Z_CHIPS), 2, devices.shape[1]),
        ("z", "y", "core", "feat"),
    )
    rows = ("z", "y", "core")
    placed = (P(rows, "feat"), P(rows, "feat"), P(None, "feat"), P(None, "feat"))
    return jax.shard_map(
        body,
        mesh=split,
        in_specs=placed,
        out_specs=(P(rows, "feat"), P(rows, "feat"), P()),
        check_vma=False,
    )
```

```python
import jax
import jax.numpy as jnp
from jax import lax
from jax.sharding import Mesh
from jax.sharding import PartitionSpec as P

OFF_WEIGHT = 0.1
EPS = 1e-05
Z_CHIPS = 4
F32 = jnp.float32
BF16 = jnp.bfloat16


def dot(a, b, dims):
    return lax.dot_general(a, b, (dims, ((), ())), preferred_element_type=F32)


def shift(x, axis, step):
    size = lax.axis_size(axis)
    return lax.ppermute(x, axis, [(i, (i + step) % size) for i in range(size)])


def flip(x, axis, bit=1):
    size = lax.axis_size(axis)
    return lax.ppermute(x, axis, [(i, i ^ bit) for i in range(size)])


def cube_sum(x, *axes):
    for axis in axes:
        bit = 1
        while bit < lax.axis_size(axis):
            x = x + flip(x, axis, bit)
            bit *= 2
    return x


def bdot(a, b, dims):
    return lax.dot_general(a, b, (dims, ((0,), (0,))), preferred_element_type=F32)


def own_block(x, index, count, axis):
    size = x.shape[axis] // count
    return lax.dynamic_slice_in_dim(x, index * size, size, axis)


def both_cores(x, axis=0):
    got = flip(x, "core")
    first = lax.axis_index("core") == 0
    return jnp.where(first, jnp.concatenate([x, got], axis), jnp.concatenate([got, x], axis))


def add_cores(x, axis=0):
    core = lax.axis_index("core")
    return own_block(x, core, 2, axis) + flip(own_block(x, 1 - core, 2, axis), "core")


def weight_blocks(proj):
    num_feat = lax.axis_size("feat")
    feat = lax.axis_index("feat")
    cols = own_block(proj, lax.axis_index("core"), 2, 1)
    return [own_block(cols, (feat - step) % num_feat, num_feat, 0) for step in range(num_feat)]


def swap_feat(x):
    return [shift(x, "feat", step) for step in range(1, lax.axis_size("feat"))]


def project(z, others, weights):
    for other, weight in zip(others, weights[1:]):
        z = z + dot(both_cores(other), weight, ((1,), (0,)))
    return z


def moments(z_table, z_text):
    count = z_table.shape[0]
    mean_table, mean_text = jnp.mean(z_table, axis=0), jnp.mean(z_text, axis=0)
    centered_table, centered_text = z_table - mean_table, z_text - mean_text
    state = jnp.stack(
        [
            mean_table,
            mean_text,
            jnp.sum(centered_table * centered_table, axis=0),
            jnp.sum(centered_text * centered_text, axis=0),
            jnp.sum(centered_table * centered_text, axis=0),
        ]
    )
    for axis in ("z", "y"):
        bit = 1
        while bit < lax.axis_size(axis):
            other = flip(state, axis, bit)
            gap = state[:2] - other[:2]
            moved = (count / 2) * jnp.concatenate([gap * gap, gap[:1] * gap[1:]], 0)
            state = jnp.concatenate([(state[:2] + other[:2]) / 2, state[2:] + other[2:] + moved], 0)
            count *= 2
            bit *= 2
    return state[:2], state[2:] / count


def send_own(own):
    return (
        flip(own, "z"),
        lax.ppermute(own, "z", [(1, 2), (2, 1)]),
        over_y(own),
    )


def send_near(near, mid):
    return (
        lax.ppermute(near, "z", [(1, 2), (2, 1)]),
        lax.ppermute(mid, "z", [(1, 0), (2, 3)]),
        over_y(near),
    )


def at_end(end, inner):
    z = lax.axis_index("z")
    return jnp.where((z == 0) | (z == Z_CHIPS - 1), end, inner)


def over_y(x):
    return [flip(x, "y", step) for step in range(1, lax.axis_size("y"))]


def gram_part(half, rows):
    return add_cores(bdot(half, rows, ((2,), (2,))), 1)


def add_feat(mine, others):
    for other in others:
        mine = mine + other.astype(F32)
    return both_cores(mine.astype(BF16), 1)


def swap_parts(sent):
    num_feat = lax.axis_size("feat")
    return [shift(part, "feat", num_feat - step) for step, part in enumerate(sent, 1)]


def body(table, text, table_proj, text_proj):
    pairs = table.shape[0] * 2 * lax.axis_size("z") * lax.axis_size("y")
    features = table_proj.shape[1] * lax.axis_size("feat")
    table_weights = weight_blocks(table_proj)
    text_weights = weight_blocks(text_proj)

    others_table = swap_feat(table)
    z_table = dot(both_cores(table), table_weights[0], ((1,), (0,)))
    z_text = dot(both_cores(text), text_weights[0], ((1,), (0,)))
    text, z_table, z_text, *others_table = lax.optimization_barrier((text, z_table, z_text, *others_table))
    others_text = swap_feat(text)

    z_table = project(z_table, others_table, table_weights)
    z_text = project(z_text, others_text, text_weights)
    centers, spreads = moments(z_table, z_text)
    inverses = lax.rsqrt(spreads[:2] + EPS)
    diag = spreads[2] * inverses[0] * inverses[1]
    diag_weight = (diag - 1.0).astype(BF16).astype(F32) - OFF_WEIGHT * diag
    normed_table = (z_table - centers[0]) * inverses[0]
    normed_text = (z_text - centers[1]) * inverses[1]
    half_table, half_text = normed_table.astype(BF16), normed_text.astype(BF16)
    half = jnp.stack([half_table, half_text])

    near, mid, y_own = lax.optimization_barrier(send_own(half))
    far_in, far_end, y_near = lax.optimization_barrier(send_near(near, mid))
    far = at_end(far_end, far_in)
    last_end = lax.ppermute(far_in, "z", [(1, 0), (2, 3)])
    y_far_table = over_y(far[:1])

    rows_first = jnp.concatenate([half, near, *y_own, *y_near], 1)
    gram_first = gram_part(half, rows_first)
    others_first = swap_feat(gram_first.astype(BF16))
    far, gram_first = lax.optimization_barrier((far, gram_first))
    y_far_text = over_y(far[1:])

    last_end, y_far_table, y_far_text, others_first = lax.optimization_barrier((last_end, y_far_table, y_far_text, others_first))
    last = at_end(last_end, mid)
    cut = half.shape[1] // 2
    y_last = over_y(last[:, :cut])
    y_flip_table = [flip(block[:, cut:], "z") for block in y_far_table]

    y_far = [jnp.concatenate(parts, 0) for parts in zip(y_far_table, y_far_text)]
    rows_second = jnp.concatenate([far, last, *y_far], 1)
    gram_second = gram_part(half, rows_second)
    others_second = swap_feat(gram_second.astype(BF16))
    y_far_text, gram_second = lax.optimization_barrier((y_far_text, gram_second))
    y_flip_text = [flip(block[:, cut:], "z") for block in y_far_text]
    gram_first = add_feat(gram_first, others_first)

    y_last, y_flip_table, y_flip_text, gram_first = lax.optimization_barrier((y_last, y_flip_table, y_flip_text, gram_first))
    y_flip = [jnp.concatenate(parts, 0) for parts in zip(y_flip_table, y_flip_text)]
    rows_third = jnp.concatenate([part for parts in zip(y_last, y_flip) for part in parts], 1)
    gram_third = gram_part(half, rows_third)
    gram_third, others_second = lax.optimization_barrier((gram_third, others_second))
    others_third = swap_feat(gram_third.astype(BF16))
    gram_second = add_feat(gram_second, others_second)
    gram_third = add_feat(gram_third, others_third)

    off_table, off_text = 0.0, 0.0
    for gram, rows in zip((gram_first, gram_second, gram_third), (rows_first, rows_second, rows_third)):
        off_table = off_table + dot(gram[1], rows[0], ((1,), (0,)))
        off_text = off_text + dot(gram[0], rows[1], ((1,), (0,)))
    d_table = (OFF_WEIGHT / pairs) * off_table + half_text.astype(F32) * diag_weight
    d_text = (OFF_WEIGHT / pairs) * off_text + half_table.astype(F32) * diag_weight
    sums = jnp.stack(
        [jnp.sum(d_table, axis=0), jnp.sum(d_table * normed_table, axis=0), jnp.sum(d_text, axis=0), jnp.sum(d_text * normed_text, axis=0)]
    )
    means = cube_sum(sums, "z", "y") / pairs

    back_text = (inverses[1] * (d_text - means[2] - normed_text * means[3])).astype(BF16)
    back_table = (inverses[0] * (d_table - means[0] - normed_table * means[1])).astype(BF16)
    parts_text = [dot(back_text, weight, ((1,), (1,))) for weight in text_weights[1:]]
    back_table, *parts_text = lax.optimization_barrier((back_table, *parts_text))
    sent_text = [add_cores(part).astype(BF16) for part in parts_text]
    parts_table = [dot(back_table, weight, ((1,), (1,))) for weight in table_weights[1:]]
    back_text, parts_table, sent_text = lax.optimization_barrier((back_text, parts_table, sent_text))
    got_text = swap_parts(sent_text)
    sent_table = [add_cores(part).astype(BF16) for part in parts_table]
    back_text, sent_table = lax.optimization_barrier((back_text, sent_table))
    own_text = dot(back_text, text_weights[0], ((1,), (1,)))
    got_table = swap_parts(sent_table)
    back_table, own_text = lax.optimization_barrier((back_table, own_text))
    own_table = dot(back_table, table_weights[0], ((1,), (1,)))
    own_table, *got_text = lax.optimization_barrier((own_table, *got_text))
    squares = means[1] - diag_weight * diag
    terms = (1.0 - diag) * (1.0 - diag) - OFF_WEIGHT * diag * diag + squares
    loss_part, own_table = lax.optimization_barrier((jnp.sum(terms).reshape(1), own_table))
    loss_total = cube_sum(loss_part, "core", "feat")
    grad_text = add_cores(own_text) + sum(part.astype(F32) for part in got_text)
    grad_table = add_cores(own_table) + sum(part.astype(F32) for part in got_table)
    return grad_table, grad_text, loss_total / features


def solution(mesh):
    devices = mesh.devices
    split = Mesh(
        devices.reshape(Z_CHIPS, devices.shape[0] // (2 * Z_CHIPS), 2, devices.shape[1]),
        ("z", "y", "core", "feat"),
    )
    rows = ("z", "y", "core")
    placed = (P(rows, "feat"), P(rows, "feat"), P(None, "feat"), P(None, "feat"))
    return jax.shard_map(
        body,
        mesh=split,
        in_specs=placed,
        out_specs=(P(rows, "feat"), P(rows, "feat"), P()),
        check_vma=False,
    )
```

```python
import jax
import jax.numpy as jnp
from jax import lax
from jax.sharding import Mesh
from jax.sharding import PartitionSpec as P

OFF_WEIGHT = 0.1
EPS = 1e-05
Z_CHIPS = 4
F32 = jnp.float32
BF16 = jnp.bfloat16


def dot(a, b, dims):
    return lax.dot_general(a, b, (dims, ((), ())), preferred_element_type=F32)


def shift(x, axis, step):
    size = lax.axis_size(axis)
    return lax.ppermute(x, axis, [(i, (i + step) % size) for i in range(size)])


def flip(x, axis, bit=1):
    size = lax.axis_size(axis)
    return lax.ppermute(x, axis, [(i, i ^ bit) for i in range(size)])


def cube_sum(x, *axes):
    for axis in axes:
        bit = 1
        while bit < lax.axis_size(axis):
            x = x + flip(x, axis, bit)
            bit *= 2
    return x


def own_block(x, index, count, axis):
    size = x.shape[axis] // count
    return lax.dynamic_slice_in_dim(x, index * size, size, axis)


def both_cores(x, axis=0):
    got = flip(x, "core")
    first = lax.axis_index("core") == 0
    return jnp.where(first, jnp.concatenate([x, got], axis), jnp.concatenate([got, x], axis))


def add_cores(x, axis=0):
    core = lax.axis_index("core")
    return own_block(x, core, 2, axis) + flip(own_block(x, 1 - core, 2, axis), "core")


def weight_blocks(proj):
    num_feat = lax.axis_size("feat")
    feat = lax.axis_index("feat")
    cols = own_block(proj, lax.axis_index("core"), 2, 1)
    return [own_block(cols, (feat - step) % num_feat, num_feat, 0) for step in range(num_feat)]


def swap_feat(x):
    return [shift(x, "feat", step) for step in range(1, lax.axis_size("feat"))]


def project(z, others, weights):
    for other, weight in zip(others, weights[1:]):
        z = z + dot(both_cores(other), weight, ((1,), (0,)))
    return z


def merge_moments(state, count, other_gaps=()):
    gaps = []
    for axis in ("z", "y"):
        bit = 1
        while bit < lax.axis_size(axis):
            got = flip(state, axis, bit)
            gap = state[0] - got[0]
            moved = [gap * gap] + [gap * other for other in other_gaps[len(gaps) : len(gaps) + 1]]
            state = jnp.stack(
                [(state[0] + got[0]) / 2] + [a + b + (count / 2) * m for a, b, m in zip(state[1:], got[1:], moved)]
            )
            gaps.append(gap)
            count *= 2
            bit *= 2
    return state, gaps


def over_y(x):
    return [flip(x, "y", step) for step in range(1, lax.axis_size("y"))]


def add_feat(mine, others):
    for other in others:
        mine = mine + other.astype(F32)
    return both_cores(mine.astype(BF16))


def column_sums(partial, plane, own, normed):
    return jnp.stack(
        [
            jnp.sum(partial, axis=0) + jnp.sum(own, axis=0),
            jnp.sum(partial * plane.astype(F32), axis=0) + jnp.sum(own * normed, axis=0),
        ]
    )


def returned(partial, rows):
    return [flip(partial[step * rows : (step + 1) * rows].astype(BF16), "y", step) for step in range(1, lax.axis_size("y"))]


def add_returned(partial, got, own):
    d = partial[: own.shape[0]] + own
    for part in got:
        d = d + part.astype(F32)
    return d


def backward(d, normed, inverse, means):
    return (inverse * (d - means[0] - normed * means[1])).astype(BF16)


def swap_parts(sent):
    num_feat = lax.axis_size("feat")
    return [shift(part, "feat", num_feat - step) for step, part in enumerate(sent, 1)]


def body(table, text, table_proj, text_proj):
    pairs = table.shape[0] * 2 * lax.axis_size("z") * lax.axis_size("y")
    features = table_proj.shape[1] * lax.axis_size("feat")
    table_weights = weight_blocks(table_proj)
    text_weights = weight_blocks(text_proj)

    others_table = swap_feat(table)
    z_table = dot(both_cores(table), table_weights[0], ((1,), (0,)))
    z_text = dot(both_cores(text), text_weights[0], ((1,), (0,)))
    text, z_table, z_text, *others_table = lax.optimization_barrier((text, z_table, z_text, *others_table))
    others_text = swap_feat(text)

    z_table = project(z_table, others_table, table_weights)
    z_table, others_text = lax.optimization_barrier((z_table, others_text))
    rows = z_table.shape[0]
    mean_table = jnp.mean(z_table, axis=0)
    centered_table = z_table - mean_table
    state_table = jnp.stack([mean_table, jnp.sum(centered_table * centered_table, axis=0)])
    state_table, gaps_table = merge_moments(state_table, rows)
    inverse_table = lax.rsqrt(state_table[1] / pairs + EPS)
    normed_table = (z_table - state_table[0]) * inverse_table
    half_table = normed_table.astype(BF16)
    column_table = lax.all_gather(half_table, "z", axis=0, tiled=True)
    plane_table = jnp.concatenate([half_table, *over_y(half_table)], 0)

    z_text = project(z_text, others_text, text_weights)
    mean_text = jnp.mean(z_text, axis=0)
    centered_text = z_text - mean_text
    state_text = jnp.stack(
        [mean_text, jnp.sum(centered_text * centered_text, axis=0), jnp.sum(centered_text * centered_table, axis=0)]
    )
    state_text, _ = merge_moments(state_text, rows, gaps_table)
    inverse_text = lax.rsqrt(state_text[1] / pairs + EPS)
    normed_text = (z_text - state_text[0]) * inverse_text
    half_text = normed_text.astype(BF16)
    column_text = lax.all_gather(half_text, "z", axis=0, tiled=True)
    plane_text = jnp.concatenate([half_text, *over_y(half_text)], 0)

    diag = inverse_table * inverse_text * (state_text[2] / pairs)
    diag_weight = (diag - 1.0).astype(BF16).astype(F32) - OFF_WEIGHT * diag
    own_d_table = half_text.astype(F32) * diag_weight
    own_d_text = half_table.astype(F32) * diag_weight
    scale = OFF_WEIGHT / pairs

    gram_table = add_cores(dot(plane_table, column_table, ((1,), (1,))))
    gram_table = add_feat(gram_table, swap_feat(gram_table.astype(BF16)))
    column_text, gram_table = lax.optimization_barrier((column_text, gram_table))

    gram_text = add_cores(dot(plane_text, column_text, ((1,), (1,))))
    partial_text = scale * dot(gram_table, column_text, ((1,), (0,)))
    gram_text, partial_text = lax.optimization_barrier((gram_text, partial_text))
    others_gram = swap_feat(gram_text.astype(BF16))
    got_text = returned(partial_text, rows)
    sums_text = cube_sum(column_sums(partial_text, plane_text, own_d_text, normed_text), "z", "y")
    others_gram, got_text, sums_text = lax.optimization_barrier((others_gram, got_text, sums_text))

    gram_text = add_feat(gram_text, others_gram)
    d_text = add_returned(partial_text, got_text, own_d_text)
    back_text = backward(d_text, normed_text, inverse_text, sums_text / pairs)
    parts_text = [dot(back_text, weight, ((1,), (1,))) for weight in text_weights[1:]]
    partial_table = scale * dot(gram_text, column_table, ((1,), (0,)))
    partial_table, parts_text = lax.optimization_barrier((partial_table, parts_text))

    got_table = returned(partial_table, rows)
    sums_table = cube_sum(column_sums(partial_table, plane_table, own_d_table, normed_table), "z", "y")
    sent_text = [add_cores(part).astype(BF16) for part in parts_text]
    back_text, sent_text = lax.optimization_barrier((back_text, sent_text))
    grads_text = swap_parts(sent_text)
    own_text = dot(back_text, text_weights[0], ((1,), (1,)))
    sums_table, got_table, own_text, grads_text = lax.optimization_barrier((sums_table, got_table, own_text, grads_text))

    means_table = sums_table / pairs
    d_table = add_returned(partial_table, got_table, own_d_table)
    back_table = backward(d_table, normed_table, inverse_table, means_table)
    sent_table = [add_cores(dot(back_table, weight, ((1,), (1,)))).astype(BF16) for weight in table_weights[1:]]
    back_table, sent_table = lax.optimization_barrier((back_table, sent_table))
    grads_table = swap_parts(sent_table)
    own_table = dot(back_table, table_weights[0], ((1,), (1,)))

    squares = means_table[1] - diag_weight * diag
    terms = (1.0 - diag) * (1.0 - diag) - OFF_WEIGHT * diag * diag + squares
    loss_part, own_table = lax.optimization_barrier((jnp.sum(terms).reshape(1), own_table))
    loss_total = cube_sum(loss_part, "core", "feat")
    grad_text = add_cores(own_text) + sum(part.astype(F32) for part in grads_text)
    grad_table = add_cores(own_table) + sum(part.astype(F32) for part in grads_table)
    return grad_table, grad_text, loss_total / features


def solution(mesh):
    devices = mesh.devices
    split = Mesh(
        devices.reshape(Z_CHIPS, devices.shape[0] // (2 * Z_CHIPS), 2, devices.shape[1]),
        ("z", "y", "core", "feat"),
    )
    rows = ("z", "y", "core")
    placed = (P(rows, "feat"), P(rows, "feat"), P(None, "feat"), P(None, "feat"))
    return jax.shard_map(
        body,
        mesh=split,
        in_specs=placed,
        out_specs=(P(rows, "feat"), P(rows, "feat"), P()),
        check_vma=False,
    )
```

```python
import jax
import jax.numpy as jnp
from jax import lax
from jax.sharding import Mesh
from jax.sharding import PartitionSpec as P

OFF_WEIGHT = 0.1
EPS = 1e-05
Z_CHIPS = 4
F32 = jnp.float32
BF16 = jnp.bfloat16


def dot(a, b, dims):
    return lax.dot_general(a, b, (dims, ((), ())), preferred_element_type=F32)


def shift(x, axis, step):
    size = lax.axis_size(axis)
    return lax.ppermute(x, axis, [(i, (i + step) % size) for i in range(size)])


def flip(x, axis, bit=1):
    size = lax.axis_size(axis)
    return lax.ppermute(x, axis, [(i, i ^ bit) for i in range(size)])


def cube_sum(x, *axes):
    for axis in axes:
        bit = 1
        while bit < lax.axis_size(axis):
            x = x + flip(x, axis, bit)
            bit *= 2
    return x


def own_block(x, index, count, axis):
    size = x.shape[axis] // count
    return lax.dynamic_slice_in_dim(x, index * size, size, axis)


def both_cores(x, axis=0):
    got = flip(x, "core")
    first = lax.axis_index("core") == 0
    return jnp.where(first, jnp.concatenate([x, got], axis), jnp.concatenate([got, x], axis))


def add_cores(x, axis=0):
    core = lax.axis_index("core")
    return own_block(x, core, 2, axis) + flip(own_block(x, 1 - core, 2, axis), "core")


def weight_blocks(proj):
    num_feat = lax.axis_size("feat")
    feat = lax.axis_index("feat")
    cols = own_block(proj, lax.axis_index("core"), 2, 1)
    return [own_block(cols, (feat - step) % num_feat, num_feat, 0) for step in range(num_feat)]


def swap_feat(x):
    return [shift(x, "feat", step) for step in range(1, lax.axis_size("feat"))]


def project(z, others, weights):
    for other, weight in zip(others, weights[1:]):
        z = z + dot(both_cores(other), weight, ((1,), (0,)))
    return z


def merge_moments(z_table, z_text):
    count = z_table.shape[0]
    mean_table, mean_text = jnp.mean(z_table, axis=0), jnp.mean(z_text, axis=0)
    centered_table, centered_text = z_table - mean_table, z_text - mean_text
    squares = [centered_table * centered_table, centered_text * centered_text, centered_table * centered_text]
    state = jnp.stack([mean_table, mean_text] + [jnp.sum(part, axis=0) for part in squares])
    for axis in ("z", "y"):
        bit = 1
        while bit < lax.axis_size(axis):
            got = flip(state, axis, bit)
            gap = state[:2] - got[:2]
            moved = (count / 2) * jnp.concatenate([gap * gap, gap[:1] * gap[1:]], 0)
            state = jnp.concatenate([(state[:2] + got[:2]) / 2, state[2:] + got[2:] + moved], 0)
            count *= 2
            bit *= 2
    return state[:2], state[2:] / count


def at_end(end, inner):
    z = lax.axis_index("z")
    return jnp.where((z == 0) | (z == Z_CHIPS - 1), end, inner)


def send_own(own):
    return flip(own, "z"), lax.ppermute(own, "z", [(1, 2), (2, 1)])


def send_near(near, mid):
    return lax.ppermute(near, "z", [(1, 2), (2, 1)]), lax.ppermute(mid, "z", [(1, 0), (2, 3)])


def send_far(far_in):
    return lax.ppermute(far_in, "z", [(1, 0), (2, 3)])


def over_y(x):
    return [flip(x, "y", step) for step in range(1, lax.axis_size("y"))]


def add_feat(mine, others):
    for other in others:
        mine = mine + other.astype(F32)
    return both_cores(mine.astype(BF16))


def column_sums(partial, plane, own, normed):
    return jnp.stack(
        [
            jnp.sum(partial, axis=0) + jnp.sum(own, axis=0),
            jnp.sum(partial * plane.astype(F32), axis=0) + jnp.sum(own * normed, axis=0),
        ]
    )


def returned(partial, rows):
    cut = rows // 2
    steps = range(1, lax.axis_size("y"))
    return [
        [flip(partial[step * rows + at : step * rows + at + cut].astype(BF16), "y", step) for step in steps] for at in (0, cut)
    ]


def add_returned(partial, got, own):
    d = partial[: own.shape[0]] + own
    for parts in zip(*got):
        d = d + jnp.concatenate(parts, 0).astype(F32)
    return d


def backward(d, normed, inverse, means):
    return (inverse * (d - means[0] - normed * means[1])).astype(BF16)


def swap_parts(sent):
    num_feat = lax.axis_size("feat")
    return [shift(part, "feat", num_feat - step) for step, part in enumerate(sent, 1)]


def body(table, text, table_proj, text_proj):
    pairs = table.shape[0] * 2 * lax.axis_size("z") * lax.axis_size("y")
    features = table_proj.shape[1] * lax.axis_size("feat")
    table_weights = weight_blocks(table_proj)
    text_weights = weight_blocks(text_proj)

    others_table = swap_feat(table)
    z_table = dot(both_cores(table), table_weights[0], ((1,), (0,)))
    z_text = dot(both_cores(text), text_weights[0], ((1,), (0,)))
    others_text = swap_feat(text)
    z_table, z_text, others_table = lax.optimization_barrier((z_table, z_text, others_table))
    z_table = project(z_table, others_table, table_weights)
    z_table, others_text = lax.optimization_barrier((z_table, others_text))
    z_text = project(z_text, others_text, text_weights)
    rows = z_table.shape[0]
    centers, spreads = merge_moments(z_table, z_text)
    inverse_table, inverse_text = lax.rsqrt(spreads[0] + EPS), lax.rsqrt(spreads[1] + EPS)
    diag = inverse_table * inverse_text * spreads[2]
    diag_weight = (diag - 1.0).astype(BF16).astype(F32) - OFF_WEIGHT * diag
    normed_table = (z_table - centers[0]) * inverse_table
    normed_text = (z_text - centers[1]) * inverse_text
    half_table, half_text = normed_table.astype(BF16), normed_text.astype(BF16)

    plane = over_y(jnp.stack([half_table, half_text]))
    near_table, mid_table = lax.optimization_barrier(send_own(half_table))
    far_in_table, far_end_table, near_text, mid_text = lax.optimization_barrier(
        send_near(near_table, mid_table) + send_own(half_text)
    )
    last_end_table, far_in_text, far_end_text = lax.optimization_barrier(
        (send_far(far_in_table), *send_near(near_text, mid_text))
    )
    last_end_text = send_far(far_in_text)
    last_table, last_text = at_end(last_end_table, mid_table), at_end(last_end_text, mid_text)
    far_table, far_text = at_end(far_end_table, far_in_table), at_end(far_end_text, far_in_text)
    column_table = jnp.concatenate([half_table, near_table, far_table, last_table], 0)
    column_text = jnp.concatenate([half_text, near_text, far_text, last_text], 0)
    plane_table = jnp.concatenate([half_table] + [block[0] for block in plane], 0)
    plane_text = jnp.concatenate([half_text] + [block[1] for block in plane], 0)

    own_d_table = half_text.astype(F32) * diag_weight
    own_d_text = half_table.astype(F32) * diag_weight
    scale = OFF_WEIGHT / pairs

    gram_table = add_cores(dot(plane_table, column_table, ((1,), (1,))))
    gram_table = add_feat(gram_table, swap_feat(gram_table.astype(BF16)))

    gram_text = add_cores(dot(plane_text, column_text, ((1,), (1,))))
    others_gram = swap_feat(gram_text.astype(BF16))
    partial_text = scale * dot(gram_table, column_text, ((1,), (0,)))
    got_text = returned(partial_text, rows)
    sums_text = cube_sum(column_sums(partial_text, plane_text, own_d_text, normed_text), "z")
    others_gram, sums_text, got_text[0] = lax.optimization_barrier((others_gram, sums_text, got_text[0]))
    gram_text = add_feat(gram_text, others_gram)
    sums_text = cube_sum(sums_text, "y")
    gram_text, got_text[1], sums_text = lax.optimization_barrier((gram_text, got_text[1], sums_text))

    d_text = add_returned(partial_text, got_text, own_d_text)
    back_text = backward(d_text, normed_text, inverse_text, sums_text / pairs)
    parts_text = [dot(back_text, weight, ((1,), (1,))) for weight in text_weights[1:]]
    partial_table = scale * dot(gram_text, column_table, ((1,), (0,)))
    partial_table, parts_text = lax.optimization_barrier((partial_table, parts_text))

    got_table = returned(partial_table, rows)
    sums_table = cube_sum(column_sums(partial_table, plane_table, own_d_table, normed_table), "z")
    sent_text = [add_cores(part).astype(BF16) for part in parts_text]
    own_text = dot(back_text, text_weights[0], ((1,), (1,)))
    sums_table, sent_text, own_text, got_table[0] = lax.optimization_barrier((sums_table, sent_text, own_text, got_table[0]))
    grads_text = swap_parts(sent_text)
    sums_table = cube_sum(sums_table, "y")
    sums_table, got_table[1], grads_text = lax.optimization_barrier((sums_table, got_table[1], grads_text))

    means_table = sums_table / pairs
    d_table = add_returned(partial_table, got_table, own_d_table)
    back_table = backward(d_table, normed_table, inverse_table, means_table)
    sent_table = [add_cores(dot(back_table, weight, ((1,), (1,)))).astype(BF16) for weight in table_weights[1:]]
    own_table = dot(back_table, table_weights[0], ((1,), (1,)))
    own_table, sent_table = lax.optimization_barrier((own_table, sent_table))
    grads_table = swap_parts(sent_table)

    squares = means_table[1] - diag_weight * diag
    terms = (1.0 - diag) * (1.0 - diag) - OFF_WEIGHT * diag * diag + squares
    loss_part, own_table = lax.optimization_barrier((jnp.sum(terms).reshape(1), own_table))
    loss_total = cube_sum(loss_part, "core", "feat")
    grad_text = add_cores(own_text) + sum(part.astype(F32) for part in grads_text)
    grad_table = add_cores(own_table) + sum(part.astype(F32) for part in grads_table)
    return grad_table, grad_text, loss_total / features


def solution(mesh):
    devices = mesh.devices
    split = Mesh(
        devices.reshape(Z_CHIPS, devices.shape[0] // (2 * Z_CHIPS), 2, devices.shape[1]),
        ("z", "y", "core", "feat"),
    )
    rows = ("z", "y", "core")
    placed = (P(rows, "feat"), P(rows, "feat"), P(None, "feat"), P(None, "feat"))
    return jax.shard_map(
        body,
        mesh=split,
        in_specs=placed,
        out_specs=(P(rows, "feat"), P(rows, "feat"), P()),
        check_vma=False,
    )
```

```python
import jax
import jax.numpy as jnp
from jax import lax
from jax.sharding import Mesh
from jax.sharding import PartitionSpec as P

OFF_WEIGHT = 0.1
EPS = 1e-05
Z_CHIPS = 4
F32 = jnp.float32
BF16 = jnp.bfloat16


def dot(a, b, dims):
    return lax.dot_general(a, b, (dims, ((), ())), preferred_element_type=F32)


def shift(x, axis, step):
    size = lax.axis_size(axis)
    return lax.ppermute(x, axis, [(i, (i + step) % size) for i in range(size)])


def flip(x, axis, bit=1):
    size = lax.axis_size(axis)
    return lax.ppermute(x, axis, [(i, i ^ bit) for i in range(size)])


def cube_sum(x, *axes):
    for axis in axes:
        bit = 1
        while bit < lax.axis_size(axis):
            x = x + flip(x, axis, bit)
            bit *= 2
    return x


def own_block(x, index, count, axis):
    size = x.shape[axis] // count
    return lax.dynamic_slice_in_dim(x, index * size, size, axis)


def both_cores(x, axis=0):
    got = flip(x, "core")
    first = lax.axis_index("core") == 0
    return jnp.where(first, jnp.concatenate([x, got], axis), jnp.concatenate([got, x], axis))


def add_cores(x, axis=0):
    core = lax.axis_index("core")
    return own_block(x, core, 2, axis) + flip(own_block(x, 1 - core, 2, axis), "core")


def weight_blocks(proj):
    num_feat = lax.axis_size("feat")
    feat = lax.axis_index("feat")
    cols = own_block(proj, lax.axis_index("core"), 2, 1)
    return [own_block(cols, (feat - step) % num_feat, num_feat, 0) for step in range(num_feat)]


def swap_feat(x):
    return [shift(x, "feat", step) for step in range(1, lax.axis_size("feat"))]


def project(z, others, weights):
    for other, weight in zip(others, weights[1:]):
        z = z + dot(both_cores(other), weight, ((1,), (0,)))
    return z


def merge_moments(z_table, z_text):
    count = z_table.shape[0]
    mean_table, mean_text = jnp.mean(z_table, axis=0), jnp.mean(z_text, axis=0)
    centered_table, centered_text = z_table - mean_table, z_text - mean_text
    squares = [centered_table * centered_table, centered_text * centered_text, centered_table * centered_text]
    state = jnp.stack([mean_table, mean_text] + [jnp.sum(part, axis=0) for part in squares])
    for axis in ("z", "y"):
        bit = 1
        while bit < lax.axis_size(axis):
            got = flip(state, axis, bit)
            gap = state[:2] - got[:2]
            moved = (count / 2) * jnp.concatenate([gap * gap, gap[:1] * gap[1:]], 0)
            state = jnp.concatenate([(state[:2] + got[:2]) / 2, state[2:] + got[2:] + moved], 0)
            count *= 2
            bit *= 2
    return state[:2], state[2:] / count


def at_end(end, inner):
    z = lax.axis_index("z")
    return jnp.where((z == 0) | (z == Z_CHIPS - 1), end, inner)


def send_own(own):
    return flip(own, "z"), lax.ppermute(own, "z", [(1, 2), (2, 1)])


def send_near(near, mid):
    return lax.ppermute(near, "z", [(1, 2), (2, 1)]), lax.ppermute(mid, "z", [(1, 0), (2, 3)])


def send_far(far_in):
    return lax.ppermute(far_in, "z", [(1, 0), (2, 3)])


def over_y(x):
    return [flip(x, "y", step) for step in range(1, lax.axis_size("y"))]


def add_feat(mine, others):
    for other in others:
        mine = mine + other.astype(F32)
    return both_cores(mine.astype(BF16))


def column_sums(partial, plane, own, normed):
    return jnp.stack(
        [
            jnp.sum(partial, axis=0) + jnp.sum(own, axis=0),
            jnp.sum(partial * plane.astype(F32), axis=0) + jnp.sum(own * normed, axis=0),
        ]
    )


def returned(partial, rows):
    cut = rows // 2
    steps = range(1, lax.axis_size("y"))
    return [
        [flip(partial[step * rows + at : step * rows + at + cut].astype(BF16), "y", step) for step in steps] for at in (0, cut)
    ]


def add_returned(partial, got, own):
    d = partial[: own.shape[0]] + own
    for parts in zip(*got):
        d = d + jnp.concatenate(parts, 0).astype(F32)
    return d


def backward(d, normed, inverse, means):
    return (inverse * (d - means[0] - normed * means[1])).astype(BF16)


def swap_parts(sent):
    num_feat = lax.axis_size("feat")
    return [shift(part, "feat", num_feat - step) for step, part in enumerate(sent, 1)]


def body(table, text, table_proj, text_proj):
    pairs = table.shape[0] * 2 * lax.axis_size("z") * lax.axis_size("y")
    features = table_proj.shape[1] * lax.axis_size("feat")
    table_weights = weight_blocks(table_proj)
    text_weights = weight_blocks(text_proj)

    others_table = swap_feat(table)
    z_table = dot(both_cores(table), table_weights[0], ((1,), (0,)))
    z_text = dot(both_cores(text), text_weights[0], ((1,), (0,)))
    others_text = swap_feat(text)
    z_table, z_text, others_table = lax.optimization_barrier((z_table, z_text, others_table))
    z_table = project(z_table, others_table, table_weights)
    z_table, others_text = lax.optimization_barrier((z_table, others_text))
    z_text = project(z_text, others_text, text_weights)
    rows = z_table.shape[0]
    centers, spreads = merge_moments(z_table, z_text)
    inverse_table, inverse_text = lax.rsqrt(spreads[0] + EPS), lax.rsqrt(spreads[1] + EPS)
    diag = inverse_table * inverse_text * spreads[2]
    diag_weight = (diag - 1.0).astype(BF16).astype(F32) - OFF_WEIGHT * diag
    normed_table = (z_table - centers[0]) * inverse_table
    normed_text = (z_text - centers[1]) * inverse_text
    half_table, half_text = normed_table.astype(BF16), normed_text.astype(BF16)

    plane = over_y(jnp.stack([half_table, half_text]))
    near_table, mid_table = lax.optimization_barrier(send_own(half_table))
    far_in_table, far_end_table = lax.optimization_barrier(send_near(near_table, mid_table))
    last_end_table, near_text, mid_text = lax.optimization_barrier((send_far(far_in_table), *send_own(half_text)))
    far_in_text, far_end_text = send_near(near_text, mid_text)

    last_table, far_table = at_end(last_end_table, mid_table), at_end(far_end_table, far_in_table)
    column_table = jnp.concatenate([half_table, near_table, far_table, last_table], 0)
    plane_table = jnp.concatenate([half_table] + [block[0] for block in plane], 0)
    gram_table = add_cores(dot(plane_table, column_table, ((1,), (1,))))
    far_in_text, far_end_text, gram_table = lax.optimization_barrier((far_in_text, far_end_text, gram_table))
    last_end_text = send_far(far_in_text)
    others_gram_table = swap_feat(gram_table.astype(BF16))
    last_end_text, others_gram_table = lax.optimization_barrier((last_end_text, others_gram_table))

    last_text, far_text = at_end(last_end_text, mid_text), at_end(far_end_text, far_in_text)
    column_text = jnp.concatenate([half_text, near_text, far_text, last_text], 0)
    plane_text = jnp.concatenate([half_text] + [block[1] for block in plane], 0)
    own_d_table = half_text.astype(F32) * diag_weight
    own_d_text = half_table.astype(F32) * diag_weight
    scale = OFF_WEIGHT / pairs

    gram_text = add_cores(dot(plane_text, column_text, ((1,), (1,))))
    gram_table = add_feat(gram_table, others_gram_table)
    others_gram_text = swap_feat(gram_text.astype(BF16))
    partial_text = scale * dot(gram_table, column_text, ((1,), (0,)))
    sums_text = cube_sum(column_sums(partial_text, plane_text, own_d_text, normed_text), "y")
    got_text = returned(partial_text, rows)
    sums_text = cube_sum(sums_text, "z")
    got_text[0], sums_text, others_gram_text = lax.optimization_barrier((got_text[0], sums_text, others_gram_text))

    gram_text = add_feat(gram_text, others_gram_text)
    partial_table = scale * dot(gram_text, column_table, ((1,), (0,)))
    sums_table = column_sums(partial_table, plane_table, own_d_table, normed_table)
    sums_table, got_text[1] = lax.optimization_barrier((sums_table, got_text[1]))
    sums_table = cube_sum(sums_table, "y")
    d_text = add_returned(partial_text, got_text, own_d_text)
    back_text = backward(d_text, normed_text, inverse_text, sums_text / pairs)
    sums_table, back_text = lax.optimization_barrier((sums_table, back_text))
    got_table = returned(partial_table, rows)
    parts_text = [dot(back_text, weight, ((1,), (1,))) for weight in text_weights[1:]]
    sums_table = sums_table + flip(sums_table, "z", 1)
    sums_table, parts_text, got_table[0] = lax.optimization_barrier((sums_table, parts_text, got_table[0]))
    sent_text = [add_cores(part).astype(BF16) for part in parts_text]
    sums_table = sums_table + flip(sums_table, "z", 2)
    own_text = dot(back_text, text_weights[0], ((1,), (1,)))
    sent_text, own_text, sums_table = lax.optimization_barrier((sent_text, own_text, sums_table))
    grads_text = [swap_parts([jnp.split(part, 2)[i] for part in sent_text]) for i in range(2)]
    sums_table, got_table[1], grads_text[0] = lax.optimization_barrier((sums_table, got_table[1], grads_text[0]))

    means_table = sums_table / pairs
    d_table = add_returned(partial_table, got_table, own_d_table)
    back_table = backward(d_table, normed_table, inverse_table, means_table)
    parts_table = [dot(back_table, weight, ((1,), (1,))) for weight in table_weights[1:]]
    sent_table = [add_cores(part).astype(BF16) for part in parts_table]
    own_table = dot(back_table, table_weights[0], ((1,), (1,)))
    own_table, sent_table, grads_text[1] = lax.optimization_barrier((own_table, sent_table, grads_text[1]))
    grads_table = swap_parts(sent_table)

    squares = means_table[1] - diag_weight * diag
    terms = (1.0 - diag) * (1.0 - diag) - OFF_WEIGHT * diag * diag + squares
    loss_part, own_table = lax.optimization_barrier((jnp.sum(terms).reshape(1), own_table))
    loss_total = cube_sum(loss_part, "core", "feat")
    grads_text = [jnp.concatenate(parts, 0) for parts in zip(*grads_text)]
    grad_text = add_cores(own_text) + sum(part.astype(F32) for part in grads_text)
    grad_table = add_cores(own_table) + sum(part.astype(F32) for part in grads_table)
    return grad_table, grad_text, loss_total / features


def solution(mesh):
    devices = mesh.devices
    split = Mesh(
        devices.reshape(Z_CHIPS, devices.shape[0] // (2 * Z_CHIPS), 2, devices.shape[1]),
        ("z", "y", "core", "feat"),
    )
    rows = ("z", "y", "core")
    placed = (P(rows, "feat"), P(rows, "feat"), P(None, "feat"), P(None, "feat"))
    return jax.shard_map(
        body,
        mesh=split,
        in_specs=placed,
        out_specs=(P(rows, "feat"), P(rows, "feat"), P()),
        check_vma=False,
    )
```

```python
import jax
import jax.numpy as jnp
from jax import lax
from jax.sharding import Mesh
from jax.sharding import PartitionSpec as P

OFF_WEIGHT = 0.1
EPS = 1e-05
Z_CHIPS = 4
F32 = jnp.float32
BF16 = jnp.bfloat16


def dot(a, b, dims):
    return lax.dot_general(a, b, (dims, ((), ())), preferred_element_type=F32)


def shift(x, axis, step):
    size = lax.axis_size(axis)
    return lax.ppermute(x, axis, [(i, (i + step) % size) for i in range(size)])


def flip(x, axis, bit=1):
    size = lax.axis_size(axis)
    return lax.ppermute(x, axis, [(i, i ^ bit) for i in range(size)])


def cube_sum(x, *axes):
    for axis in axes:
        bit = 1
        while bit < lax.axis_size(axis):
            x = x + flip(x, axis, bit)
            bit *= 2
    return x


def own_block(x, index, count, axis):
    size = x.shape[axis] // count
    return lax.dynamic_slice_in_dim(x, index * size, size, axis)


def both_cores(x, axis=0):
    got = flip(x, "core")
    first = lax.axis_index("core") == 0
    return jnp.where(first, jnp.concatenate([x, got], axis), jnp.concatenate([got, x], axis))


def add_cores(x, axis=0):
    core = lax.axis_index("core")
    return own_block(x, core, 2, axis) + flip(own_block(x, 1 - core, 2, axis), "core")


def weight_blocks(proj):
    num_feat = lax.axis_size("feat")
    feat = lax.axis_index("feat")
    cols = own_block(proj, lax.axis_index("core"), 2, 1)
    return [own_block(cols, (feat - step) % num_feat, num_feat, 0) for step in range(num_feat)]


def swap_feat(x):
    return [shift(x, "feat", step) for step in range(1, lax.axis_size("feat"))]


def project(z, others, weights):
    for other, weight in zip(others, weights[1:]):
        z = z + dot(both_cores(other), weight, ((1,), (0,)))
    return z


def gather_step(x, axis, bit):
    return jnp.concatenate([x, flip(x, axis, bit)], 0)


def merge(x):
    while x.shape[0] > 1:
        x = x[: x.shape[0] // 2] + x[x.shape[0] // 2 :]
    return x[0]


def split_two(x):
    high = x.astype(BF16)
    return high, (x - high.astype(F32)).astype(BF16)


def center_rows(z):
    mean = jnp.mean(z, axis=0)
    centered = z - mean
    return centered, mean, jnp.sum(centered * centered, axis=0)


def normalization(rows, means, squares, pairs):
    center = merge(means) / means.shape[0]
    offsets = means - center
    spread = (merge(squares) + rows * merge(offsets * offsets)) / pairs
    return lax.rsqrt(spread + EPS), offsets


def normalize_plane(centered, blocks, inverse, offsets):
    rows = [centered] + [block.astype(F32) for block in blocks]
    return jnp.concatenate([(part + offset) * inverse for part, offset in zip(rows, offsets)], 0)


def members(count, width):
    chips = jnp.repeat(jnp.arange(count, dtype=jnp.int32), width)
    return (jnp.arange(count, dtype=jnp.int32)[:, None] == chips[None, :]).astype(BF16)


def gram_part(plane, inverse, column, offsets):
    scaled = (plane * inverse).astype(BF16)
    count = offsets.shape[0]
    shifts = dot(scaled, jnp.concatenate(split_two(offsets), 0), ((1,), (1,)))
    shifts = jnp.concatenate(split_two(shifts[:, :count] + shifts[:, count:]), 1)
    chips = members(count, column.shape[0] // count)
    return dot(scaled, column, ((1,), (1,))) + dot(shifts, jnp.concatenate([chips, chips], 0), ((1,), (0,)))


def gram_times(gram, column, inverse, offsets):
    count = offsets.shape[0]
    sums = dot(gram, members(count, column.shape[0] // count), ((1,), (1,)))
    moved = lax.dot_general(
        sums, offsets, (((1,), (0,)), ((), ())), precision=lax.Precision.HIGHEST, preferred_element_type=F32
    )
    return inverse * (dot(gram, column, ((1,), (0,))) + moved)


def at_end(end, inner):
    z = lax.axis_index("z")
    return jnp.where((z == 0) | (z == Z_CHIPS - 1), end, inner)


def send_own(own):
    return flip(own, "z"), lax.ppermute(own, "z", [(1, 2), (2, 1)])


def send_near(near, mid):
    return lax.ppermute(near, "z", [(1, 2), (2, 1)]), lax.ppermute(mid, "z", [(1, 0), (2, 3)])


def send_far(far_in):
    return lax.ppermute(far_in, "z", [(1, 0), (2, 3)])


def over_y(x):
    return [flip(x, "y", step) for step in range(1, lax.axis_size("y"))]


def add_feat(mine, others):
    for other in others:
        mine = mine + other.astype(F32)
    return both_cores(mine.astype(BF16))


def column_sums(partial, plane, own, normed):
    return jnp.stack(
        [
            jnp.sum(partial, axis=0) + jnp.sum(own, axis=0),
            jnp.sum(partial * plane, axis=0) + jnp.sum(own * normed, axis=0),
        ]
    )


def returned(partial, rows):
    cut = rows // 2
    steps = range(1, lax.axis_size("y"))
    return [
        [flip(partial[step * rows + at : step * rows + at + cut].astype(BF16), "y", step) for step in steps] for at in (0, cut)
    ]


def add_returned(partial, got, own):
    d = partial[: own.shape[0]] + own
    for parts in zip(*got):
        d = d + jnp.concatenate(parts, 0).astype(F32)
    return d


def backward(d, normed, inverse, means):
    return (inverse * (d - means[0] - normed * means[1])).astype(BF16)


def swap_parts(sent):
    num_feat = lax.axis_size("feat")
    return [shift(part, "feat", num_feat - step) for step, part in enumerate(sent, 1)]


def body(table, text, table_proj, text_proj):
    pairs = table.shape[0] * 2 * lax.axis_size("z") * lax.axis_size("y")
    features = table_proj.shape[1] * lax.axis_size("feat")
    table_weights = weight_blocks(table_proj)
    text_weights = weight_blocks(text_proj)

    others_table = swap_feat(table)
    z_table = dot(both_cores(table), table_weights[0], ((1,), (0,)))
    z_text = dot(both_cores(text), text_weights[0], ((1,), (0,)))
    others_text = swap_feat(text)
    z_table, z_text, others_table = lax.optimization_barrier((z_table, z_text, others_table))
    z_table = project(z_table, others_table, table_weights)
    z_table, others_text = lax.optimization_barrier((z_table, others_text))
    rows = z_table.shape[0]
    y_size = lax.axis_size("y")
    centered_table, mean_table, square_table = center_rows(z_table)
    sent_rows_table = centered_table.astype(BF16)
    near_table, mid_table = send_own(sent_rows_table)

    z_text = project(z_text, others_text, text_weights)
    z_text, near_table, mid_table = lax.optimization_barrier((z_text, near_table, mid_table))
    centered_text, mean_text, square_text = center_rows(z_text)
    sent_rows_text = centered_text.astype(BF16)
    cross = jnp.sum(centered_table * centered_text, axis=0)
    stats = jnp.stack([mean_table, square_table, mean_text, square_text, cross])[None]
    while stats.shape[0] < y_size:
        stats = gather_step(stats, "y", stats.shape[0])

    stats = gather_step(stats, "z", 1)
    plane = over_y(jnp.stack([sent_rows_table, sent_rows_text]))
    far_in_table, far_end_table, near_text, mid_text, stats = lax.optimization_barrier(
        (*send_near(near_table, mid_table), *send_own(sent_rows_text), stats)
    )
    stats = gather_step(stats, "z", 2)
    last_end_table, far_in_text, far_end_text, stats = lax.optimization_barrier(
        (send_far(far_in_table), *send_near(near_text, mid_text), stats)
    )
    last_end_text = send_far(far_in_text)

    inverse_table, offsets_table = normalization(rows, stats[:, 0], stats[:, 1], pairs)
    inverse_text, offsets_text = normalization(rows, stats[:, 2], stats[:, 3], pairs)
    diag = inverse_table * inverse_text * ((merge(stats[:, 4]) + rows * merge(offsets_table * offsets_text)) / pairs)
    diag_weight = (diag - 1.0).astype(BF16).astype(F32) - OFF_WEIGHT * diag
    plane_table = normalize_plane(centered_table, [block[0] for block in plane], inverse_table, offsets_table)
    plane_text = normalize_plane(centered_text, [block[1] for block in plane], inverse_text, offsets_text)
    normed_table, normed_text = plane_table[:rows], plane_text[:rows]
    own_d_table = normed_text.astype(BF16).astype(F32) * diag_weight
    own_d_text = normed_table.astype(BF16).astype(F32) * diag_weight
    scale = OFF_WEIGHT / pairs
    moved_table, moved_text = offsets_table[::y_size], offsets_text[::y_size]

    last_table, far_table = at_end(last_end_table, mid_table), at_end(far_end_table, far_in_table)
    column_table = jnp.concatenate([sent_rows_table, near_table, far_table, last_table], 0)
    gram_table = add_cores(gram_part(plane_table, inverse_table, column_table, moved_table))
    others_gram_table = swap_feat(gram_table.astype(BF16))

    last_text, far_text = at_end(last_end_text, mid_text), at_end(far_end_text, far_in_text)
    column_text = jnp.concatenate([sent_rows_text, near_text, far_text, last_text], 0)
    gram_text = add_cores(gram_part(plane_text, inverse_text, column_text, moved_text))
    gram_table = add_feat(gram_table, others_gram_table)
    others_gram_text = swap_feat(gram_text.astype(BF16))
    partial_text = scale * gram_times(gram_table, column_text, inverse_text, moved_text)
    sums_text = cube_sum(column_sums(partial_text, plane_text, own_d_text, normed_text), "y")
    got_text = returned(partial_text, rows)
    sums_text = cube_sum(sums_text, "z")
    got_text[0], sums_text, others_gram_text = lax.optimization_barrier((got_text[0], sums_text, others_gram_text))

    gram_text = add_feat(gram_text, others_gram_text)
    partial_table = scale * gram_times(gram_text, column_table, inverse_table, moved_table)
    sums_table = column_sums(partial_table, plane_table, own_d_table, normed_table)
    sums_table, got_text[1] = lax.optimization_barrier((sums_table, got_text[1]))
    sums_table = cube_sum(sums_table, "y")
    d_text = add_returned(partial_text, got_text, own_d_text)
    back_text = backward(d_text, normed_text, inverse_text, sums_text / pairs)
    sums_table, back_text = lax.optimization_barrier((sums_table, back_text))
    got_table = returned(partial_table, rows)
    parts_text = [dot(back_text, weight, ((1,), (1,))) for weight in text_weights[1:]]
    sums_table = sums_table + flip(sums_table, "z", 1)
    sums_table, parts_text, got_table[0] = lax.optimization_barrier((sums_table, parts_text, got_table[0]))
    sent_text = [add_cores(part).astype(BF16) for part in parts_text]
    sums_table = sums_table + flip(sums_table, "z", 2)
    own_text = dot(back_text, text_weights[0], ((1,), (1,)))
    sent_text, own_text, sums_table = lax.optimization_barrier((sent_text, own_text, sums_table))
    grads_text = [swap_parts([jnp.split(part, 2)[i] for part in sent_text]) for i in range(2)]
    sums_table, got_table[1], grads_text[0] = lax.optimization_barrier((sums_table, got_table[1], grads_text[0]))

    means_table = sums_table / pairs
    d_table = add_returned(partial_table, got_table, own_d_table)
    back_table = backward(d_table, normed_table, inverse_table, means_table)
    parts_table = [dot(back_table, weight, ((1,), (1,))) for weight in table_weights[1:]]
    sent_table = [add_cores(part).astype(BF16) for part in parts_table]
    own_table = dot(back_table, table_weights[0], ((1,), (1,)))
    own_table, sent_table, grads_text[1] = lax.optimization_barrier((own_table, sent_table, grads_text[1]))
    grads_table = swap_parts(sent_table)

    squares = means_table[1] - diag_weight * diag
    terms = (1.0 - diag) * (1.0 - diag) - OFF_WEIGHT * diag * diag + squares
    loss_part, own_table = lax.optimization_barrier((jnp.sum(terms).reshape(1), own_table))
    loss_total = cube_sum(loss_part, "core", "feat")
    grads_text = [jnp.concatenate(parts, 0) for parts in zip(*grads_text)]
    grad_text = add_cores(own_text) + sum(part.astype(F32) for part in grads_text)
    grad_table = add_cores(own_table) + sum(part.astype(F32) for part in grads_table)
    return grad_table, grad_text, loss_total / features


def solution(mesh):
    devices = mesh.devices
    split = Mesh(
        devices.reshape(Z_CHIPS, devices.shape[0] // (2 * Z_CHIPS), 2, devices.shape[1]),
        ("z", "y", "core", "feat"),
    )
    rows = ("z", "y", "core")
    placed = (P(rows, "feat"), P(rows, "feat"), P(None, "feat"), P(None, "feat"))
    return jax.shard_map(
        body,
        mesh=split,
        in_specs=placed,
        out_specs=(P(rows, "feat"), P(rows, "feat"), P()),
        check_vma=False,
    )
```

```python
import jax
import jax.numpy as jnp
from jax import lax
from jax.sharding import Mesh
from jax.sharding import PartitionSpec as P

OFF_WEIGHT = 0.1
EPS = 1e-05
Z_CHIPS = 4
F32 = jnp.float32
BF16 = jnp.bfloat16


def dot(a, b, dims):
    return lax.dot_general(a, b, (dims, ((), ())), preferred_element_type=F32)


def shift(x, axis, step):
    size = lax.axis_size(axis)
    return lax.ppermute(x, axis, [(i, (i + step) % size) for i in range(size)])


def flip(x, axis, bit=1):
    size = lax.axis_size(axis)
    return lax.ppermute(x, axis, [(i, i ^ bit) for i in range(size)])


def cube_sum(x, *axes):
    for axis in axes:
        bit = 1
        while bit < lax.axis_size(axis):
            x = x + flip(x, axis, bit)
            bit *= 2
    return x


def own_block(x, index, count, axis):
    size = x.shape[axis] // count
    return lax.dynamic_slice_in_dim(x, index * size, size, axis)


def both_cores(x, axis=0):
    got = flip(x, "core")
    first = lax.axis_index("core") == 0
    return jnp.where(first, jnp.concatenate([x, got], axis), jnp.concatenate([got, x], axis))


def add_cores(x, axis=0):
    core = lax.axis_index("core")
    return own_block(x, core, 2, axis) + flip(own_block(x, 1 - core, 2, axis), "core")


def weight_blocks(proj):
    num_feat = lax.axis_size("feat")
    feat = lax.axis_index("feat")
    cols = own_block(proj, lax.axis_index("core"), 2, 1)
    return [own_block(cols, (feat - step) % num_feat, num_feat, 0) for step in range(num_feat)]


def swap_feat(x):
    return [shift(x, "feat", step) for step in range(1, lax.axis_size("feat"))]


def project(z, others, weights):
    for other, weight in zip(others, weights[1:]):
        z = z + dot(both_cores(other), weight, ((1,), (0,)))
    return z


def gather_step(x, axis, bit):
    return jnp.concatenate([x, flip(x, axis, bit)], 0)


def merge(x):
    while x.shape[0] > 1:
        x = x[: x.shape[0] // 2] + x[x.shape[0] // 2 :]
    return x[0]


def split_two(x):
    high = x.astype(BF16)
    return high, (x - high.astype(F32)).astype(BF16)


def center_rows(z):
    mean = jnp.mean(z, axis=0)
    centered = z - mean
    return centered, mean, jnp.sum(centered * centered, axis=0)


def normalization(rows, means, squares, pairs):
    center = merge(means) / means.shape[0]
    offsets = means - center
    spread = (merge(squares) + rows * merge(offsets * offsets)) / pairs
    return lax.rsqrt(spread + EPS), offsets


def normalize_plane(centered, blocks, inverse, offsets):
    rows = [centered] + [block.astype(F32) for block in blocks]
    return jnp.concatenate([(part + offset) * inverse for part, offset in zip(rows, offsets)], 0)


def members(count, width):
    chips = jnp.repeat(jnp.arange(count, dtype=jnp.int32), width)
    return (jnp.arange(count, dtype=jnp.int32)[:, None] == chips[None, :]).astype(BF16)


def gram_part(plane, inverse, column, offsets):
    scaled = (plane * inverse).astype(BF16)
    count = offsets.shape[0]
    shifts = dot(scaled, jnp.concatenate(split_two(offsets), 0), ((1,), (1,)))
    shifts = jnp.concatenate(split_two(shifts[:, :count] + shifts[:, count:]), 1)
    chips = members(count, column.shape[0] // count)
    return dot(scaled, column, ((1,), (1,))) + dot(shifts, jnp.concatenate([chips, chips], 0), ((1,), (0,)))


def gram_times(gram, column, inverse, offsets):
    count = offsets.shape[0]
    sums = dot(gram, members(count, column.shape[0] // count), ((1,), (1,)))
    moved = lax.dot_general(
        sums, offsets, (((1,), (0,)), ((), ())), precision=lax.Precision.HIGHEST, preferred_element_type=F32
    )
    return inverse * (dot(gram, column, ((1,), (0,))) + moved)


def at_end(end, inner):
    z = lax.axis_index("z")
    return jnp.where((z == 0) | (z == Z_CHIPS - 1), end, inner)


def send_own(own):
    return flip(own, "z"), lax.ppermute(own, "z", [(1, 2), (2, 1)])


def send_near(near, mid):
    return lax.ppermute(near, "z", [(1, 2), (2, 1)]), lax.ppermute(mid, "z", [(1, 0), (2, 3)])


def send_far(far_in):
    return lax.ppermute(far_in, "z", [(1, 0), (2, 3)])


def over_y(x):
    return [flip(x, "y", step) for step in range(1, lax.axis_size("y"))]


def add_feat(mine, others):
    for other in others:
        mine = mine + other.astype(F32)
    return both_cores(mine.astype(BF16))


def column_sums(partial, plane, own, normed):
    return jnp.stack(
        [
            jnp.sum(partial, axis=0) + jnp.sum(own, axis=0),
            jnp.sum(partial * plane, axis=0) + jnp.sum(own * normed, axis=0),
        ]
    )


def returned(partial, rows):
    cut = rows // 2
    steps = range(1, lax.axis_size("y"))
    return [
        [flip(partial[step * rows + at : step * rows + at + cut].astype(BF16), "y", step) for step in steps] for at in (0, cut)
    ]


def add_returned(partial, got, own):
    d = partial[: own.shape[0]] + own
    for parts in zip(*got):
        d = d + jnp.concatenate(parts, 0).astype(F32)
    return d


def backward(d, normed, inverse, means):
    return (inverse * (d - means[0] - normed * means[1])).astype(BF16)


def swap_parts(sent):
    num_feat = lax.axis_size("feat")
    return [shift(part, "feat", num_feat - step) for step, part in enumerate(sent, 1)]


def body(table, text, table_proj, text_proj):
    pairs = table.shape[0] * 2 * lax.axis_size("z") * lax.axis_size("y")
    features = table_proj.shape[1] * lax.axis_size("feat")
    table_weights = weight_blocks(table_proj)
    text_weights = weight_blocks(text_proj)

    others_table = swap_feat(table)
    tail_weights = lax.optimization_barrier((table_weights, text_weights))
    z_table = dot(both_cores(table), table_weights[0], ((1,), (0,)))
    z_text = dot(both_cores(text), text_weights[0], ((1,), (0,)))
    others_text = swap_feat(text)
    z_table, z_text, others_table = lax.optimization_barrier((z_table, z_text, others_table))
    z_table = project(z_table, others_table, table_weights)
    z_table, others_text = lax.optimization_barrier((z_table, others_text))
    front_weights = text_weights
    table_weights, text_weights = tail_weights
    rows = z_table.shape[0]
    y_size = lax.axis_size("y")
    centered_table, mean_table, square_table = center_rows(z_table)
    sent_rows_table = centered_table.astype(BF16)
    near_table, mid_table = send_own(sent_rows_table)

    z_text = project(z_text, others_text, front_weights)
    z_text, near_table, mid_table = lax.optimization_barrier((z_text, near_table, mid_table))
    centered_text, mean_text, square_text = center_rows(z_text)
    sent_rows_text = centered_text.astype(BF16)
    cross = jnp.sum(centered_table * centered_text, axis=0)
    stats = jnp.stack([mean_table, square_table, mean_text, square_text, cross])[None]
    while stats.shape[0] < y_size:
        stats = gather_step(stats, "y", stats.shape[0])

    stats = gather_step(stats, "z", 1)
    plane = over_y(jnp.stack([sent_rows_table, sent_rows_text]))
    far_in_table, far_end_table, near_text, mid_text, stats = lax.optimization_barrier(
        (*send_near(near_table, mid_table), *send_own(sent_rows_text), stats)
    )
    stats = gather_step(stats, "z", 2)
    last_end_table, far_in_text, far_end_text, stats = lax.optimization_barrier(
        (send_far(far_in_table), *send_near(near_text, mid_text), stats)
    )
    last_end_text = send_far(far_in_text)

    inverse_table, offsets_table = normalization(rows, stats[:, 0], stats[:, 1], pairs)
    inverse_text, offsets_text = normalization(rows, stats[:, 2], stats[:, 3], pairs)
    diag = inverse_table * inverse_text * ((merge(stats[:, 4]) + rows * merge(offsets_table * offsets_text)) / pairs)
    diag_weight = (diag - 1.0).astype(BF16).astype(F32) - OFF_WEIGHT * diag
    plane_table = normalize_plane(centered_table, [block[0] for block in plane], inverse_table, offsets_table)
    plane_text = normalize_plane(centered_text, [block[1] for block in plane], inverse_text, offsets_text)
    normed_table, normed_text = plane_table[:rows], plane_text[:rows]
    own_d_table = normed_text.astype(BF16).astype(F32) * diag_weight
    own_d_text = normed_table.astype(BF16).astype(F32) * diag_weight
    scale = OFF_WEIGHT / pairs
    moved_table, moved_text = offsets_table[::y_size], offsets_text[::y_size]

    last_table, far_table = at_end(last_end_table, mid_table), at_end(far_end_table, far_in_table)
    column_table = jnp.concatenate([sent_rows_table, near_table, far_table, last_table], 0)
    gram_table = add_cores(gram_part(plane_table, inverse_table, column_table, moved_table))
    others_gram_table = swap_feat(gram_table.astype(BF16))

    last_text, far_text = at_end(last_end_text, mid_text), at_end(far_end_text, far_in_text)
    column_text = jnp.concatenate([sent_rows_text, near_text, far_text, last_text], 0)
    gram_text = add_cores(gram_part(plane_text, inverse_text, column_text, moved_text))
    gram_table = add_feat(gram_table, others_gram_table)
    others_gram_text = swap_feat(gram_text.astype(BF16))
    partial_text = scale * gram_times(gram_table, column_text, inverse_text, moved_text)
    got_text = returned(partial_text, rows)
    sums_text = column_sums(partial_text, plane_text, own_d_text, normed_text)
    sums_text, got_text[0] = lax.optimization_barrier((sums_text, got_text[0]))

    gram_text = add_feat(gram_text, others_gram_text)
    partial_table = scale * gram_times(gram_text, column_table, inverse_table, moved_table)
    sums_table = column_sums(partial_table, plane_table, own_d_table, normed_table)
    got_table = returned(partial_table, rows)
    sums = cube_sum(jnp.concatenate([sums_text, sums_table], 0), "y")
    sums, got_text[1] = lax.optimization_barrier((sums, got_text[1]))
    sums = sums + flip(sums, "z", 1)
    sums, got_table[0] = lax.optimization_barrier((sums, got_table[0]))
    sums = sums + flip(sums, "z", 2)
    sums, got_table[1] = lax.optimization_barrier((sums, got_table[1]))

    means_text, means_table = sums[:2] / pairs, sums[2:] / pairs
    d_text = add_returned(partial_text, got_text, own_d_text)
    d_table = add_returned(partial_table, got_table, own_d_table)
    back_text = backward(d_text, normed_text, inverse_text, means_text)
    parts_text = [dot(back_text, weight, ((1,), (1,))) for weight in text_weights[1:]]
    d_table, parts_text = lax.optimization_barrier((d_table, parts_text))
    sent_text = [add_cores(part).astype(BF16) for part in parts_text]
    back_table = backward(d_table, normed_table, inverse_table, means_table)
    parts_table = [dot(back_table, weight, ((1,), (1,))) for weight in table_weights[1:]]
    sent_text, parts_table, back_text = lax.optimization_barrier((sent_text, parts_table, back_text))
    grads_text = swap_parts(sent_text)
    sent_table = [add_cores(part).astype(BF16) for part in parts_table]
    back_text, back_table, sent_table = lax.optimization_barrier((back_text, back_table, sent_table))
    own_text = dot(back_text, text_weights[0], ((1,), (1,)))
    sent_table, own_text, *grads_text = lax.optimization_barrier((sent_table, own_text, *grads_text))
    grads_table = swap_parts(sent_table)
    own_table = dot(back_table, table_weights[0], ((1,), (1,)))

    squares = means_table[1] - diag_weight * diag
    terms = (1.0 - diag) * (1.0 - diag) - OFF_WEIGHT * diag * diag + squares
    loss_part, own_table = lax.optimization_barrier((jnp.sum(terms).reshape(1), own_table))
    loss_total = cube_sum(loss_part, "core", "feat")
    grad_text = add_cores(own_text) + sum(part.astype(F32) for part in grads_text)
    grad_table = add_cores(own_table) + sum(part.astype(F32) for part in grads_table)
    return grad_table, grad_text, loss_total / features


def solution(mesh):
    devices = mesh.devices
    split = Mesh(
        devices.reshape(Z_CHIPS, devices.shape[0] // (2 * Z_CHIPS), 2, devices.shape[1]),
        ("z", "y", "core", "feat"),
    )
    rows = ("z", "y", "core")
    placed = (P(rows, "feat"), P(rows, "feat"), P(None, "feat"), P(None, "feat"))
    return jax.shard_map(
        body,
        mesh=split,
        in_specs=placed,
        out_specs=(P(rows, "feat"), P(rows, "feat"), P()),
        check_vma=False,
    )
```

```python
import jax
import jax.numpy as jnp
from jax import lax
from jax.sharding import Mesh
from jax.sharding import PartitionSpec as P

OFF_WEIGHT = 0.1
EPS = 1e-05
Z_CHIPS = 4
F32 = jnp.float32
BF16 = jnp.bfloat16


def dot(a, b, dims):
    return lax.dot_general(a, b, (dims, ((), ())), preferred_element_type=F32)


def shift(x, axis, step):
    size = lax.axis_size(axis)
    return lax.ppermute(x, axis, [(i, (i + step) % size) for i in range(size)])


def flip(x, axis, bit=1):
    size = lax.axis_size(axis)
    return lax.ppermute(x, axis, [(i, i ^ bit) for i in range(size)])


def cube_sum(x, *axes):
    for axis in axes:
        bit = 1
        while bit < lax.axis_size(axis):
            x = x + flip(x, axis, bit)
            bit *= 2
    return x


def own_block(x, index, count, axis):
    size = x.shape[axis] // count
    return lax.dynamic_slice_in_dim(x, index * size, size, axis)


def both_cores(x, axis=0):
    got = flip(x, "core")
    first = lax.axis_index("core") == 0
    return jnp.where(first, jnp.concatenate([x, got], axis), jnp.concatenate([got, x], axis))


def add_cores(x):
    core = lax.axis_index("core")
    return own_block(x, core, 2, 0) + flip(own_block(x, 1 - core, 2, 0), "core")


def weight_blocks(proj):
    num_feat = lax.axis_size("feat")
    feat = lax.axis_index("feat")
    cols = own_block(proj, lax.axis_index("core"), 2, 1)
    return [own_block(cols, (feat - step) % num_feat, num_feat, 0) for step in range(num_feat)]


def swap_feat(x):
    return [shift(x, "feat", step) for step in range(1, lax.axis_size("feat"))]


def moments(z_table, z_text):
    count = z_table.shape[0]
    mean_table, mean_text = jnp.mean(z_table, axis=0), jnp.mean(z_text, axis=0)
    centered_table, centered_text = z_table - mean_table, z_text - mean_text
    state = jnp.stack(
        [
            mean_table,
            mean_text,
            jnp.sum(centered_table * centered_table, axis=0),
            jnp.sum(centered_text * centered_text, axis=0),
            jnp.sum(centered_table * centered_text, axis=0),
        ]
    )
    for axis in ("z", "y"):
        bit = 1
        while bit < lax.axis_size(axis):
            other = flip(state, axis, bit)
            gap = state[:2] - other[:2]
            moved = (count / 2) * jnp.concatenate([gap * gap, gap[:1] * gap[1:]], 0)
            state = jnp.concatenate([(state[:2] + other[:2]) / 2, state[2:] + other[2:] + moved], 0)
            count *= 2
            bit *= 2
    return state[:2], state[2:] / count


def gather_rows(own):
    z = lax.axis_index("z")
    end = (z == 0) | (z == Z_CHIPS - 1)
    half = own.shape[0] // 2
    near = flip(own, "z")
    mid = lax.ppermute(own, "z", [(1, 2), (2, 1)])
    far_in = lax.ppermute(near, "z", [(1, 2), (2, 1)])
    far_end = lax.ppermute(mid, "z", [(1, 0), (2, 3)])
    far = jnp.where(end, far_end, far_in)
    last_end = lax.ppermute(far_in, "z", [(1, 0), (2, 3)])
    last = jnp.where(end, last_end, mid)
    early, late = [own, near, far], [last]
    for step in range(1, lax.axis_size("y")):
        y_own = shift(own, "y", step)
        y_near = [shift(near[:half], "y", step), flip(y_own[half:], "z")]
        early += [y_own, *y_near, shift(far, "y", step)]
        late += [shift(last, "y", step)]
    return jnp.concatenate(early, 0), jnp.concatenate(late, 0)


def gram_part(half, rows):
    return add_cores(dot(half, rows, ((1,), (1,))))


def add_feat(mine, others, axis):
    for other in others:
        mine = mine + other.astype(F32)
    return both_cores(mine.astype(BF16), axis)


def column_sums(d, normed):
    return jnp.stack([jnp.sum(d, axis=0), jnp.sum(d * normed, axis=0)])


def backward(d, normed, inverse, means):
    return (inverse * (d - means[0] - normed * means[1])).astype(BF16)


def swap_parts(sent):
    num_feat = lax.axis_size("feat")
    return [shift(part, "feat", num_feat - step) for step, part in enumerate(sent, 1)]


def body(table, text, table_proj, text_proj):
    pairs = table.shape[0] * 2 * lax.axis_size("z") * lax.axis_size("y")
    features = table_proj.shape[1] * lax.axis_size("feat")
    mine = jnp.stack([table, text])
    others = swap_feat(mine)
    weights = lax.optimization_barrier((weight_blocks(table_proj), weight_blocks(text_proj)))
    table_weights, text_weights = weights
    mine = both_cores(mine, 1)
    z_table = dot(mine[0], table_weights[0], ((1,), (0,)))
    z_text = dot(mine[1], text_weights[0], ((1,), (0,)))
    z_table, z_text, others = lax.optimization_barrier((z_table, z_text, others))
    for other, table_weight, text_weight in zip(others, table_weights[1:], text_weights[1:]):
        other = both_cores(other, 1)
        z_table = z_table + dot(other[0], table_weight, ((1,), (0,)))
        z_text = z_text + dot(other[1], text_weight, ((1,), (0,)))

    centers, spreads = moments(z_table, z_text)
    inverse_table, inverse_text = lax.rsqrt(spreads[0] + EPS), lax.rsqrt(spreads[1] + EPS)
    diag = inverse_table * inverse_text * spreads[2]
    diag_weight = (diag - 1.0).astype(BF16).astype(F32) - OFF_WEIGHT * diag
    normed_table = (z_table - centers[0]) * inverse_table
    normed_text = (z_text - centers[1]) * inverse_text
    half_table, half_text = normed_table.astype(BF16), normed_text.astype(BF16)
    all_table = gather_rows(half_table)
    all_text = gather_rows(half_text)

    gram_table = gram_part(half_table, all_table[0])
    others_table = swap_feat(gram_table.astype(BF16))
    early_text, late_text, late_table, others_table = lax.optimization_barrier(
        (all_text[0], all_text[1], all_table[1], others_table)
    )
    all_table, all_text = (all_table[0], late_table), (early_text, late_text)
    gram_text = gram_part(half_text, early_text)
    others_text = swap_feat(gram_text.astype(BF16))
    late = jnp.stack([gram_part(half_table, all_table[1]), gram_part(half_text, all_text[1])])
    late = add_feat(late, swap_feat(late.astype(BF16)), 1)
    gram_table = add_feat(gram_table, others_table, 0)
    gram_text = add_feat(gram_text, others_text, 0)
    grams = (gram_table, gram_text), late

    off_table, off_text = 0.0, 0.0
    for gram, rows_table, rows_text in zip(grams, all_table, all_text):
        off_table = off_table + dot(gram[1], rows_table, ((1,), (0,)))
        off_text = off_text + dot(gram[0], rows_text, ((1,), (0,)))
    d_table = (OFF_WEIGHT / pairs) * off_table + half_text.astype(F32) * diag_weight
    d_text = (OFF_WEIGHT / pairs) * off_text + half_table.astype(F32) * diag_weight
    sums = jnp.concatenate([column_sums(d_text, normed_text), column_sums(d_table, normed_table)], 0)
    means = cube_sum(sums, "z", "y") / pairs

    back_text = backward(d_text, normed_text, inverse_text, means[:2])
    parts_text = [dot(back_text, weight, ((1,), (1,))) for weight in text_weights[1:]]
    d_table, parts_text = lax.optimization_barrier((d_table, parts_text))
    sent_text = [add_cores(part).astype(BF16) for part in parts_text]
    back_table = backward(d_table, normed_table, inverse_table, means[2:])
    parts_table = [dot(back_table, weight, ((1,), (1,))) for weight in table_weights[1:]]
    sent_text, parts_table, back_text = lax.optimization_barrier((sent_text, parts_table, back_text))
    grads_text = swap_parts(sent_text)
    sent_table = [add_cores(part).astype(BF16) for part in parts_table]
    back_text, back_table, sent_table = lax.optimization_barrier((back_text, back_table, sent_table))
    own_text = dot(back_text, text_weights[0], ((1,), (1,)))
    sent_table, own_text, *grads_text = lax.optimization_barrier((sent_table, own_text, *grads_text))
    grads_table = swap_parts(sent_table)
    own_table = dot(back_table, table_weights[0], ((1,), (1,)))

    squares = means[3] - diag_weight * diag
    terms = (1.0 - diag) * (1.0 - diag) - OFF_WEIGHT * diag * diag + squares
    loss_part, own_table = lax.optimization_barrier((jnp.sum(terms).reshape(1), own_table))
    loss_total = cube_sum(loss_part, "core", "feat")
    grad_text = add_cores(own_text) + sum(part.astype(F32) for part in grads_text)
    grad_table = add_cores(own_table) + sum(part.astype(F32) for part in grads_table)
    return grad_table, grad_text, loss_total / features


def solution(mesh):
    devices = mesh.devices
    split = Mesh(
        devices.reshape(Z_CHIPS, devices.shape[0] // (2 * Z_CHIPS), 2, devices.shape[1]),
        ("z", "y", "core", "feat"),
    )
    rows = ("z", "y", "core")
    placed = (P(rows, "feat"), P(rows, "feat"), P(None, "feat"), P(None, "feat"))
    return jax.shard_map(
        body,
        mesh=split,
        in_specs=placed,
        out_specs=(P(rows, "feat"), P(rows, "feat"), P()),
        check_vma=False,
    )
```

```python
import jax
import jax.numpy as jnp
from jax import lax
from jax.sharding import Mesh
from jax.sharding import PartitionSpec as P

OFF_WEIGHT = 0.1
EPS = 1e-05
Z_CHIPS = 4
F32 = jnp.float32
BF16 = jnp.bfloat16


def dot(a, b, dims):
    return lax.dot_general(a, b, (dims, ((), ())), preferred_element_type=F32)


def shift(x, axis, step):
    size = lax.axis_size(axis)
    return lax.ppermute(x, axis, [(i, (i + step) % size) for i in range(size)])


def flip(x, axis, bit=1):
    size = lax.axis_size(axis)
    return lax.ppermute(x, axis, [(i, i ^ bit) for i in range(size)])


def cube_sum(x, *axes):
    for axis in axes:
        bit = 1
        while bit < lax.axis_size(axis):
            x = x + flip(x, axis, bit)
            bit *= 2
    return x


def own_block(x, index, count, axis):
    size = x.shape[axis] // count
    return lax.dynamic_slice_in_dim(x, index * size, size, axis)


def both_cores(x, axis=0):
    got = flip(x, "core")
    first = lax.axis_index("core") == 0
    return jnp.where(first, jnp.concatenate([x, got], axis), jnp.concatenate([got, x], axis))


def add_cores(x):
    core = lax.axis_index("core")
    return own_block(x, core, 2, 0) + flip(own_block(x, 1 - core, 2, 0), "core")


def weight_blocks(proj):
    num_feat = lax.axis_size("feat")
    feat = lax.axis_index("feat")
    cols = own_block(proj, lax.axis_index("core"), 2, 1)
    return [own_block(cols, (feat - step) % num_feat, num_feat, 0) for step in range(num_feat)]


def swap_feat(x):
    return [shift(x, "feat", step) for step in range(1, lax.axis_size("feat"))]


def moments(z_table, z_text):
    count = z_table.shape[0]
    mean_table, mean_text = jnp.mean(z_table, axis=0), jnp.mean(z_text, axis=0)
    centered_table, centered_text = z_table - mean_table, z_text - mean_text
    state = jnp.stack(
        [
            mean_table,
            mean_text,
            jnp.sum(centered_table * centered_table, axis=0),
            jnp.sum(centered_text * centered_text, axis=0),
            jnp.sum(centered_table * centered_text, axis=0),
        ]
    )
    for axis in ("z", "y"):
        bit = 1
        while bit < lax.axis_size(axis):
            other = flip(state, axis, bit)
            gap = state[:2] - other[:2]
            moved = (count / 2) * jnp.concatenate([gap * gap, gap[:1] * gap[1:]], 0)
            state = jnp.concatenate([(state[:2] + other[:2]) / 2, state[2:] + other[2:] + moved], 0)
            count *= 2
            bit *= 2
    return state[:2], state[2:] / count


def at_end(end, inner):
    z = lax.axis_index("z")
    return jnp.where((z == 0) | (z == Z_CHIPS - 1), end, inner)


def over_y(x):
    return [flip(x, "y", step) for step in range(1, lax.axis_size("y"))]


def gram_part(half, rows):
    return add_cores(dot(half, rows, ((1,), (1,))))


def add_feat(mine, others, axis):
    for other in others:
        mine = mine + other.astype(F32)
    return both_cores(mine.astype(BF16), axis)


def column_sums(d, normed):
    return jnp.stack([jnp.sum(d, axis=0), jnp.sum(d * normed, axis=0)])


def backward(d, normed, inverse, means):
    return (inverse * (d - means[0] - normed * means[1])).astype(BF16)


def swap_parts(sent):
    num_feat = lax.axis_size("feat")
    return [shift(part, "feat", num_feat - step) for step, part in enumerate(sent, 1)]


def body(table, text, table_proj, text_proj):
    pairs = table.shape[0] * 2 * lax.axis_size("z") * lax.axis_size("y")
    features = table_proj.shape[1] * lax.axis_size("feat")
    mine = jnp.stack([table, text])
    others = swap_feat(mine)
    weights = lax.optimization_barrier((weight_blocks(table_proj), weight_blocks(text_proj)))
    table_weights, text_weights = weights
    mine = both_cores(mine, 1)
    z_table = dot(mine[0], table_weights[0], ((1,), (0,)))
    z_text = dot(mine[1], text_weights[0], ((1,), (0,)))
    z_table, z_text, others = lax.optimization_barrier((z_table, z_text, others))
    for other, table_weight, text_weight in zip(others, table_weights[1:], text_weights[1:]):
        other = both_cores(other, 1)
        z_table = z_table + dot(other[0], table_weight, ((1,), (0,)))
        z_text = z_text + dot(other[1], text_weight, ((1,), (0,)))

    centers, spreads = moments(z_table, z_text)
    inverse_table, inverse_text = lax.rsqrt(spreads[0] + EPS), lax.rsqrt(spreads[1] + EPS)
    diag = inverse_table * inverse_text * spreads[2]
    diag_weight = (diag - 1.0).astype(BF16).astype(F32) - OFF_WEIGHT * diag
    normed_table = (z_table - centers[0]) * inverse_table
    normed_text = (z_text - centers[1]) * inverse_text
    half_table, half_text = normed_table.astype(BF16), normed_text.astype(BF16)

    half = jnp.stack([half_table, half_text])
    near, mid, y_own = lax.optimization_barrier((flip(half, "z"), lax.ppermute(half, "z", [(1, 2), (2, 1)]), over_y(half)))
    far_in, far_end, y_near = lax.optimization_barrier(
        (lax.ppermute(near, "z", [(1, 2), (2, 1)]), lax.ppermute(mid, "z", [(1, 0), (2, 3)]), over_y(near))
    )
    far = at_end(far_end, far_in)
    last_end, y_far = lax.optimization_barrier((lax.ppermute(far_in, "z", [(1, 0), (2, 3)]), over_y(far)))
    last = at_end(last_end, mid)
    cut = half.shape[1] // 2
    y_last = over_y(last[:, :cut])
    y_flip = [flip(block[:, cut:], "z") for block in y_far]

    early = [half, near, far, *y_own, *y_near, *y_far]
    early_table, early_text = [jnp.concatenate([block[i] for block in early], 0) for i in range(2)]
    gram_table = gram_part(half_table, early_table)
    others_table = swap_feat(gram_table.astype(BF16))
    gram_text = gram_part(half_text, early_text)
    y_last, y_flip, others_table, gram_text = lax.optimization_barrier((y_last, y_flip, others_table, gram_text))
    late = [last] + [block for pair in zip(y_last, y_flip) for block in pair]
    late_table, late_text = [jnp.concatenate([block[i] for block in late], 0) for i in range(2)]
    all_table, all_text = (early_table, late_table), (early_text, late_text)
    parts = [gram_part(half_table, late_table), gram_text, gram_part(half_text, late_text)]
    rest = jnp.concatenate(parts, 1)
    rest = add_feat(rest, swap_feat(rest.astype(BF16)), 0)
    gram_table = add_feat(gram_table, others_table, 0)
    cuts = [late_table.shape[0], late_table.shape[0] + early_text.shape[0]]
    late_gram, *gram_text = jnp.split(rest, cuts, 1)
    grams = (gram_table, gram_text[0]), (late_gram, gram_text[1])

    off_table, off_text = 0.0, 0.0
    for gram, rows_table, rows_text in zip(grams, all_table, all_text):
        off_table = off_table + dot(gram[1], rows_table, ((1,), (0,)))
        off_text = off_text + dot(gram[0], rows_text, ((1,), (0,)))
    d_table = (OFF_WEIGHT / pairs) * off_table + half_text.astype(F32) * diag_weight
    d_text = (OFF_WEIGHT / pairs) * off_text + half_table.astype(F32) * diag_weight
    sums = jnp.concatenate([column_sums(d_text, normed_text), column_sums(d_table, normed_table)], 0)
    means = cube_sum(sums, "z", "y") / pairs

    back_text = backward(d_text, normed_text, inverse_text, means[:2])
    parts_text = [dot(back_text, weight, ((1,), (1,))) for weight in text_weights[1:]]
    d_table, parts_text = lax.optimization_barrier((d_table, parts_text))
    sent_text = [add_cores(part).astype(BF16) for part in parts_text]
    back_table = backward(d_table, normed_table, inverse_table, means[2:])
    parts_table = [dot(back_table, weight, ((1,), (1,))) for weight in table_weights[1:]]
    sent_text, parts_table, back_text = lax.optimization_barrier((sent_text, parts_table, back_text))
    grads_text = swap_parts(sent_text)
    sent_table = [add_cores(part).astype(BF16) for part in parts_table]
    back_text, back_table, sent_table = lax.optimization_barrier((back_text, back_table, sent_table))
    own_text = dot(back_text, text_weights[0], ((1,), (1,)))
    sent_table, own_text, *grads_text = lax.optimization_barrier((sent_table, own_text, *grads_text))
    grads_table = swap_parts(sent_table)
    own_table = dot(back_table, table_weights[0], ((1,), (1,)))

    squares = means[3] - diag_weight * diag
    terms = (1.0 - diag) * (1.0 - diag) - OFF_WEIGHT * diag * diag + squares
    loss_part, own_table = lax.optimization_barrier((jnp.sum(terms).reshape(1), own_table))
    loss_total = cube_sum(loss_part, "core", "feat")
    grad_text = add_cores(own_text) + sum(part.astype(F32) for part in grads_text)
    grad_text, *grads_table = lax.optimization_barrier((grad_text, *grads_table))
    grad_table = add_cores(own_table) + sum(part.astype(F32) for part in grads_table)
    return grad_table, grad_text, loss_total / features


def solution(mesh):
    devices = mesh.devices
    split = Mesh(
        devices.reshape(Z_CHIPS, devices.shape[0] // (2 * Z_CHIPS), 2, devices.shape[1]),
        ("z", "y", "core", "feat"),
    )
    rows = ("z", "y", "core")
    placed = (P(rows, "feat"), P(rows, "feat"), P(None, "feat"), P(None, "feat"))
    return jax.shard_map(
        body,
        mesh=split,
        in_specs=placed,
        out_specs=(P(rows, "feat"), P(rows, "feat"), P()),
        check_vma=False,
    )
```

```python
import jax
import jax.numpy as jnp
from jax import lax
from jax.experimental import pallas as pl
from jax.experimental.pallas import tpu as pltpu
from jax.sharding import Mesh
from jax.sharding import PartitionSpec as P

OFF_WEIGHT = 0.1
EPS = 1e-05
Z_CHIPS = 4
F32 = jnp.float32
BF16 = jnp.bfloat16


def dot(a, b, dims):
    return lax.dot_general(a, b, (dims, ((), ())), preferred_element_type=F32)


def shift(x, axis, step):
    size = lax.axis_size(axis)
    return lax.ppermute(x, axis, [(i, (i + step) % size) for i in range(size)])


def flip(x, axis, bit=1):
    size = lax.axis_size(axis)
    return lax.ppermute(x, axis, [(i, i ^ bit) for i in range(size)])


def cube_sum(x, *axes):
    for axis in axes:
        bit = 1
        while bit < lax.axis_size(axis):
            x = x + flip(x, axis, bit)
            bit *= 2
    return x


def own_block(x, index, count, axis):
    size = x.shape[axis] // count
    return lax.dynamic_slice_in_dim(x, index * size, size, axis)


def both_cores(x, axis=0):
    got = flip(x, "core")
    first = lax.axis_index("core") == 0
    return jnp.where(first, jnp.concatenate([x, got], axis), jnp.concatenate([got, x], axis))


def add_cores(x):
    core = lax.axis_index("core")
    return own_block(x, core, 2, 0) + flip(own_block(x, 1 - core, 2, 0), "core")


def cut_kernel(starts, *refs):
    sources, blocks, sems = refs[:2], refs[2:-1], refs[-1]
    count = len(blocks) // 2
    rows, cols = blocks[0].shape
    copies = []
    for i, block in enumerate(blocks):
        row = pl.multiple_of(starts[1 + i % count], 16)
        col = pl.multiple_of(starts[0], 128)
        source = sources[i // count].at[pl.ds(row, rows), pl.ds(col, cols)]
        copies.append(pltpu.make_async_copy(source, block, sems.at[i]))
    for copy in copies:
        copy.start()
    for copy in copies:
        copy.wait()


def weight_blocks(table_proj, text_proj):
    num_feat = lax.axis_size("feat")
    feat = lax.axis_index("feat")
    rows, cols = table_proj.shape[0] // num_feat, table_proj.shape[1] // 2
    firsts = [(feat - step) % num_feat * rows for step in range(num_feat)]
    starts = jnp.stack([lax.axis_index("core") * cols, *firsts]).astype(jnp.int32)
    count = 2 * num_feat
    blocks = pl.pallas_call(
        cut_kernel,
        out_shape=[jax.ShapeDtypeStruct((rows, cols), BF16)] * count,
        in_specs=[pl.BlockSpec(memory_space=pltpu.SMEM), pl.BlockSpec(memory_space=pl.ANY), pl.BlockSpec(memory_space=pl.ANY)],
        out_specs=[pl.BlockSpec(memory_space=pltpu.VMEM)] * count,
        scratch_shapes=[pltpu.SemaphoreType.DMA((count,))],
        compiler_params=pltpu.CompilerParams(vmem_limit_bytes=40 * 1024 * 1024),
    )(starts, table_proj, text_proj)
    return blocks[:num_feat], blocks[num_feat:]


def swap_feat(x):
    return [shift(x, "feat", step) for step in range(1, lax.axis_size("feat"))]


def moments(z_table, z_text):
    count = z_table.shape[0]
    mean_table, mean_text = jnp.mean(z_table, axis=0), jnp.mean(z_text, axis=0)
    centered_table, centered_text = z_table - mean_table, z_text - mean_text
    state = jnp.stack(
        [
            mean_table,
            mean_text,
            jnp.sum(centered_table * centered_table, axis=0),
            jnp.sum(centered_text * centered_text, axis=0),
            jnp.sum(centered_table * centered_text, axis=0),
        ]
    )
    for axis in ("z", "y"):
        bit = 1
        while bit < lax.axis_size(axis):
            other = flip(state, axis, bit)
            gap = state[:2] - other[:2]
            moved = (count / 2) * jnp.concatenate([gap * gap, gap[:1] * gap[1:]], 0)
            state = jnp.concatenate([(state[:2] + other[:2]) / 2, state[2:] + other[2:] + moved], 0)
            count *= 2
            bit *= 2
    return state[:2], state[2:] / count


def at_end(end, inner):
    z = lax.axis_index("z")
    return jnp.where((z == 0) | (z == Z_CHIPS - 1), end, inner)


def over_y(x):
    return [flip(x, "y", step) for step in range(1, lax.axis_size("y"))]


def gram_part(half, rows):
    return add_cores(dot(half, rows, ((1,), (1,))))


def add_feat(mine, others, axis):
    for other in others:
        mine = mine + other.astype(F32)
    return both_cores(mine.astype(BF16), axis)


def column_sums(d, normed):
    return jnp.stack([jnp.sum(d, axis=0), jnp.sum(d * normed, axis=0)])


def backward(d, normed, inverse, means):
    return (inverse * (d - means[0] - normed * means[1])).astype(BF16)


def swap_parts(sent):
    num_feat = lax.axis_size("feat")
    return [shift(part, "feat", num_feat - step) for step, part in enumerate(sent, 1)]


def body(table, text, table_proj, text_proj):
    pairs = table.shape[0] * 2 * lax.axis_size("z") * lax.axis_size("y")
    features = table_proj.shape[1] * lax.axis_size("feat")
    mine = jnp.stack([table, text])
    others = swap_feat(mine)
    table_weights, text_weights = weight_blocks(table_proj, text_proj)
    mine = both_cores(mine, 1)
    z_table = dot(mine[0], table_weights[0], ((1,), (0,)))
    z_text = dot(mine[1], text_weights[0], ((1,), (0,)))
    z_table, z_text, others = lax.optimization_barrier((z_table, z_text, others))
    for other, table_weight, text_weight in zip(others, table_weights[1:], text_weights[1:]):
        other = both_cores(other, 1)
        z_table = z_table + dot(other[0], table_weight, ((1,), (0,)))
        z_text = z_text + dot(other[1], text_weight, ((1,), (0,)))

    centers, spreads = moments(z_table, z_text)
    inverse_table, inverse_text = lax.rsqrt(spreads[0] + EPS), lax.rsqrt(spreads[1] + EPS)
    diag = inverse_table * inverse_text * spreads[2]
    diag_weight = (diag - 1.0).astype(BF16).astype(F32) - OFF_WEIGHT * diag
    normed_table = (z_table - centers[0]) * inverse_table
    normed_text = (z_text - centers[1]) * inverse_text
    half_table, half_text = normed_table.astype(BF16), normed_text.astype(BF16)

    half = jnp.stack([half_table, half_text])
    near, mid, y_own = lax.optimization_barrier((flip(half, "z"), lax.ppermute(half, "z", [(1, 2), (2, 1)]), over_y(half)))
    far_in, far_end, y_near = lax.optimization_barrier(
        (lax.ppermute(near, "z", [(1, 2), (2, 1)]), lax.ppermute(mid, "z", [(1, 0), (2, 3)]), over_y(near))
    )
    far = at_end(far_end, far_in)
    last_end, y_far = lax.optimization_barrier((lax.ppermute(far_in, "z", [(1, 0), (2, 3)]), over_y(far)))
    last = at_end(last_end, mid)
    cut = half.shape[1] // 2
    y_last = over_y(last[:, :cut])
    y_flip = [flip(block[:, cut:], "z") for block in y_far]

    early = [half, near, far, *y_own, *y_near, *y_far]
    early_table, early_text = [jnp.concatenate([block[i] for block in early], 0) for i in range(2)]
    gram_table = gram_part(half_table, early_table)
    others_table = swap_feat(gram_table.astype(BF16))
    gram_text = gram_part(half_text, early_text)
    y_last, y_flip, others_table, gram_text = lax.optimization_barrier((y_last, y_flip, others_table, gram_text))
    late = [last] + [block for pair in zip(y_last, y_flip) for block in pair]
    late_table, late_text = [jnp.concatenate([block[i] for block in late], 0) for i in range(2)]
    all_table, all_text = (early_table, late_table), (early_text, late_text)
    parts = [gram_part(half_table, late_table), gram_text, gram_part(half_text, late_text)]
    rest = jnp.concatenate(parts, 1)
    rest = add_feat(rest, swap_feat(rest.astype(BF16)), 0)
    gram_table = add_feat(gram_table, others_table, 0)
    cuts = [late_table.shape[0], late_table.shape[0] + early_text.shape[0]]
    late_gram, *gram_text = jnp.split(rest, cuts, 1)
    grams = (gram_table, gram_text[0]), (late_gram, gram_text[1])

    off_table, off_text = 0.0, 0.0
    for gram, rows_table, rows_text in zip(grams, all_table, all_text):
        off_table = off_table + dot(gram[1], rows_table, ((1,), (0,)))
        off_text = off_text + dot(gram[0], rows_text, ((1,), (0,)))
    d_table = (OFF_WEIGHT / pairs) * off_table + half_text.astype(F32) * diag_weight
    d_text = (OFF_WEIGHT / pairs) * off_text + half_table.astype(F32) * diag_weight
    sums = jnp.concatenate([column_sums(d_text, normed_text), column_sums(d_table, normed_table)], 0)
    means = cube_sum(sums, "z", "y") / pairs

    squares = means[3] - diag_weight * diag
    terms = (1.0 - diag) * (1.0 - diag) - OFF_WEIGHT * diag * diag + squares
    loss_total = cube_sum(jnp.sum(terms).reshape(1), "feat")

    back_text = backward(d_text, normed_text, inverse_text, means[:2])
    parts_text = [dot(back_text, weight, ((1,), (1,))) for weight in text_weights[1:]]
    d_table, parts_text = lax.optimization_barrier((d_table, parts_text))
    sent_text = [add_cores(part).astype(BF16) for part in parts_text]
    back_table = backward(d_table, normed_table, inverse_table, means[2:])
    parts_table = [dot(back_table, weight, ((1,), (1,))) for weight in table_weights[1:]]
    sent_text, parts_table, back_text, loss_total = lax.optimization_barrier((sent_text, parts_table, back_text, loss_total))
    grads_text = swap_parts(sent_text)
    sent_table = [add_cores(part).astype(BF16) for part in parts_table]
    back_text, back_table, sent_table = lax.optimization_barrier((back_text, back_table, sent_table))
    grads_table = swap_parts(sent_table)
    own_text = dot(back_text, text_weights[0], ((1,), (1,)))
    loss_total = cube_sum(loss_total, "core")
    back_table, *grads_text = lax.optimization_barrier((back_table, *grads_text))
    own_table = dot(back_table, table_weights[0], ((1,), (1,)))

    grad_text = add_cores(own_text) + sum(part.astype(F32) for part in grads_text)
    grad_text, *grads_table = lax.optimization_barrier((grad_text, *grads_table))
    grad_table = add_cores(own_table) + sum(part.astype(F32) for part in grads_table)
    return grad_table, grad_text, loss_total / features


def solution(mesh):
    devices = mesh.devices
    split = Mesh(
        devices.reshape(Z_CHIPS, devices.shape[0] // (2 * Z_CHIPS), 2, devices.shape[1]),
        ("z", "y", "core", "feat"),
    )
    rows = ("z", "y", "core")
    placed = (P(rows, "feat"), P(rows, "feat"), P(None, "feat"), P(None, "feat"))
    return jax.shard_map(
        body,
        mesh=split,
        in_specs=placed,
        out_specs=(P(rows, "feat"), P(rows, "feat"), P()),
        check_vma=False,
    )
```

```python
import jax
import jax.numpy as jnp
from jax import lax
from jax.experimental import pallas as pl
from jax.experimental.pallas import tpu as pltpu
from jax.sharding import Mesh
from jax.sharding import PartitionSpec as P

OFF_WEIGHT = 0.1
EPS = 1e-05
Z_CHIPS = 4
F32 = jnp.float32
BF16 = jnp.bfloat16


def dot(a, b, dims):
    return lax.dot_general(a, b, (dims, ((), ())), preferred_element_type=F32)


def shift(x, axis, step):
    size = lax.axis_size(axis)
    return lax.ppermute(x, axis, [(i, (i + step) % size) for i in range(size)])


def flip(x, axis, bit=1):
    size = lax.axis_size(axis)
    return lax.ppermute(x, axis, [(i, i ^ bit) for i in range(size)])


def cube_sum(x, *axes):
    for axis in axes:
        bit = 1
        while bit < lax.axis_size(axis):
            x = x + flip(x, axis, bit)
            bit *= 2
    return x


def own_block(x, index, count, axis):
    size = x.shape[axis] // count
    return lax.dynamic_slice_in_dim(x, index * size, size, axis)


def both_cores(x, axis=0):
    got = flip(x, "core")
    first = lax.axis_index("core") == 0
    return jnp.where(first, jnp.concatenate([x, got], axis), jnp.concatenate([got, x], axis))


def add_cores(x):
    core = lax.axis_index("core")
    return own_block(x, core, 2, 0) + flip(own_block(x, 1 - core, 2, 0), "core")


def cut_kernel(starts, *refs):
    sources, blocks, sems = refs[:2], refs[2:-1], refs[-1]
    count = len(blocks) // 2
    rows, cols = blocks[0].shape
    copies = []
    for i, block in enumerate(blocks):
        row = pl.multiple_of(starts[1 + i % count], 16)
        col = pl.multiple_of(starts[0], 128)
        source = sources[i // count].at[pl.ds(row, rows), pl.ds(col, cols)]
        copies.append(pltpu.make_async_copy(source, block, sems.at[i]))
    for copy in copies:
        copy.start()
    for copy in copies:
        copy.wait()


def weight_blocks(table_proj, text_proj):
    num_feat = lax.axis_size("feat")
    feat = lax.axis_index("feat")
    rows, cols = table_proj.shape[0] // num_feat, table_proj.shape[1] // 2
    firsts = [(feat - step) % num_feat * rows for step in range(num_feat)]
    starts = jnp.stack([lax.axis_index("core") * cols, *firsts]).astype(jnp.int32)
    count = 2 * num_feat
    blocks = pl.pallas_call(
        cut_kernel,
        out_shape=[jax.ShapeDtypeStruct((rows, cols), BF16)] * count,
        in_specs=[pl.BlockSpec(memory_space=pltpu.SMEM), pl.BlockSpec(memory_space=pl.ANY), pl.BlockSpec(memory_space=pl.ANY)],
        out_specs=[pl.BlockSpec(memory_space=pltpu.VMEM)] * count,
        scratch_shapes=[pltpu.SemaphoreType.DMA((count,))],
        compiler_params=pltpu.CompilerParams(vmem_limit_bytes=40 * 1024 * 1024),
    )(starts, table_proj, text_proj)
    return blocks[:num_feat], blocks[num_feat:]


def swap_feat(x):
    return [shift(x, "feat", step) for step in range(1, lax.axis_size("feat"))]


def moments(z_table, z_text):
    count = z_table.shape[0]
    mean_table, mean_text = jnp.mean(z_table, axis=0), jnp.mean(z_text, axis=0)
    centered_table, centered_text = z_table - mean_table, z_text - mean_text
    state = jnp.stack(
        [
            mean_table,
            mean_text,
            jnp.sum(centered_table * centered_table, axis=0),
            jnp.sum(centered_text * centered_text, axis=0),
            jnp.sum(centered_table * centered_text, axis=0),
        ]
    )
    for axis in ("z", "y"):
        bit = 1
        while bit < lax.axis_size(axis):
            other = flip(state, axis, bit)
            gap = state[:2] - other[:2]
            moved = (count / 2) * jnp.concatenate([gap * gap, gap[:1] * gap[1:]], 0)
            state = jnp.concatenate([(state[:2] + other[:2]) / 2, state[2:] + other[2:] + moved], 0)
            count *= 2
            bit *= 2
    return state[:2], state[2:] / count


def at_end(end, inner):
    z = lax.axis_index("z")
    return jnp.where((z == 0) | (z == Z_CHIPS - 1), end, inner)


def over_y(x):
    return [flip(x, "y", step) for step in range(1, lax.axis_size("y"))]


def gram_part(half, rows):
    return add_cores(dot(half, rows, ((1,), (1,))))


def add_feat(mine, others, axis):
    for other in others:
        mine = mine + other.astype(F32)
    return both_cores(mine.astype(BF16), axis)


def column_sums(d, normed):
    return jnp.stack([jnp.sum(d, axis=0), jnp.sum(d * normed, axis=0)])


def backward(d, normed, inverse, means):
    return (inverse * (d - means[0] - normed * means[1])).astype(BF16)


def swap_parts(sent):
    num_feat = lax.axis_size("feat")
    return [shift(part, "feat", num_feat - step) for step, part in enumerate(sent, 1)]


def body(table, text, table_proj, text_proj):
    pairs = table.shape[0] * 2 * lax.axis_size("z") * lax.axis_size("y")
    features = table_proj.shape[1] * lax.axis_size("feat")
    mine = jnp.stack([table, text])
    others = swap_feat(mine)
    table_weights, text_weights = weight_blocks(table_proj, text_proj)
    mine = both_cores(mine, 1)
    z_table = dot(mine[0], table_weights[0], ((1,), (0,)))
    z_text = dot(mine[1], text_weights[0], ((1,), (0,)))
    z_table, z_text, others = lax.optimization_barrier((z_table, z_text, others))
    for other, table_weight, text_weight in zip(others, table_weights[1:], text_weights[1:]):
        other = both_cores(other, 1)
        z_table = z_table + dot(other[0], table_weight, ((1,), (0,)))
        z_text = z_text + dot(other[1], text_weight, ((1,), (0,)))

    centers, spreads = moments(z_table, z_text)
    inverse_table, inverse_text = lax.rsqrt(spreads[0] + EPS), lax.rsqrt(spreads[1] + EPS)
    diag = inverse_table * inverse_text * spreads[2]
    diag_weight = (diag - 1.0).astype(BF16).astype(F32) - OFF_WEIGHT * diag
    normed_table = (z_table - centers[0]) * inverse_table
    normed_text = (z_text - centers[1]) * inverse_text
    half_table, half_text = normed_table.astype(BF16), normed_text.astype(BF16)

    half = jnp.stack([half_table, half_text])
    near, mid, y_own = lax.optimization_barrier((flip(half, "z"), lax.ppermute(half, "z", [(1, 2), (2, 1)]), over_y(half)))
    far_in, far_end, y_near = lax.optimization_barrier(
        (lax.ppermute(near, "z", [(1, 2), (2, 1)]), lax.ppermute(mid, "z", [(1, 0), (2, 3)]), over_y(near))
    )
    far = at_end(far_end, far_in)
    last_end, y_far = lax.optimization_barrier((lax.ppermute(far_in, "z", [(1, 0), (2, 3)]), over_y(far)))
    last = at_end(last_end, mid)
    cut = half.shape[1] // 2
    y_last = over_y(last[:, :cut])
    y_flip = [flip(block[:, cut:], "z") for block in y_far]

    early = [half, near, far, *y_own, *y_near, *y_far]
    early_table, early_text = [jnp.concatenate([block[i] for block in early], 0) for i in range(2)]
    gram_table = gram_part(half_table, early_table)
    others_table = swap_feat(gram_table.astype(BF16))
    gram_text = gram_part(half_text, early_text)
    others_text = swap_feat(gram_text.astype(BF16))
    y_last, y_flip, others_table, gram_text = lax.optimization_barrier((y_last, y_flip, others_table, gram_text))
    late = [last] + [block for pair in zip(y_last, y_flip) for block in pair]
    late_table, late_text = [jnp.concatenate([block[i] for block in late], 0) for i in range(2)]
    all_table, all_text = (early_table, late_table), (early_text, late_text)
    late_gram = jnp.concatenate([gram_part(half_table, late_table), gram_part(half_text, late_text)], 1)
    late_gram = add_feat(late_gram, swap_feat(late_gram.astype(BF16)), 0)
    gram_table = add_feat(gram_table, others_table, 0)
    gram_text = add_feat(gram_text, others_text, 0)
    grams = (gram_table, gram_text), jnp.split(late_gram, 2, 1)

    off_table, off_text = 0.0, 0.0
    for gram, rows_table, rows_text in zip(grams, all_table, all_text):
        off_table = off_table + dot(gram[1], rows_table, ((1,), (0,)))
        off_text = off_text + dot(gram[0], rows_text, ((1,), (0,)))
    d_table = (OFF_WEIGHT / pairs) * off_table + half_text.astype(F32) * diag_weight
    d_text = (OFF_WEIGHT / pairs) * off_text + half_table.astype(F32) * diag_weight
    sums = jnp.concatenate([column_sums(d_text, normed_text), column_sums(d_table, normed_table)], 0)
    means = cube_sum(sums, "z", "y") / pairs

    squares = means[3] - diag_weight * diag
    terms = (1.0 - diag) * (1.0 - diag) - OFF_WEIGHT * diag * diag + squares
    loss_total = cube_sum(jnp.sum(terms).reshape(1), "feat")

    back_text = backward(d_text, normed_text, inverse_text, means[:2])
    parts_text = [dot(back_text, weight, ((1,), (1,))) for weight in text_weights[1:]]
    d_table, parts_text = lax.optimization_barrier((d_table, parts_text))
    sent_text = [add_cores(part).astype(BF16) for part in parts_text]
    back_table = backward(d_table, normed_table, inverse_table, means[2:])
    parts_table = [dot(back_table, weight, ((1,), (1,))) for weight in table_weights[1:]]
    sent_text, parts_table, back_text, loss_total = lax.optimization_barrier((sent_text, parts_table, back_text, loss_total))
    sent_table = [add_cores(part).astype(BF16) for part in parts_table]
    sent = [jnp.stack(pair) for pair in zip(sent_text, sent_table)]
    back_text, back_table, sent = lax.optimization_barrier((back_text, back_table, sent))
    grads = swap_parts(sent)
    own_text = dot(back_text, text_weights[0], ((1,), (1,)))
    own_table = dot(back_table, table_weights[0], ((1,), (1,)))
    loss_total = cube_sum(loss_total, "core")
    grad_text = add_cores(own_text) + sum(part[0].astype(F32) for part in grads)
    grad_table = add_cores(own_table) + sum(part[1].astype(F32) for part in grads)
    return grad_table, grad_text, loss_total / features


def solution(mesh):
    devices = mesh.devices
    split = Mesh(
        devices.reshape(Z_CHIPS, devices.shape[0] // (2 * Z_CHIPS), 2, devices.shape[1]),
        ("z", "y", "core", "feat"),
    )
    rows = ("z", "y", "core")
    placed = (P(rows, "feat"), P(rows, "feat"), P(None, "feat"), P(None, "feat"))
    return jax.shard_map(
        body,
        mesh=split,
        in_specs=placed,
        out_specs=(P(rows, "feat"), P(rows, "feat"), P()),
        check_vma=False,
    )
```

```python
import jax
import jax.numpy as jnp
from jax import lax
from jax.experimental import pallas as pl
from jax.experimental.pallas import tpu as pltpu
from jax.sharding import Mesh
from jax.sharding import PartitionSpec as P

OFF_WEIGHT = 0.1
EPS = 1e-05
Z_CHIPS = 4
F32 = jnp.float32
BF16 = jnp.bfloat16


def dot(a, b, dims):
    return lax.dot_general(a, b, (dims, ((), ())), preferred_element_type=F32)


def shift(x, axis, step):
    size = lax.axis_size(axis)
    return lax.ppermute(x, axis, [(i, (i + step) % size) for i in range(size)])


def flip(x, axis, bit=1):
    size = lax.axis_size(axis)
    return lax.ppermute(x, axis, [(i, i ^ bit) for i in range(size)])


def cube_sum(x, *axes):
    for axis in axes:
        bit = 1
        while bit < lax.axis_size(axis):
            x = x + flip(x, axis, bit)
            bit *= 2
    return x


def own_block(x, index, count, axis):
    size = x.shape[axis] // count
    return lax.dynamic_slice_in_dim(x, index * size, size, axis)


def both_cores(x, axis=0):
    got = flip(x, "core")
    first = lax.axis_index("core") == 0
    return jnp.where(first, jnp.concatenate([x, got], axis), jnp.concatenate([got, x], axis))


def add_cores(x):
    core = lax.axis_index("core")
    return own_block(x, core, 2, 0) + flip(own_block(x, 1 - core, 2, 0), "core")


def cut_kernel(starts, *refs):
    sources, blocks, sems = refs[:2], refs[2:-1], refs[-1]
    count = len(blocks) // 2
    rows, cols = blocks[0].shape
    copies = []
    for i, block in enumerate(blocks):
        row = pl.multiple_of(starts[1 + i % count], 16)
        col = pl.multiple_of(starts[0], 128)
        source = sources[i // count].at[pl.ds(row, rows), pl.ds(col, cols)]
        copies.append(pltpu.make_async_copy(source, block, sems.at[i]))
    for copy in copies:
        copy.start()
    for copy in copies:
        copy.wait()


def weight_blocks(table_proj, text_proj):
    num_feat = lax.axis_size("feat")
    feat = lax.axis_index("feat")
    rows, cols = table_proj.shape[0] // num_feat, table_proj.shape[1] // 2
    firsts = [(feat - step) % num_feat * rows for step in range(num_feat)]
    starts = jnp.stack([lax.axis_index("core") * cols, *firsts]).astype(jnp.int32)
    count = 2 * num_feat
    blocks = pl.pallas_call(
        cut_kernel,
        out_shape=[jax.ShapeDtypeStruct((rows, cols), BF16)] * count,
        in_specs=[pl.BlockSpec(memory_space=pltpu.SMEM), pl.BlockSpec(memory_space=pl.ANY), pl.BlockSpec(memory_space=pl.ANY)],
        out_specs=[pl.BlockSpec(memory_space=pltpu.VMEM)] * count,
        scratch_shapes=[pltpu.SemaphoreType.DMA((count,))],
        compiler_params=pltpu.CompilerParams(vmem_limit_bytes=40 * 1024 * 1024),
    )(starts, table_proj, text_proj)
    return blocks[:num_feat], blocks[num_feat:]


def swap_feat(x):
    return [shift(x, "feat", step) for step in range(1, lax.axis_size("feat"))]


def moments(z_table, z_text):
    count = z_table.shape[0]
    mean_table, mean_text = jnp.mean(z_table, axis=0), jnp.mean(z_text, axis=0)
    centered_table, centered_text = z_table - mean_table, z_text - mean_text
    state = jnp.stack(
        [
            mean_table,
            mean_text,
            jnp.sum(centered_table * centered_table, axis=0),
            jnp.sum(centered_text * centered_text, axis=0),
            jnp.sum(centered_table * centered_text, axis=0),
        ]
    )
    for axis in ("z", "y"):
        bit = 1
        while bit < lax.axis_size(axis):
            other = flip(state, axis, bit)
            gap = state[:2] - other[:2]
            moved = (count / 2) * jnp.concatenate([gap * gap, gap[:1] * gap[1:]], 0)
            state = jnp.concatenate([(state[:2] + other[:2]) / 2, state[2:] + other[2:] + moved], 0)
            count *= 2
            bit *= 2
    return state[:2], state[2:] / count


def at_end(end, inner):
    z = lax.axis_index("z")
    return jnp.where((z == 0) | (z == Z_CHIPS - 1), end, inner)


def over_y(x):
    return [flip(x, "y", step) for step in range(1, lax.axis_size("y"))]


def gram_part(half, rows):
    return add_cores(dot(half, rows, ((1,), (1,))))


def add_feat(mine, others, axis):
    for other in others:
        mine = mine + other.astype(F32)
    return both_cores(mine.astype(BF16), axis)


def column_sums(d, normed):
    return jnp.stack([jnp.sum(d, axis=0), jnp.sum(d * normed, axis=0)])


def backward(d, normed, inverse, means):
    return (inverse * (d - means[0] - normed * means[1])).astype(BF16)


def swap_parts(sent):
    num_feat = lax.axis_size("feat")
    return [shift(part, "feat", num_feat - step) for step, part in enumerate(sent, 1)]


def body(table, text, table_proj, text_proj):
    pairs = table.shape[0] * 2 * lax.axis_size("z") * lax.axis_size("y")
    features = table_proj.shape[1] * lax.axis_size("feat")
    others_table, others_text = swap_feat(table), swap_feat(text)
    table_weights, text_weights = weight_blocks(table_proj, text_proj)
    z_table = dot(both_cores(table), table_weights[0], ((1,), (0,)))
    z_text = dot(both_cores(text), text_weights[0], ((1,), (0,)))
    z_table, z_text, others_table, others_text = lax.optimization_barrier((z_table, z_text, others_table, others_text))
    for other, weight in zip(others_table, table_weights[1:]):
        z_table = z_table + dot(both_cores(other), weight, ((1,), (0,)))
    for other, weight in zip(others_text, text_weights[1:]):
        z_text = z_text + dot(both_cores(other), weight, ((1,), (0,)))

    centers, spreads = moments(z_table, z_text)
    inverse_table, inverse_text = lax.rsqrt(spreads[0] + EPS), lax.rsqrt(spreads[1] + EPS)
    diag = inverse_table * inverse_text * spreads[2]
    diag_weight = (diag - 1.0).astype(BF16).astype(F32) - OFF_WEIGHT * diag
    normed_table = (z_table - centers[0]) * inverse_table
    normed_text = (z_text - centers[1]) * inverse_text
    half_table, half_text = normed_table.astype(BF16), normed_text.astype(BF16)

    half = jnp.stack([half_table, half_text])
    near, mid, y_own = lax.optimization_barrier((flip(half, "z"), lax.ppermute(half, "z", [(1, 2), (2, 1)]), over_y(half)))
    far_in, far_end, y_near = lax.optimization_barrier(
        (lax.ppermute(near, "z", [(1, 2), (2, 1)]), lax.ppermute(mid, "z", [(1, 0), (2, 3)]), over_y(near))
    )
    far = at_end(far_end, far_in)
    last_end, y_far = lax.optimization_barrier((lax.ppermute(far_in, "z", [(1, 0), (2, 3)]), over_y(far)))
    last = at_end(last_end, mid)
    cut = half.shape[1] // 2
    y_last = over_y(last[:, :cut])
    y_flip = [flip(block[:, cut:], "z") for block in y_far]

    early = [half, near, far, *y_own, *y_near, *y_far]
    early_table, early_text = [jnp.concatenate([block[i] for block in early], 0) for i in range(2)]
    gram_table = gram_part(half_table, early_table)
    others_table = swap_feat(gram_table.astype(BF16))
    gram_text = gram_part(half_text, early_text)
    others_text = swap_feat(gram_text.astype(BF16))
    y_last, y_flip, others_table, gram_text = lax.optimization_barrier((y_last, y_flip, others_table, gram_text))
    late = [last] + [block for pair in zip(y_last, y_flip) for block in pair]
    late_table, late_text = [jnp.concatenate([block[i] for block in late], 0) for i in range(2)]
    all_table, all_text = (early_table, late_table), (early_text, late_text)
    late_gram = jnp.concatenate([gram_part(half_table, late_table), gram_part(half_text, late_text)], 1)
    late_gram = add_feat(late_gram, swap_feat(late_gram.astype(BF16)), 0)
    gram_table = add_feat(gram_table, others_table, 0)
    gram_text = add_feat(gram_text, others_text, 0)
    grams = (gram_table, gram_text), jnp.split(late_gram, 2, 1)

    off_table, off_text = 0.0, 0.0
    for gram, rows_table, rows_text in zip(grams, all_table, all_text):
        off_table = off_table + dot(gram[1], rows_table, ((1,), (0,)))
        off_text = off_text + dot(gram[0], rows_text, ((1,), (0,)))
    d_table = (OFF_WEIGHT / pairs) * off_table + half_text.astype(F32) * diag_weight
    d_text = (OFF_WEIGHT / pairs) * off_text + half_table.astype(F32) * diag_weight
    sums = jnp.concatenate([column_sums(d_text, normed_text), column_sums(d_table, normed_table)], 0)
    means = cube_sum(sums, "z", "y") / pairs

    squares = means[3] - diag_weight * diag
    terms = (1.0 - diag) * (1.0 - diag) - OFF_WEIGHT * diag * diag + squares
    loss_total = cube_sum(jnp.sum(terms).reshape(1), "feat")

    back_text = backward(d_text, normed_text, inverse_text, means[:2])
    parts_text = [dot(back_text, weight, ((1,), (1,))) for weight in text_weights[1:]]
    d_table, parts_text = lax.optimization_barrier((d_table, parts_text))
    sent_text = [add_cores(part).astype(BF16) for part in parts_text]
    back_table = backward(d_table, normed_table, inverse_table, means[2:])
    parts_table = [dot(back_table, weight, ((1,), (1,))) for weight in table_weights[1:]]
    sent_text, parts_table, back_text, loss_total = lax.optimization_barrier((sent_text, parts_table, back_text, loss_total))
    sent_table = [add_cores(part).astype(BF16) for part in parts_table]
    sent = [jnp.stack(pair) for pair in zip(sent_text, sent_table)]
    own_text = dot(back_text, text_weights[0], ((1,), (1,)))
    own_table = dot(back_table, table_weights[0], ((1,), (1,)))
    own_text, own_table, sent = lax.optimization_barrier((own_text, own_table, sent))
    grads = swap_parts(sent)
    loss_total = cube_sum(loss_total, "core")
    grad_text = add_cores(own_text) + sum(part[0].astype(F32) for part in grads)
    grad_table = add_cores(own_table) + sum(part[1].astype(F32) for part in grads)
    return grad_table, grad_text, loss_total / features


def solution(mesh):
    devices = mesh.devices
    split = Mesh(
        devices.reshape(Z_CHIPS, devices.shape[0] // (2 * Z_CHIPS), 2, devices.shape[1]),
        ("z", "y", "core", "feat"),
    )
    rows = ("z", "y", "core")
    placed = (P(rows, "feat"), P(rows, "feat"), P(None, "feat"), P(None, "feat"))
    return jax.shard_map(
        body,
        mesh=split,
        in_specs=placed,
        out_specs=(P(rows, "feat"), P(rows, "feat"), P()),
        check_vma=False,
    )
```

```python
import jax
import jax.numpy as jnp
from jax import lax
from jax.experimental import pallas as pl
from jax.experimental.pallas import tpu as pltpu
from jax.sharding import Mesh
from jax.sharding import PartitionSpec as P

OFF_WEIGHT = 0.1
EPS = 1e-05
Z_CHIPS = 4
F32 = jnp.float32
BF16 = jnp.bfloat16


def dot(a, b, dims):
    return lax.dot_general(a, b, (dims, ((), ())), preferred_element_type=F32)


def shift(x, axis, step):
    size = lax.axis_size(axis)
    return lax.ppermute(x, axis, [(i, (i + step) % size) for i in range(size)])


def flip(x, axis, bit=1):
    size = lax.axis_size(axis)
    return lax.ppermute(x, axis, [(i, i ^ bit) for i in range(size)])


def cube_sum(x, *axes):
    for axis in axes:
        bit = 1
        while bit < lax.axis_size(axis):
            x = x + flip(x, axis, bit)
            bit *= 2
    return x


def own_block(x, index, count, axis):
    size = x.shape[axis] // count
    return lax.dynamic_slice_in_dim(x, index * size, size, axis)


def both_cores(x, axis=0):
    got = flip(x, "core")
    first = lax.axis_index("core") == 0
    return jnp.where(first, jnp.concatenate([x, got], axis), jnp.concatenate([got, x], axis))


def add_cores(x):
    core = lax.axis_index("core")
    return own_block(x, core, 2, 0) + flip(own_block(x, 1 - core, 2, 0), "core")


def cut_kernel(starts, *refs):
    sources, blocks, sems = refs[:2], refs[2:-1], refs[-1]
    count = len(blocks) // 2
    rows, cols = blocks[0].shape
    copies = []
    for i, block in enumerate(blocks):
        row = pl.multiple_of(starts[1 + i % count], 16)
        col = pl.multiple_of(starts[0], 128)
        source = sources[i // count].at[pl.ds(row, rows), pl.ds(col, cols)]
        copies.append(pltpu.make_async_copy(source, block, sems.at[i]))
    for copy in copies:
        copy.start()
    for copy in copies:
        copy.wait()


def weight_blocks(table_proj, text_proj):
    num_feat = lax.axis_size("feat")
    feat = lax.axis_index("feat")
    rows, cols = table_proj.shape[0] // num_feat, table_proj.shape[1] // 2
    firsts = [(feat - step) % num_feat * rows for step in range(num_feat)]
    starts = jnp.stack([lax.axis_index("core") * cols, *firsts]).astype(jnp.int32)
    count = 2 * num_feat
    blocks = pl.pallas_call(
        cut_kernel,
        out_shape=[jax.ShapeDtypeStruct((rows, cols), BF16)] * count,
        in_specs=[pl.BlockSpec(memory_space=pltpu.SMEM), pl.BlockSpec(memory_space=pl.ANY), pl.BlockSpec(memory_space=pl.ANY)],
        out_specs=[pl.BlockSpec(memory_space=pltpu.VMEM)] * count,
        scratch_shapes=[pltpu.SemaphoreType.DMA((count,))],
        compiler_params=pltpu.CompilerParams(vmem_limit_bytes=40 * 1024 * 1024),
    )(starts, table_proj, text_proj)
    return blocks[:num_feat], blocks[num_feat:]


def swap_feat(x):
    return [shift(x, "feat", step) for step in range(1, lax.axis_size("feat"))]


def moments(z_table, z_text):
    count = z_table.shape[0]
    mean_table, mean_text = jnp.mean(z_table, axis=0), jnp.mean(z_text, axis=0)
    centered_table, centered_text = z_table - mean_table, z_text - mean_text
    state = jnp.stack(
        [
            mean_table,
            mean_text,
            jnp.sum(centered_table * centered_table, axis=0),
            jnp.sum(centered_text * centered_text, axis=0),
            jnp.sum(centered_table * centered_text, axis=0),
        ]
    )
    for axis in ("z", "y"):
        bit = 1
        while bit < lax.axis_size(axis):
            other = flip(state, axis, bit)
            gap = state[:2] - other[:2]
            moved = (count / 2) * jnp.concatenate([gap * gap, gap[:1] * gap[1:]], 0)
            state = jnp.concatenate([(state[:2] + other[:2]) / 2, state[2:] + other[2:] + moved], 0)
            count *= 2
            bit *= 2
    return state[:2], state[2:] / count


def at_end(end, inner):
    z = lax.axis_index("z")
    return jnp.where((z == 0) | (z == Z_CHIPS - 1), end, inner)


def over_y(x):
    return [flip(x, "y", step) for step in range(1, lax.axis_size("y"))]


def gram_part(half, rows):
    return add_cores(dot(half, rows, ((1,), (1,))))


def add_feat(mine, others, axis):
    for other in others:
        mine = mine + other.astype(F32)
    return both_cores(mine.astype(BF16), axis)


def column_sums(d, normed):
    return jnp.stack([jnp.sum(d, axis=0), jnp.sum(d * normed, axis=0)])


def backward(d, normed, inverse, means):
    return (inverse * (d - means[0] - normed * means[1])).astype(BF16)


def swap_parts(sent):
    num_feat = lax.axis_size("feat")
    return [shift(part, "feat", num_feat - step) for step, part in enumerate(sent, 1)]


def body(table, text, table_proj, text_proj):
    pairs = table.shape[0] * 2 * lax.axis_size("z") * lax.axis_size("y")
    features = table_proj.shape[1] * lax.axis_size("feat")
    others_table, others_text = swap_feat(table), swap_feat(text)
    table_weights, text_weights = weight_blocks(table_proj, text_proj)
    z_table = dot(both_cores(table), table_weights[0], ((1,), (0,)))
    z_text = dot(both_cores(text), text_weights[0], ((1,), (0,)))
    z_table, z_text, others_table, others_text = lax.optimization_barrier((z_table, z_text, others_table, others_text))
    for other, weight in zip(others_table, table_weights[1:]):
        z_table = z_table + dot(both_cores(other), weight, ((1,), (0,)))
    for other, weight in zip(others_text, text_weights[1:]):
        z_text = z_text + dot(both_cores(other), weight, ((1,), (0,)))

    centers, spreads = moments(z_table, z_text)
    inverse_table, inverse_text = lax.rsqrt(spreads[0] + EPS), lax.rsqrt(spreads[1] + EPS)
    diag = inverse_table * inverse_text * spreads[2]
    diag_weight = (diag - 1.0).astype(BF16).astype(F32) - OFF_WEIGHT * diag
    normed_table = (z_table - centers[0]) * inverse_table
    normed_text = (z_text - centers[1]) * inverse_text
    half_table, half_text = normed_table.astype(BF16), normed_text.astype(BF16)

    half = jnp.stack([half_table, half_text])
    near, mid, y_own = lax.optimization_barrier((flip(half, "z"), lax.ppermute(half, "z", [(1, 2), (2, 1)]), over_y(half)))
    far_in, far_end, y_near = lax.optimization_barrier(
        (lax.ppermute(near, "z", [(1, 2), (2, 1)]), lax.ppermute(mid, "z", [(1, 0), (2, 3)]), over_y(near))
    )
    far = at_end(far_end, far_in)
    last_end, y_far = lax.optimization_barrier((lax.ppermute(far_in, "z", [(1, 0), (2, 3)]), over_y(far)))
    last = at_end(last_end, mid)
    cut = half.shape[1] // 2
    y_last = over_y(last[:, :cut])
    y_flip = [flip(block[:, cut:], "z") for block in y_far]

    early = [half, near, far, *y_own, *y_near, *y_far]
    early_table, early_text = [jnp.concatenate([block[i] for block in early], 0) for i in range(2)]
    gram_table = gram_part(half_table, early_table)
    others_table = swap_feat(gram_table.astype(BF16))
    gram_text = gram_part(half_text, early_text)
    gram_text = jnp.split(gram_text, 2, 1)
    others_text = [swap_feat(part.astype(BF16)) for part in gram_text]
    y_last, y_flip, others_table, others_text[0] = lax.optimization_barrier((y_last, y_flip, others_table, others_text[0]))
    late = [last] + [block for pair in zip(y_last, y_flip) for block in pair]
    late_table, late_text = [jnp.concatenate([block[i] for block in late], 0) for i in range(2)]
    all_table, all_text = (early_table, late_table), (early_text, late_text)
    late_gram = jnp.concatenate([gram_part(half_table, late_table), gram_part(half_text, late_text)], 1)
    late_gram = add_feat(late_gram, swap_feat(late_gram.astype(BF16)), 0)
    gram_table = add_feat(gram_table, others_table, 0)
    others_text = [jnp.concatenate(parts, 1) for parts in zip(*others_text)]
    gram_text = add_feat(jnp.concatenate(gram_text, 1), others_text, 0)
    grams = (gram_table, gram_text), jnp.split(late_gram, 2, 1)

    off_table, off_text = 0.0, 0.0
    for gram, rows_table, rows_text in zip(grams, all_table, all_text):
        off_table = off_table + dot(gram[1], rows_table, ((1,), (0,)))
        off_text = off_text + dot(gram[0], rows_text, ((1,), (0,)))
    d_table = (OFF_WEIGHT / pairs) * off_table + half_text.astype(F32) * diag_weight
    d_text = (OFF_WEIGHT / pairs) * off_text + half_table.astype(F32) * diag_weight
    sums = jnp.concatenate([column_sums(d_text, normed_text), column_sums(d_table, normed_table)], 0)
    means = cube_sum(sums, "z", "y") / pairs

    squares = means[3] - diag_weight * diag
    terms = (1.0 - diag) * (1.0 - diag) - OFF_WEIGHT * diag * diag + squares
    loss_total = cube_sum(jnp.sum(terms).reshape(1), "feat")

    back_text = backward(d_text, normed_text, inverse_text, means[:2])
    parts_text = [dot(back_text, weight, ((1,), (1,))) for weight in text_weights[1:]]
    d_table, parts_text = lax.optimization_barrier((d_table, parts_text))
    sent_text = [add_cores(part).astype(BF16) for part in parts_text]
    back_table = backward(d_table, normed_table, inverse_table, means[2:])
    parts_table = [dot(back_table, weight, ((1,), (1,))) for weight in table_weights[1:]]
    sent_text, parts_table, back_text, loss_total = lax.optimization_barrier((sent_text, parts_table, back_text, loss_total))
    sent_table = [add_cores(part).astype(BF16) for part in parts_table]
    sent = [jnp.stack(pair) for pair in zip(sent_text, sent_table)]
    own_text = dot(back_text, text_weights[0], ((1,), (1,)))
    own_table = dot(back_table, table_weights[0], ((1,), (1,)))
    own_text, own_table, sent = lax.optimization_barrier((own_text, own_table, sent))
    grads = swap_parts(sent)
    loss_total = cube_sum(loss_total, "core")
    grad_text = add_cores(own_text) + sum(part[0].astype(F32) for part in grads)
    grad_table = add_cores(own_table) + sum(part[1].astype(F32) for part in grads)
    return grad_table, grad_text, loss_total / features


def solution(mesh):
    devices = mesh.devices
    split = Mesh(
        devices.reshape(Z_CHIPS, devices.shape[0] // (2 * Z_CHIPS), 2, devices.shape[1]),
        ("z", "y", "core", "feat"),
    )
    rows = ("z", "y", "core")
    placed = (P(rows, "feat"), P(rows, "feat"), P(None, "feat"), P(None, "feat"))
    return jax.shard_map(
        body,
        mesh=split,
        in_specs=placed,
        out_specs=(P(rows, "feat"), P(rows, "feat"), P()),
        check_vma=False,
    )
```

```python
import jax
import jax.numpy as jnp
from jax import lax
from jax.experimental import pallas as pl
from jax.experimental.pallas import tpu as pltpu
from jax.sharding import Mesh
from jax.sharding import PartitionSpec as P

OFF_WEIGHT = 0.1
EPS = 1e-05
Z_CHIPS = 4
F32 = jnp.float32
BF16 = jnp.bfloat16


def dot(a, b, dims):
    return lax.dot_general(a, b, (dims, ((), ())), preferred_element_type=F32)


def shift(x, axis, step):
    size = lax.axis_size(axis)
    return lax.ppermute(x, axis, [(i, (i + step) % size) for i in range(size)])


def flip(x, axis, bit=1):
    size = lax.axis_size(axis)
    return lax.ppermute(x, axis, [(i, i ^ bit) for i in range(size)])


def cube_sum(x, *axes):
    for axis in axes:
        bit = 1
        while bit < lax.axis_size(axis):
            x = x + flip(x, axis, bit)
            bit *= 2
    return x


def own_block(x, index, count, axis):
    size = x.shape[axis] // count
    return lax.dynamic_slice_in_dim(x, index * size, size, axis)


def both_cores(x, axis=0):
    got = flip(x, "core")
    first = lax.axis_index("core") == 0
    return jnp.where(first, jnp.concatenate([x, got], axis), jnp.concatenate([got, x], axis))


def add_cores(x):
    core = lax.axis_index("core")
    return own_block(x, core, 2, 0) + flip(own_block(x, 1 - core, 2, 0), "core")


def cut_kernel(starts, *refs):
    sources, blocks, sems = refs[:2], refs[2:-1], refs[-1]
    count = len(blocks) // 2
    rows, cols = blocks[0].shape
    copies = []
    for i, block in enumerate(blocks):
        row = pl.multiple_of(starts[1 + i % count], 16)
        col = pl.multiple_of(starts[0], 128)
        source = sources[i // count].at[pl.ds(row, rows), pl.ds(col, cols)]
        copies.append(pltpu.make_async_copy(source, block, sems.at[i]))
    for copy in copies:
        copy.start()
    for copy in copies:
        copy.wait()


def weight_blocks(table_proj, text_proj):
    num_feat = lax.axis_size("feat")
    feat = lax.axis_index("feat")
    rows, cols = table_proj.shape[0] // num_feat, table_proj.shape[1] // 2
    firsts = [(feat - step) % num_feat * rows for step in range(num_feat)]
    starts = jnp.stack([lax.axis_index("core") * cols, *firsts]).astype(jnp.int32)
    count = 2 * num_feat
    blocks = pl.pallas_call(
        cut_kernel,
        out_shape=[jax.ShapeDtypeStruct((rows, cols), BF16)] * count,
        in_specs=[pl.BlockSpec(memory_space=pltpu.SMEM), pl.BlockSpec(memory_space=pl.ANY), pl.BlockSpec(memory_space=pl.ANY)],
        out_specs=[pl.BlockSpec(memory_space=pltpu.VMEM)] * count,
        scratch_shapes=[pltpu.SemaphoreType.DMA((count,))],
        compiler_params=pltpu.CompilerParams(vmem_limit_bytes=40 * 1024 * 1024),
    )(starts, table_proj, text_proj)
    return blocks[:num_feat], blocks[num_feat:]


def swap_feat(x):
    return [shift(x, "feat", step) for step in range(1, lax.axis_size("feat"))]


def moments(z_table, z_text):
    count = z_table.shape[0]
    mean_table, mean_text = jnp.mean(z_table, axis=0), jnp.mean(z_text, axis=0)
    centered_table, centered_text = z_table - mean_table, z_text - mean_text
    state = jnp.stack(
        [
            mean_table,
            mean_text,
            jnp.sum(centered_table * centered_table, axis=0),
            jnp.sum(centered_text * centered_text, axis=0),
            jnp.sum(centered_table * centered_text, axis=0),
        ]
    )
    for axis in ("z", "y"):
        bit = 1
        while bit < lax.axis_size(axis):
            other = flip(state, axis, bit)
            gap = state[:2] - other[:2]
            moved = (count / 2) * jnp.concatenate([gap * gap, gap[:1] * gap[1:]], 0)
            state = jnp.concatenate([(state[:2] + other[:2]) / 2, state[2:] + other[2:] + moved], 0)
            count *= 2
            bit *= 2
    return state[:2], state[2:] / count


def at_end(end, inner):
    z = lax.axis_index("z")
    return jnp.where((z == 0) | (z == Z_CHIPS - 1), end, inner)


def over_y(x):
    return [flip(x, "y", step) for step in range(1, lax.axis_size("y"))]


def gram_part(half, rows):
    return add_cores(dot(half, rows, ((1,), (1,))))


def add_feat(mine, others, axis):
    for other in others:
        mine = mine + other.astype(F32)
    return both_cores(mine.astype(BF16), axis)


def column_sums(d, normed):
    return jnp.stack([jnp.sum(d, axis=0), jnp.sum(d * normed, axis=0)])


def backward(d, normed, inverse, means):
    return (inverse * (d - means[0] - normed * means[1])).astype(BF16)


def swap_parts(sent):
    num_feat = lax.axis_size("feat")
    return [shift(part, "feat", num_feat - step) for step, part in enumerate(sent, 1)]


def body(table, text, table_proj, text_proj):
    pairs = table.shape[0] * 2 * lax.axis_size("z") * lax.axis_size("y")
    features = table_proj.shape[1] * lax.axis_size("feat")
    others_table, others_text = swap_feat(table), swap_feat(text)
    table_weights, text_weights = weight_blocks(table_proj, text_proj)
    z_table = dot(both_cores(table), table_weights[0], ((1,), (0,)))
    z_text = dot(both_cores(text), text_weights[0], ((1,), (0,)))
    z_table, z_text, others_table, others_text = lax.optimization_barrier((z_table, z_text, others_table, others_text))
    for other, weight in zip(others_table, table_weights[1:]):
        z_table = z_table + dot(both_cores(other), weight, ((1,), (0,)))
    for other, weight in zip(others_text, text_weights[1:]):
        z_text = z_text + dot(both_cores(other), weight, ((1,), (0,)))

    centers, spreads = moments(z_table, z_text)
    inverse_table, inverse_text = lax.rsqrt(spreads[0] + EPS), lax.rsqrt(spreads[1] + EPS)
    diag = inverse_table * inverse_text * spreads[2]
    diag_weight = (diag - 1.0).astype(BF16).astype(F32) - OFF_WEIGHT * diag
    normed_table = (z_table - centers[0]) * inverse_table
    normed_text = (z_text - centers[1]) * inverse_text
    half_table, half_text = normed_table.astype(BF16), normed_text.astype(BF16)

    half = jnp.stack([half_table, half_text])
    near, mid, y_own = lax.optimization_barrier((flip(half, "z"), lax.ppermute(half, "z", [(1, 2), (2, 1)]), over_y(half)))
    far_in, far_end, y_near = lax.optimization_barrier(
        (lax.ppermute(near, "z", [(1, 2), (2, 1)]), lax.ppermute(mid, "z", [(1, 0), (2, 3)]), over_y(near))
    )
    far = at_end(far_end, far_in)
    last_end, y_far = lax.optimization_barrier((lax.ppermute(far_in, "z", [(1, 0), (2, 3)]), over_y(far)))
    last = at_end(last_end, mid)
    cut = half.shape[1] // 2
    y_last = over_y(last[:, :cut])
    y_flip = [flip(block[:, cut:], "z") for block in y_far]

    early = [half, near, far, *y_own, *y_near, *y_far]
    early_table, early_text = [jnp.concatenate([block[i] for block in early], 0) for i in range(2)]
    gram_table = gram_part(half_table, early_table)
    others_table = swap_feat(gram_table.astype(BF16))
    gram_text = gram_part(half_text, early_text)
    gram_text = jnp.split(gram_text, 2, 1)
    others_text = [swap_feat(part.astype(BF16)) for part in gram_text]
    y_last, y_flip, others_table, others_text[0] = lax.optimization_barrier((y_last, y_flip, others_table, others_text[0]))
    late = [last] + [block for pair in zip(y_last, y_flip) for block in pair]
    late_table, late_text = [jnp.concatenate([block[i] for block in late], 0) for i in range(2)]
    all_table, all_text = (early_table, late_table), (early_text, late_text)
    late_gram = jnp.concatenate([gram_part(half_table, late_table), gram_part(half_text, late_text)], 1)
    late_gram = add_feat(late_gram, swap_feat(late_gram.astype(BF16)), 0)
    gram_table = add_feat(gram_table, others_table, 0)
    others_text = [jnp.concatenate(parts, 1) for parts in zip(*others_text)]
    gram_text = add_feat(jnp.concatenate(gram_text, 1), others_text, 0)
    grams = (gram_table, gram_text), jnp.split(late_gram, 2, 1)

    off_table, off_text = 0.0, 0.0
    for gram, rows_table, rows_text in zip(grams, all_table, all_text):
        off_table = off_table + dot(gram[1], rows_table, ((1,), (0,)))
        off_text = off_text + dot(gram[0], rows_text, ((1,), (0,)))
    d_table = (OFF_WEIGHT / pairs) * off_table + half_text.astype(F32) * diag_weight
    d_text = (OFF_WEIGHT / pairs) * off_text + half_table.astype(F32) * diag_weight
    sums = jnp.concatenate([column_sums(d_text, normed_text), column_sums(d_table, normed_table)], 0)
    means = cube_sum(sums, "z", "y") / pairs

    squares = means[3] - diag_weight * diag
    terms = (1.0 - diag) * (1.0 - diag) - OFF_WEIGHT * diag * diag + squares
    loss_total = cube_sum(jnp.sum(terms).reshape(1), "feat")

    back_text = backward(d_text, normed_text, inverse_text, means[:2])
    parts_text = [dot(back_text, weight, ((1,), (1,))) for weight in text_weights[1:]]
    d_table, parts_text = lax.optimization_barrier((d_table, parts_text))
    sent_text = [add_cores(part).astype(BF16) for part in parts_text]
    back_table = backward(d_table, normed_table, inverse_table, means[2:])
    parts_table = [dot(back_table, weight, ((1,), (1,))) for weight in table_weights[1:]]
    sent_text, parts_table, back_text, loss_total = lax.optimization_barrier((sent_text, parts_table, back_text, loss_total))
    sent_table = [add_cores(part).astype(BF16) for part in parts_table]
    cut = sent_text[0].shape[0] // 4
    first_grads = swap_parts([part[:cut] for part in sent_text])
    sent = [jnp.concatenate([first[cut:], second], 0) for first, second in zip(sent_text, sent_table)]
    own_text = dot(back_text, text_weights[0], ((1,), (1,)))
    own_table = dot(back_table, table_weights[0], ((1,), (1,)))
    own_text, own_table, sent, first_grads = lax.optimization_barrier((own_text, own_table, sent, first_grads))
    grads = [jnp.concatenate(parts, 0) for parts in zip(first_grads, swap_parts(sent))]
    loss_total = cube_sum(loss_total, "core")
    grad_text, grad_table = add_cores(own_text), add_cores(own_table)
    for part in grads:
        got_text, got_table = jnp.split(part, 2)
        grad_text, grad_table = grad_text + got_text.astype(F32), grad_table + got_table.astype(F32)
    return grad_table, grad_text, loss_total / features


def solution(mesh):
    devices = mesh.devices
    split = Mesh(
        devices.reshape(Z_CHIPS, devices.shape[0] // (2 * Z_CHIPS), 2, devices.shape[1]),
        ("z", "y", "core", "feat"),
    )
    rows = ("z", "y", "core")
    placed = (P(rows, "feat"), P(rows, "feat"), P(None, "feat"), P(None, "feat"))
    return jax.shard_map(
        body,
        mesh=split,
        in_specs=placed,
        out_specs=(P(rows, "feat"), P(rows, "feat"), P()),
        check_vma=False,
    )
```

```python
import jax
import jax.numpy as jnp
from jax import lax
from jax.experimental import pallas as pl
from jax.experimental.pallas import tpu as pltpu
from jax.sharding import Mesh
from jax.sharding import PartitionSpec as P

OFF_WEIGHT = 0.1
EPS = 1e-05
Z_CHIPS = 4
F32 = jnp.float32
BF16 = jnp.bfloat16


def dot(a, b, dims):
    return lax.dot_general(a, b, (dims, ((), ())), preferred_element_type=F32)


def shift(x, axis, step):
    size = lax.axis_size(axis)
    return lax.ppermute(x, axis, [(i, (i + step) % size) for i in range(size)])


def flip(x, axis, bit=1):
    size = lax.axis_size(axis)
    return lax.ppermute(x, axis, [(i, i ^ bit) for i in range(size)])


def cube_sum(x, *axes):
    for axis in axes:
        bit = 1
        while bit < lax.axis_size(axis):
            x = x + flip(x, axis, bit)
            bit *= 2
    return x


def own_block(x, index, count, axis):
    size = x.shape[axis] // count
    return lax.dynamic_slice_in_dim(x, index * size, size, axis)


def both_cores(x, axis=0):
    got = flip(x, "core")
    first = lax.axis_index("core") == 0
    return jnp.where(first, jnp.concatenate([x, got], axis), jnp.concatenate([got, x], axis))


def add_cores(x):
    core = lax.axis_index("core")
    return own_block(x, core, 2, 0) + flip(own_block(x, 1 - core, 2, 0), "core")


def cut_kernel(starts, *refs):
    sources, blocks, sems = refs[:2], refs[2:-1], refs[-1]
    count = len(blocks) // 2
    rows, cols = blocks[0].shape
    copies = []
    for i, block in enumerate(blocks):
        row = pl.multiple_of(starts[1 + i % count], 16)
        col = pl.multiple_of(starts[0], 128)
        source = sources[i // count].at[pl.ds(row, rows), pl.ds(col, cols)]
        copies.append(pltpu.make_async_copy(source, block, sems.at[i]))
    for copy in copies:
        copy.start()
    for copy in copies:
        copy.wait()


def weight_blocks(table_proj, text_proj):
    num_feat = lax.axis_size("feat")
    feat = lax.axis_index("feat")
    rows, cols = table_proj.shape[0] // num_feat, table_proj.shape[1] // 2
    firsts = [(feat - step) % num_feat * rows for step in range(num_feat)]
    starts = jnp.stack([lax.axis_index("core") * cols, *firsts]).astype(jnp.int32)
    count = 2 * num_feat
    blocks = pl.pallas_call(
        cut_kernel,
        out_shape=[jax.ShapeDtypeStruct((rows, cols), BF16)] * count,
        in_specs=[pl.BlockSpec(memory_space=pltpu.SMEM), pl.BlockSpec(memory_space=pl.ANY), pl.BlockSpec(memory_space=pl.ANY)],
        out_specs=[pl.BlockSpec(memory_space=pltpu.VMEM)] * count,
        scratch_shapes=[pltpu.SemaphoreType.DMA((count,))],
        compiler_params=pltpu.CompilerParams(vmem_limit_bytes=40 * 1024 * 1024),
    )(starts, table_proj, text_proj)
    return blocks[:num_feat], blocks[num_feat:]


def swap_feat(x):
    return [shift(x, "feat", step) for step in range(1, lax.axis_size("feat"))]


def moments(z_table, z_text):
    count = z_table.shape[0]
    mean_table, mean_text = jnp.mean(z_table, axis=0), jnp.mean(z_text, axis=0)
    centered_table, centered_text = z_table - mean_table, z_text - mean_text
    state = jnp.stack(
        [
            mean_table,
            mean_text,
            jnp.sum(centered_table * centered_table, axis=0),
            jnp.sum(centered_text * centered_text, axis=0),
            jnp.sum(centered_table * centered_text, axis=0),
        ]
    )
    for axis in ("z", "y"):
        bit = 1
        while bit < lax.axis_size(axis):
            other = flip(state, axis, bit)
            gap = state[:2] - other[:2]
            moved = (count / 2) * jnp.concatenate([gap * gap, gap[:1] * gap[1:]], 0)
            state = jnp.concatenate([(state[:2] + other[:2]) / 2, state[2:] + other[2:] + moved], 0)
            count *= 2
            bit *= 2
    return state[:2], state[2:] / count


def at_end(end, inner):
    z = lax.axis_index("z")
    return jnp.where((z == 0) | (z == Z_CHIPS - 1), end, inner)


def over_y(x):
    return [flip(x, "y", step) for step in range(1, lax.axis_size("y"))]


def gram_part(half, rows):
    return add_cores(dot(half, rows, ((1,), (1,))))


def add_feat(mine, others, axis):
    for other in others:
        mine = mine + other.astype(F32)
    return both_cores(mine.astype(BF16), axis)


def column_sums(d, normed):
    return jnp.stack([jnp.sum(d, axis=0), jnp.sum(d * normed, axis=0)])


def backward(d, normed, inverse, means):
    return (inverse * (d - means[0] - normed * means[1])).astype(BF16)


def swap_parts(sent):
    num_feat = lax.axis_size("feat")
    return [shift(part, "feat", num_feat - step) for step, part in enumerate(sent, 1)]


def body(table, text, table_proj, text_proj):
    pairs = table.shape[0] * 2 * lax.axis_size("z") * lax.axis_size("y")
    features = table_proj.shape[1] * lax.axis_size("feat")
    others_table, others_text = swap_feat(table), swap_feat(text)
    table_weights, text_weights = weight_blocks(table_proj, text_proj)
    z_table = dot(both_cores(table), table_weights[0], ((1,), (0,)))
    z_text = dot(both_cores(text), text_weights[0], ((1,), (0,)))
    z_table, z_text, others_table, others_text = lax.optimization_barrier((z_table, z_text, others_table, others_text))
    for other, weight in zip(others_table, table_weights[1:]):
        z_table = z_table + dot(both_cores(other), weight, ((1,), (0,)))
    for other, weight in zip(others_text, text_weights[1:]):
        z_text = z_text + dot(both_cores(other), weight, ((1,), (0,)))

    centers, spreads = moments(z_table, z_text)
    inverse_table, inverse_text = lax.rsqrt(spreads[0] + EPS), lax.rsqrt(spreads[1] + EPS)
    diag = inverse_table * inverse_text * spreads[2]
    diag_weight = (diag - 1.0).astype(BF16).astype(F32) - OFF_WEIGHT * diag
    normed_table = (z_table - centers[0]) * inverse_table
    normed_text = (z_text - centers[1]) * inverse_text
    half_table, half_text = normed_table.astype(BF16), normed_text.astype(BF16)

    half = jnp.stack([half_table, half_text])
    near, mid, y_own = lax.optimization_barrier((flip(half, "z"), lax.ppermute(half, "z", [(1, 2), (2, 1)]), over_y(half)))
    far_in, far_end, y_near = lax.optimization_barrier(
        (lax.ppermute(near, "z", [(1, 2), (2, 1)]), lax.ppermute(mid, "z", [(1, 0), (2, 3)]), over_y(near))
    )
    far = at_end(far_end, far_in)
    last_end, y_far = lax.optimization_barrier((lax.ppermute(far_in, "z", [(1, 0), (2, 3)]), over_y(far)))
    last = at_end(last_end, mid)
    cut = half.shape[1] // 2
    y_last = over_y(last[:, :cut])
    y_flip = [flip(block[:, cut:], "z") for block in y_far]

    early = [half, near, far, *y_own, *y_near, *y_far]
    early_table, early_text = [jnp.concatenate([block[i] for block in early], 0) for i in range(2)]
    gram_table = gram_part(half_table, early_table)
    others_table = swap_feat(gram_table.astype(BF16))
    gram_text = gram_part(half_text, early_text)
    gram_text = jnp.split(gram_text, 2, 1)
    others_text = [swap_feat(part.astype(BF16)) for part in gram_text]
    y_last, y_flip, others_table, others_text[0] = lax.optimization_barrier((y_last, y_flip, others_table, others_text[0]))
    late = [last] + [block for pair in zip(y_last, y_flip) for block in pair]
    late_table, late_text = [jnp.concatenate([block[i] for block in late], 0) for i in range(2)]
    all_table, all_text = (early_table, late_table), (early_text, late_text)
    late_gram = jnp.concatenate([gram_part(half_table, late_table), gram_part(half_text, late_text)], 1)
    late_gram = add_feat(late_gram, swap_feat(late_gram.astype(BF16)), 0)
    gram_table = add_feat(gram_table, others_table, 0)
    others_text = [jnp.concatenate(parts, 1) for parts in zip(*others_text)]
    gram_text = add_feat(jnp.concatenate(gram_text, 1), others_text, 0)
    grams = (gram_table, gram_text), jnp.split(late_gram, 2, 1)

    off_table, off_text = 0.0, 0.0
    for gram, rows_table, rows_text in zip(grams, all_table, all_text):
        off_table = off_table + dot(gram[1], rows_table, ((1,), (0,)))
        off_text = off_text + dot(gram[0], rows_text, ((1,), (0,)))
    d_table = (OFF_WEIGHT / pairs) * off_table + half_text.astype(F32) * diag_weight
    d_text = (OFF_WEIGHT / pairs) * off_text + half_table.astype(F32) * diag_weight
    sums = jnp.concatenate([column_sums(d_text, normed_text), column_sums(d_table, normed_table)], 0)
    means = cube_sum(sums, "z", "y") / pairs

    squares = means[3] - diag_weight * diag
    terms = (1.0 - diag) * (1.0 - diag) - OFF_WEIGHT * diag * diag + squares
    loss_part = jnp.sum(terms).reshape(1)

    back_text = backward(d_text, normed_text, inverse_text, means[:2])
    parts_text = [dot(back_text, weight, ((1,), (1,))) for weight in text_weights[1:]]
    d_table, parts_text = lax.optimization_barrier((d_table, parts_text))
    sent_text = [add_cores(part).astype(BF16) for part in parts_text]
    back_table = backward(d_table, normed_table, inverse_table, means[2:])
    parts_table = [dot(back_table, weight, ((1,), (1,))) for weight in table_weights[1:]]
    sent_text, parts_table, back_text, loss_part = lax.optimization_barrier((sent_text, parts_table, back_text, loss_part))
    loss_total = cube_sum(loss_part, "feat")
    sent_table = [add_cores(part).astype(BF16) for part in parts_table]
    sent = [jnp.stack(pair) for pair in zip(sent_text, sent_table)]
    own_text = dot(back_text, text_weights[0], ((1,), (1,)))
    own_table = dot(back_table, table_weights[0], ((1,), (1,)))
    own_text, own_table, sent, loss_total = lax.optimization_barrier((own_text, own_table, sent, loss_total))
    grads = swap_parts(sent)
    loss_total = cube_sum(loss_total, "core")
    grad_text = add_cores(own_text) + sum(part[0].astype(F32) for part in grads)
    grad_table = add_cores(own_table) + sum(part[1].astype(F32) for part in grads)
    return grad_table, grad_text, loss_total / features


def solution(mesh):
    devices = mesh.devices
    split = Mesh(
        devices.reshape(Z_CHIPS, devices.shape[0] // (2 * Z_CHIPS), 2, devices.shape[1]),
        ("z", "y", "core", "feat"),
    )
    rows = ("z", "y", "core")
    placed = (P(rows, "feat"), P(rows, "feat"), P(None, "feat"), P(None, "feat"))
    return jax.shard_map(
        body,
        mesh=split,
        in_specs=placed,
        out_specs=(P(rows, "feat"), P(rows, "feat"), P()),
        check_vma=False,
    )
```

```python
import jax
import jax.numpy as jnp
from jax import lax
from jax.experimental import pallas as pl
from jax.experimental.pallas import tpu as pltpu
from jax.sharding import Mesh
from jax.sharding import PartitionSpec as P

OFF_WEIGHT = 0.1
EPS = 1e-05
Z_CHIPS = 4
F32 = jnp.float32
BF16 = jnp.bfloat16


def dot(a, b, dims):
    return lax.dot_general(a, b, (dims, ((), ())), preferred_element_type=F32)


def shift(x, axis, step):
    size = lax.axis_size(axis)
    return lax.ppermute(x, axis, [(i, (i + step) % size) for i in range(size)])


def flip(x, axis, bit=1):
    size = lax.axis_size(axis)
    return lax.ppermute(x, axis, [(i, i ^ bit) for i in range(size)])


def cube_sum(x, *axes):
    for axis in axes:
        bit = 1
        while bit < lax.axis_size(axis):
            x = x + flip(x, axis, bit)
            bit *= 2
    return x


def own_block(x, index, count, axis):
    size = x.shape[axis] // count
    return lax.dynamic_slice_in_dim(x, index * size, size, axis)


def both_cores(x, axis=0):
    got = flip(x, "core")
    first = lax.axis_index("core") == 0
    return jnp.where(first, jnp.concatenate([x, got], axis), jnp.concatenate([got, x], axis))


def add_cores(x):
    core = lax.axis_index("core")
    return own_block(x, core, 2, 0) + flip(own_block(x, 1 - core, 2, 0), "core")


def cut_kernel(starts, *refs):
    sources, blocks, sems = refs[:2], refs[2:-1], refs[-1]
    count = len(blocks) // 2
    rows, cols = blocks[0].shape
    copies = []
    for i, block in enumerate(blocks):
        row = pl.multiple_of(starts[1 + i % count], 16)
        col = pl.multiple_of(starts[0], 128)
        source = sources[i // count].at[pl.ds(row, rows), pl.ds(col, cols)]
        copies.append(pltpu.make_async_copy(source, block, sems.at[i]))
    for copy in copies:
        copy.start()
    for copy in copies:
        copy.wait()


def weight_blocks(table_proj, text_proj):
    num_feat = lax.axis_size("feat")
    feat = lax.axis_index("feat")
    rows, cols = table_proj.shape[0] // num_feat, table_proj.shape[1] // 2
    firsts = [(feat - step) % num_feat * rows for step in range(num_feat)]
    starts = jnp.stack([lax.axis_index("core") * cols, *firsts]).astype(jnp.int32)
    count = 2 * num_feat
    blocks = pl.pallas_call(
        cut_kernel,
        out_shape=[jax.ShapeDtypeStruct((rows, cols), BF16)] * count,
        in_specs=[pl.BlockSpec(memory_space=pltpu.SMEM), pl.BlockSpec(memory_space=pl.ANY), pl.BlockSpec(memory_space=pl.ANY)],
        out_specs=[pl.BlockSpec(memory_space=pltpu.VMEM)] * count,
        scratch_shapes=[pltpu.SemaphoreType.DMA((count,))],
        compiler_params=pltpu.CompilerParams(vmem_limit_bytes=40 * 1024 * 1024),
    )(starts, table_proj, text_proj)
    return blocks[:num_feat], blocks[num_feat:]


def swap_feat(x):
    return [shift(x, "feat", step) for step in range(1, lax.axis_size("feat"))]


def moments(z_table, z_text):
    count = z_table.shape[0]
    mean_table, mean_text = jnp.mean(z_table, axis=0), jnp.mean(z_text, axis=0)
    centered_table, centered_text = z_table - mean_table, z_text - mean_text
    state = jnp.stack(
        [
            mean_table,
            mean_text,
            jnp.sum(centered_table * centered_table, axis=0),
            jnp.sum(centered_text * centered_text, axis=0),
            jnp.sum(centered_table * centered_text, axis=0),
        ]
    )
    for axis in ("z", "y"):
        bit = 1
        while bit < lax.axis_size(axis):
            other = flip(state, axis, bit)
            gap = state[:2] - other[:2]
            moved = (count / 2) * jnp.concatenate([gap * gap, gap[:1] * gap[1:]], 0)
            state = jnp.concatenate([(state[:2] + other[:2]) / 2, state[2:] + other[2:] + moved], 0)
            count *= 2
            bit *= 2
    return state[:2], state[2:] / count


def at_end(end, inner):
    z = lax.axis_index("z")
    return jnp.where((z == 0) | (z == Z_CHIPS - 1), end, inner)


def over_y(x):
    return [flip(x, "y", step) for step in range(1, lax.axis_size("y"))]


def gram_part(half, rows):
    return add_cores(dot(half, rows, ((1,), (1,))))


def add_feat(mine, others, axis):
    for other in others:
        mine = mine + other.astype(F32)
    return both_cores(mine.astype(BF16), axis)


def column_sums(d, normed):
    return jnp.stack([jnp.sum(d, axis=0), jnp.sum(d * normed, axis=0)])


def backward(d, normed, inverse, means):
    return (inverse * (d - means[0] - normed * means[1])).astype(BF16)


def swap_parts(sent):
    num_feat = lax.axis_size("feat")
    return [shift(part, "feat", num_feat - step) for step, part in enumerate(sent, 1)]


def body(table, text, table_proj, text_proj):
    pairs = table.shape[0] * 2 * lax.axis_size("z") * lax.axis_size("y")
    features = table_proj.shape[1] * lax.axis_size("feat")
    others_table, others_text = swap_feat(table), swap_feat(text)
    table_weights, text_weights = weight_blocks(table_proj, text_proj)
    z_table = dot(both_cores(table), table_weights[0], ((1,), (0,)))
    z_text = dot(both_cores(text), text_weights[0], ((1,), (0,)))
    z_table, z_text, others_table, others_text = lax.optimization_barrier((z_table, z_text, others_table, others_text))
    for other, weight in zip(others_table, table_weights[1:]):
        z_table = z_table + dot(both_cores(other), weight, ((1,), (0,)))
    for other, weight in zip(others_text, text_weights[1:]):
        z_text = z_text + dot(both_cores(other), weight, ((1,), (0,)))

    centers, spreads = moments(z_table, z_text)
    inverse_table, inverse_text = lax.rsqrt(spreads[0] + EPS), lax.rsqrt(spreads[1] + EPS)
    diag = inverse_table * inverse_text * spreads[2]
    diag_weight = (diag - 1.0).astype(BF16).astype(F32) - OFF_WEIGHT * diag
    normed_table = (z_table - centers[0]) * inverse_table
    normed_text = (z_text - centers[1]) * inverse_text
    half = jnp.stack([z_table, z_text])
    half = ((half - centers[:, None]) * lax.rsqrt(spreads[:2] + EPS)[:, None]).astype(BF16)
    half_table, half_text = half[0], half[1]

    near, mid, y_own = lax.optimization_barrier((flip(half, "z"), lax.ppermute(half, "z", [(1, 2), (2, 1)]), over_y(half)))
    far_in, far_end, y_near = lax.optimization_barrier(
        (lax.ppermute(near, "z", [(1, 2), (2, 1)]), lax.ppermute(mid, "z", [(1, 0), (2, 3)]), over_y(near))
    )
    far = at_end(far_end, far_in)
    last_end, y_far = lax.optimization_barrier((lax.ppermute(far_in, "z", [(1, 0), (2, 3)]), over_y(far)))
    last = at_end(last_end, mid)
    cut = half.shape[1] // 2
    y_last = over_y(last[:, :cut])
    y_flip = [flip(block[:, cut:], "z") for block in y_far]

    early = [half, near, far, *y_own, *y_near, *y_far]
    early_table, early_text = [jnp.concatenate([block[i] for block in early], 0) for i in range(2)]
    gram_table = gram_part(half_table, early_table)
    others_table = swap_feat(gram_table.astype(BF16))
    gram_text = gram_part(half_text, early_text)
    gram_text = jnp.split(gram_text, 2, 1)
    others_text = [swap_feat(part.astype(BF16)) for part in gram_text]
    y_last, y_flip, others_table, others_text[0] = lax.optimization_barrier((y_last, y_flip, others_table, others_text[0]))
    late = [last] + [block for pair in zip(y_last, y_flip) for block in pair]
    late_table, late_text = [jnp.concatenate([block[i] for block in late], 0) for i in range(2)]
    all_table, all_text = (early_table, late_table), (early_text, late_text)
    late_gram = jnp.concatenate([gram_part(half_table, late_table), gram_part(half_text, late_text)], 1)
    late_gram = add_feat(late_gram, swap_feat(late_gram.astype(BF16)), 0)
    gram_table = add_feat(gram_table, others_table, 0)
    others_text = [jnp.concatenate(parts, 1) for parts in zip(*others_text)]
    gram_text = add_feat(jnp.concatenate(gram_text, 1), others_text, 0)
    grams = (gram_table, gram_text), jnp.split(late_gram, 2, 1)

    off_table, off_text = 0.0, 0.0
    for gram, rows_table, rows_text in zip(grams, all_table, all_text):
        off_table = off_table + dot(gram[1], rows_table, ((1,), (0,)))
        off_text = off_text + dot(gram[0], rows_text, ((1,), (0,)))
    d_table = (OFF_WEIGHT / pairs) * off_table + half_text.astype(F32) * diag_weight
    d_text = (OFF_WEIGHT / pairs) * off_text + half_table.astype(F32) * diag_weight
    sums = jnp.concatenate([column_sums(d_text, normed_text), column_sums(d_table, normed_table)], 0)
    means = cube_sum(sums, "z", "y") / pairs

    squares = means[3] - diag_weight * diag
    terms = (1.0 - diag) * (1.0 - diag) - OFF_WEIGHT * diag * diag + squares
    loss_total = cube_sum(jnp.sum(terms).reshape(1), "feat")

    back_text = backward(d_text, normed_text, inverse_text, means[:2])
    parts_text = [dot(back_text, weight, ((1,), (1,))) for weight in text_weights[1:]]
    d_table, parts_text = lax.optimization_barrier((d_table, parts_text))
    sent_text = [add_cores(part).astype(BF16) for part in parts_text]
    back_table = backward(d_table, normed_table, inverse_table, means[2:])
    parts_table = [dot(back_table, weight, ((1,), (1,))) for weight in table_weights[1:]]
    sent_text, parts_table, back_text, loss_total = lax.optimization_barrier((sent_text, parts_table, back_text, loss_total))
    sent_table = [add_cores(part).astype(BF16) for part in parts_table]
    sent = [jnp.stack(pair) for pair in zip(sent_text, sent_table)]
    own_text = dot(back_text, text_weights[0], ((1,), (1,)))
    own_table = dot(back_table, table_weights[0], ((1,), (1,)))
    own_text, own_table, sent = lax.optimization_barrier((own_text, own_table, sent))
    grads = swap_parts(sent)
    loss_total = cube_sum(loss_total, "core")
    grad_text = add_cores(own_text) + sum(part[0].astype(F32) for part in grads)
    grad_table = add_cores(own_table) + sum(part[1].astype(F32) for part in grads)
    return grad_table, grad_text, loss_total / features


def solution(mesh):
    devices = mesh.devices
    split = Mesh(
        devices.reshape(Z_CHIPS, devices.shape[0] // (2 * Z_CHIPS), 2, devices.shape[1]),
        ("z", "y", "core", "feat"),
    )
    rows = ("z", "y", "core")
    placed = (P(rows, "feat"), P(rows, "feat"), P(None, "feat"), P(None, "feat"))
    return jax.shard_map(
        body,
        mesh=split,
        in_specs=placed,
        out_specs=(P(rows, "feat"), P(rows, "feat"), P()),
        check_vma=False,
    )
```
